32 devices in a mesh: runs: 2 (over y), area: 16 (over z, x, core).
Axes of the slice: x: 2, y: 2, z: 4, core: 2. Of those that a mesh axis runs over, the one named last changes fastest.
Arguments:
- spikes: int32 [8, 10, 6144], P('runs', None, 'area'), parts along dimension 0, may hold values 0 or 1
- weights: bfloat16 [1536, 384, 128], P('area'), may hold values from -0.625 to 0.625
- destination: int32 [1536, 1], P('area'), may hold values from 0 to 15; in each aligned block of 96 rows (0 to 95, 96 to 191, ...) at most 6 rows name the same one
- target_block: int32 [1536], P('area'), may hold values from 0 to 2
- delay_slot: int32 [1536], P('area'), may hold values from 0 to 3
- population: int32 [6144], P('area'), may hold values from 0 to 3
- leak_rate: float32 [6144], P('area'), may hold values from 0.3 to 0.95
- membrane_start: float32 [8, 6144], P('runs', 'area'), parts along dimension 0, may hold values from -6 to 6
- cycle_start: float32 [8, 4, 6144], P('runs', None, 'area'), parts along dimension 0, may hold values from -3 to 3
- history: float32 [64, 2, 8, 256], P('area', None, 'runs'), parts along dimension 2, may hold values from -1.2 to 1.2
- lfp_kernel: bfloat16 [384, 64, 2, 256], P(None, 'area'), may hold values from -0.375 to 0.375
Outputs:
- membrane: float32 [8, 6144], P('runs', 'area'), parts along dimension 0
- cycle_out: float32 [8, 4, 6144], P('runs', None, 'area'), parts along dimension 0
- lfp: float32 [384, 80], P('area', 'runs'), parts along dimension 1
The draws below stay inside these ranges and needn't reach their ends.
There are 2 independent parts, one for each index of `runs`. The reference program is written for one: setup_inputs(seed, part) draws one part's arguments, and reference() takes and returns one part's arrays. A program takes and returns all parts, laid end to end along the dimension named above; an argument that names none is the same for every part. Nothing has to cross between parts.
Inputs may be any that keep to these rules, and one draw needn't show every extreme that they name: Of the 96 units of one device at most 6 have the same destination; in every draw some device sends exactly 6 units to one destination.
All inputs are finite; a program needn't handle non-finite values. No bound on the sum of `spikes` on one device may be relied on, other than what follows from the above.
Results may differ from the reference program's by a relative error of at most 0.0029.
Values may be sent and summed in bfloat16 or wider, within the bound.
No kernel may reach another device: no remote copies, remote signals or barrier semaphores. Data moves between devices by JAX's collectives and lax.ppermute only.
A program may use at most 64 MiB of HBM per device.

```python
import math
import jax
import jax.numpy as jnp
import numpy as np
from jax import lax

NEUR_DEV = 384
UNITS = 96
TRIALS = 4
STEPS = 10
DELAYS = 4
POP_DEV = 4
CH = 384
TAPS = 256
BLOCKS = 3
CAP = 6
NEURONS = 6144
POPS = 64
N_AREA = 16


def plant(result, rng, smallest, high):
    place = [jax.random.randint(jax.random.fold_in(rng, axis), (), 0, length) for axis, length in enumerate(result.shape)]
    main_axis = result.shape.index(max(result.shape))
    beside = place[:main_axis] + [(place[main_axis] + 1) % result.shape[main_axis]] + place[main_axis + 1:]
    return result.at[tuple(place)].set(smallest).at[tuple(beside)].set(high)


def levels(own_key, shape, cuts, smallest, largest):
    def one(dim, blocks):
        draws = jax.random.uniform(jax.random.fold_in(jax.random.fold_in(own_key, 6), dim), (blocks,), jnp.float32, smallest / len(cuts), largest / len(cuts))
        return jnp.repeat(jnp.exp(draws), shape[dim] // blocks).reshape((-1,) + (1,) * (len(shape) - dim - 1))

    loudness = one(*cuts[0])
    for cut in cuts[1:]:
        loudness = loudness * one(*cut)
    return loudness


def shared_out(key, own, number, rows, count, top, bound, lean):
    order = jax.random.permutation(key, count)
    packed, ordinary = shares(count, rows * top, bound, lean, True), shares(count, rows * top, bound, lean, False)
    places = jnp.arange(count)

    def named(lengths, turn):
        used = int((lengths > 0).sum())
        fixed = max(1, used // 4)
        passed = fixed + (places - fixed + turn * (used - fixed)) % max(1, count - fixed)
        return jnp.zeros((count,), jnp.int32).at[order[jnp.where(places < fixed, places, passed)]].set(jnp.asarray(lengths, jnp.int32))

    lengths = jnp.where(number % 4 == 0, named(packed, number // 4), named(ordinary, number - number // 4 - 1))
    mixed = jax.random.permutation(jax.random.fold_in(own, 3), count)
    giver, taker = mixed[0:count // 2 * 2:2], mixed[1:count // 2 * 2:2]
    margin = jnp.minimum(lengths[giver] - 1, bound - lengths[taker]) // 2
    margin = jnp.where((giver == order[0]) | (taker == order[0]) | (lengths[taker] == 0), 0, jnp.maximum(margin, 0))
    passed = jax.random.randint(jax.random.fold_in(own, 4), (count // 2,), 0, 1 << 20) % (margin + 1)
    lengths = lengths.at[giver].add(-passed).at[taker].add(passed)
    labels = jnp.searchsorted(jnp.cumsum(lengths), jnp.arange(rows * top), side="right").astype(jnp.int32)
    listing = labels.reshape(top, rows).T
    listing = listing[jax.random.permutation(jax.random.fold_in(own, 1), rows)]
    turn = jax.random.randint(jax.random.fold_in(own, 2), (rows, 1), 0, top)
    return jnp.take_along_axis(listing, (jnp.arange(top)[None, :] + turn) % top, axis=1)


def shares(count, total, reach, slope, full):
    loads = [(1 << 20) // math.isqrt(grade ** slope) + 1 for grade in range(1, count + 1)]
    largest = reach if full else min(reach, max(-(-total // count), total * loads[0] // sum(loads)))
    least = 1 if total - largest >= count - 1 else 0
    counts, rest = [largest] + [least] * (count - 1), total - largest - least * (count - 1)
    while rest > 0:
        free = [i for i in range(1, count) if counts[i] < largest] or [i for i in range(1, count) if counts[i] < reach]
        whole, remaining = sum([loads[i] for i in free]), rest
        for i in free:
            addition = min(reach - counts[i], max(1, remaining * loads[i] // whole), rest)
            counts[i] = counts[i] + addition
            rest = rest - addition
    return np.array(counts)


def normal_values(rng, dims, deviation, bound, pieces=(), kind=jnp.bfloat16):
    array = jax.random.normal(rng, dims, jnp.float32) * deviation
    if len(pieces) > 0:
        array = levels(rng, dims, pieces, -0.22, 0.18) * array
    return jnp.clip(array, min=-bound, max=bound).astype(kind)


def setup_inputs(seed: int = 0, part: int = 0) -> dict:
    key_list = jax.random.split(jax.random.key(seed), 12)
    part_keys = jax.random.split(jax.random.fold_in(key_list[11], part), 12)
    spikes = plant((jax.random.randint(part_keys[0], (TRIALS, STEPS, NEURONS), 0, 8) < 1).astype(jnp.int32), jax.random.fold_in(part_keys[0], 1), 0, 1)
    weights = normal_values(key_list[1], (N_AREA * UNITS, NEUR_DEV, 128), (NEUR_DEV // 4) ** -0.5, 0.625, ((0, 16),))
    destination_keys = jax.random.split(jax.random.fold_in(key_list[2], 1), (N_AREA * UNITS) // UNITS)
    destination_turns = jax.random.permutation(jax.random.fold_in(key_list[2], 3), (N_AREA * UNITS) // UNITS)
    destination = jax.vmap(lambda own, number: shared_out(jax.random.fold_in(key_list[2], 2), own, number, UNITS, N_AREA, 1, CAP, 2))(destination_keys, destination_turns).reshape((N_AREA * UNITS, 1))
    target_block = plant(jax.random.randint(key_list[3], (N_AREA * UNITS,), 0, BLOCKS), jax.random.fold_in(key_list[3], 1), 0, BLOCKS - 1).astype(jnp.int32)
    delay_slot = plant(jax.random.randint(key_list[4], (N_AREA * UNITS,), 0, DELAYS), jax.random.fold_in(key_list[4], 1), 0, DELAYS - 1).astype(jnp.int32)
    population = plant(jax.random.randint(key_list[5], (NEURONS,), 0, POP_DEV), jax.random.fold_in(key_list[5], 1), 0, POP_DEV - 1).astype(jnp.int32)
    leak_rate = jnp.clip(jnp.exp(math.log(0.95) - 1.1526795 * jax.random.uniform(key_list[6], (NEURONS,), jnp.float32) ** levels(key_list[6], (NEURONS,), ((0, 16),), -0.2, 0.2)), 0.3, 0.95)
    membrane_start = normal_values(part_keys[7], (TRIALS, NEURONS), 1.0, 6.0, ((1, 16),), jnp.float32)
    cycle_start = normal_values(part_keys[8], (TRIALS, DELAYS, NEURONS), 0.5, 3.0, ((2, 16),), jnp.float32)
    history = normal_values(part_keys[9], (POPS, 2, TRIALS, TAPS), 0.2, 1.2, ((0, 16),), jnp.float32)
    lfp_kernel = normal_values(key_list[10], (CH, POPS, 2, TAPS), TAPS ** -0.5, 0.375, ((1, 16),))
    return dict(spikes=spikes, weights=weights, destination=destination, target_block=target_block, delay_slot=delay_slot, population=population, leak_rate=leak_rate, membrane_start=membrane_start, cycle_start=cycle_start, history=history, lfp_kernel=lfp_kernel)


def arrivals_from(blocks_acc, cycle_start):
    total = jnp.zeros((blocks_acc.shape[0], TRIALS, STEPS + DELAYS, 128), jnp.float32)
    for delay_index in range(DELAYS):
        piece = blocks_acc[:, delay_index]
        total = total + jnp.pad(piece, ((0, 0), (0, 0), (delay_index + 1, DELAYS - 1 - delay_index), (0, 0)))
    total = jnp.transpose(total, (1, 2, 0, 3)).reshape(TRIALS, STEPS + DELAYS, -1)
    return total + jnp.pad(cycle_start, ((0, 0), (0, STEPS), (0, 0)))


def build_lags(series):
    windows = [series[..., step:step + TAPS][..., ::-1] for step in range(STEPS)]
    stacked = jnp.stack(windows, axis=-1)
    lead = series.shape[:-2]
    order = tuple(range(len(lead))) + (len(lead) + 1, len(lead), len(lead) + 2)
    stacked = jnp.transpose(stacked, order)
    return stacked.reshape(-1, TRIALS * STEPS)


def reference(spikes, weights, destination, target_block, delay_slot, population, leak_rate, membrane_start, cycle_start, history, lfp_kernel):
    row_count = TRIALS * STEPS
    spike_f = spikes.astype(jnp.float32)
    spike_rows = spike_f.reshape(row_count, NEURONS)
    unit_weights = weights.reshape(N_AREA, UNITS, NEUR_DEV, 128)
    index_all = ((destination[:, 0] * BLOCKS + target_block) * DELAYS + delay_slot).astype(jnp.int32).reshape(N_AREA, UNITS)

    def one_source(acc, inputs):
        source_weights, index_here, device = inputs
        local = lax.dynamic_slice_in_dim(spike_rows, (device * NEUR_DEV).astype(jnp.int32), NEUR_DEV, 1)
        payload = jnp.einsum('rk,ukn->urn', local, source_weights.astype(jnp.float32), precision=lax.Precision.HIGHEST).astype(jnp.bfloat16)
        return acc.at[index_here].add(payload.astype(jnp.float32).reshape(UNITS, row_count * 128)), None

    start_acc = jnp.zeros((N_AREA * BLOCKS * DELAYS, row_count * 128), jnp.float32)
    acc, _ = lax.scan(one_source, start_acc, (unit_weights, index_all, jnp.arange(N_AREA, dtype=jnp.int32)))
    blocks_acc = acc.reshape(N_AREA * BLOCKS, DELAYS, TRIALS, STEPS, 128)
    arrivals = arrivals_from(blocks_acc, cycle_start)
    current = arrivals[:, :STEPS]
    cycle_out = arrivals[:, STEPS:]
    membrane = membrane_start
    for step in range(STEPS):
        membrane = (leak_rate * membrane + current[:, step]) * (1.0 - spike_f[:, step])
    group = ((jnp.arange(NEURONS, dtype=jnp.int32) // NEUR_DEV) * POP_DEV + population).astype(jnp.int32)
    pop_size = NEUR_DEV / POP_DEV
    rate_signal = jax.ops.segment_sum(spike_rows.T, group, num_segments=POPS) / pop_size
    current_signal = jax.ops.segment_sum(current.reshape(row_count, NEURONS).T, group, num_segments=POPS) / pop_size
    fresh = jnp.stack([rate_signal, current_signal], axis=1).reshape(POPS, 2, TRIALS, STEPS)
    series = jnp.concatenate([history, fresh], axis=-1).astype(jnp.bfloat16)
    lagged = build_lags(series).astype(jnp.float32)
    kernel_flat = lfp_kernel.reshape(CH, POPS * 2 * TAPS).astype(jnp.float32)
    lfp = jnp.dot(kernel_flat, lagged, precision=lax.Precision.HIGHEST, preferred_element_type=jnp.float32)
    return membrane, cycle_out, lfp
```

```python
import functools

import jax
import jax.numpy as jnp
from jax import lax
from jax.experimental import pallas as pl
from jax.experimental.pallas import tpu as pltpu
from jax.sharding import PartitionSpec as P

BF16, F32 = jnp.bfloat16, jnp.float32


def chunk_of(unit_count):
    for size in (8, 6, 4, 3, 2):
        if unit_count % size == 0:
            return size
    return 1


def payload_kernel(
    destination, target_block, delay_slot, spikes, weights, keep, send, held, lagged, plain, sems
):
    trials, steps, neurons = spikes.shape
    unit_count = weights.shape[0]
    delays = lagged.shape[0]
    blocks = neurons // 128
    rows = keep.shape[1]
    chunk = held.shape[0] // sems.shape[0]
    chunks = unit_count // chunk

    def copy(index):
        part = pl.ds(index * chunk, chunk)
        return pltpu.make_async_copy(weights.at[part], held.at[part], sems.at[index])

    for index in range(chunks):
        copy(index).start()
    keep[...] = jnp.zeros_like(keep)
    send[...] = jnp.zeros_like(send)
    plain[...] = jnp.zeros_like(plain)
    front = trials * delays
    for trial in range(trials):
        for step in range(steps):
            plain[front + step * trials + trial, :] = spikes[trial, step, :].astype(F32)
    lagged[...] = jnp.zeros_like(lagged)
    for delay in range(delays):
        start = front - trials * (delay + 1)
        lagged[delay, 0:rows, :] = plain[start : start + rows, :].astype(BF16)
    me = lax.axis_index("area")

    def some(index, _):
        copy(index).wait()
        for inner in range(chunk):
            unit = index * chunk + inner
            device = lax.bitwise_xor(destination[unit, 0], me)
            place = (device // 2) * blocks + target_block[unit]
            value = jnp.dot(lagged[delay_slot[unit]], held[unit], preferred_element_type=F32)
            value = value[0:rows].astype(BF16).astype(F32)

            @pl.when(device % 2 == 0)
            def _():
                keep[place] += value

            @pl.when(device % 2 == 1)
            def _():
                send[place] += value

        return 0

    lax.fori_loop(0, chunks, some, 0)


def payload_sums(spikes, weights, destination, target_block, delay_slot, area_count, delays):
    trials, steps, neurons = spikes.shape
    unit_count = weights.shape[0]
    blocks = neurons // 128
    rows = trials * (steps + delays)
    padded = -(-rows // 16) * 16
    chunk = chunk_of(unit_count)
    half = jax.ShapeDtypeStruct((area_count // 2 * blocks, rows, 128), F32)
    smem = pl.BlockSpec(memory_space=pltpu.SMEM)
    vmem = pl.BlockSpec(memory_space=pltpu.VMEM)
    front = trials * delays
    return pl.pallas_call(
        payload_kernel,
        out_shape=(half, half),
        in_specs=[smem, smem, smem, vmem, pl.BlockSpec(memory_space=pl.ANY)],
        out_specs=(vmem, vmem),
        scratch_shapes=[
            pltpu.VMEM(weights.shape, BF16),
            pltpu.VMEM((delays, padded, neurons), BF16),
            pltpu.VMEM((front + rows, neurons), F32),
            pltpu.SemaphoreType.DMA((unit_count // chunk,)),
        ],
        compiler_params=pltpu.CompilerParams(vmem_limit_bytes=40 * 2**20),
        cost_estimate=pl.CostEstimate(
            flops=2 * unit_count * rows * neurons * 128,
            bytes_accessed=unit_count * neurons * 256,
            transcendentals=0,
        ),
        name="payload",
    )(destination, target_block, delay_slot, spikes, weights)


def swap(values, bit, area_count):
    return lax.ppermute(values, "area", [(i, i ^ bit) for i in range(area_count)])


def halve(values, bit_dim, narrow):
    keep = lax.index_in_dim(values, 0, bit_dim, keepdims=False)
    send = lax.index_in_dim(values, 1, bit_dim, keepdims=False)
    return keep, send.astype(BF16) if narrow else send


def scatter_sum(values, bits, direct, area_count, narrow):
    lead = values.shape[1:]
    for bit in bits:
        count = values.shape[0]
        keep, send = halve(values.reshape((count // 2, 2) + lead), 1, narrow)
        values = keep + swap(send, bit, area_count).astype(F32)
    total = values[0]
    for index, bit in enumerate(direct, 1):
        send = values[index]
        send = send.astype(BF16) if narrow else send
        total = total + swap(send, bit, area_count).astype(F32)
    return total


def lag_rows(series, step_count, taps):
    windows = [series[..., step : step + taps][..., ::-1] for step in range(step_count)]
    stacked = jnp.stack(windows, axis=-1)
    lead = series.shape[:-2]
    order = tuple(range(len(lead))) + (len(lead) + 1, len(lead), len(lead) + 2)
    stacked = jnp.transpose(stacked, order)
    return stacked.reshape(-1, series.shape[-2] * step_count)


def body(
    spikes,
    weights,
    destination,
    target_block,
    delay_slot,
    population,
    leak_rate,
    membrane_start,
    cycle_start,
    history,
    lfp_kernel,
):
    area_count = lax.axis_size("area")
    neurons_here = weights.shape[1]
    blocks = neurons_here // 128
    trials, step_count = spikes.shape[:2]
    row_count = trials * step_count
    delays = cycle_start.shape[1]
    channels = lfp_kernel.shape[0]
    pop_count = history.shape[0]
    taps = history.shape[3]
    me = lax.axis_index("area")
    span = step_count + delays

    keep, send = payload_sums(
        spikes, weights, destination, target_block, delay_slot, area_count, delays
    )

    spike_f = spikes.astype(F32)
    pop_table = (population[:, None] == jnp.arange(pop_count, dtype=jnp.int32)[None, :]).astype(F32)
    pop_size = neurons_here / pop_count

    def signal(values):
        summed = jnp.dot(
            values.reshape(-1, neurons_here),
            pop_table,
            precision=lax.Precision.HIGHEST,
            preferred_element_type=F32,
        )
        return (summed / pop_size).T.reshape(pop_count, trials, -1)

    rate_fresh = signal(spike_f)
    fresh = jnp.stack([rate_fresh, jnp.zeros_like(rate_fresh)], axis=1)
    series = jnp.concatenate([history, fresh], axis=-1).astype(BF16)
    known = jnp.dot(
        lfp_kernel.reshape(channels, -1),
        lag_rows(series, step_count, taps),
        preferred_element_type=F32,
    )
    recent = lfp_kernel[:, :, 1, : step_count - 1].reshape(channels, -1)

    high = [1 << index for index in range(1, area_count.bit_length() - 1)]
    bits, last = high[:-2], high[-2:]
    direct = [last[0], last[1], last[0] + last[1]]
    summed = keep + swap(send, 1, area_count)
    summed = summed.reshape((area_count // 2, blocks, span * trials, 128))
    summed = scatter_sum(summed, bits, direct, area_count, True)

    arrivals = jnp.transpose(summed.reshape(blocks, span, trials, 128), (2, 1, 0, 3))
    arrivals = arrivals.reshape(trials, span, neurons_here)
    arrivals = arrivals + jnp.pad(cycle_start, ((0, 0), (0, step_count), (0, 0)))
    current = arrivals[:, :step_count]
    cycle_out = arrivals[:, step_count:]
    membrane = membrane_start
    for step in range(step_count):
        membrane = (leak_rate * membrane + current[:, step]) * (1.0 - spike_f[:, step])

    current_fresh = signal(current[:, : step_count - 1]).astype(BF16)
    padded = jnp.pad(current_fresh, ((0, 0), (0, 0), (step_count - 1, 0)))
    partial = known + jnp.dot(
        recent, lag_rows(padded, step_count, step_count - 1), preferred_element_type=F32
    )

    share = channels // area_count
    partial = partial.reshape(area_count, share, row_count)
    partial = partial[jnp.bitwise_xor(jnp.arange(area_count), me)]
    lfp = scatter_sum(partial, [1] + bits, direct, area_count, False)
    return (membrane, cycle_out, lfp)


def solution(mesh):
    return jax.shard_map(
        body,
        mesh=mesh,
        in_specs=(
            P("runs", None, "area"),
            P("area", None, None),
            P("area", None),
            P("area"),
            P("area"),
            P("area"),
            P("area"),
            P("runs", "area"),
            P("runs", None, "area"),
            P("area", None, "runs", None),
            P(None, "area", None, None),
        ),
        out_specs=(P("runs", "area"), P("runs", None, "area"), P("area", "runs")),
        check_vma=False,
    )
```

```python
import functools

import jax
import jax.numpy as jnp
from jax import lax
from jax.experimental import pallas as pl
from jax.experimental.pallas import tpu as pltpu
from jax.sharding import PartitionSpec as P

BF16, F32 = jnp.bfloat16, jnp.float32
VMEM = pl.BlockSpec(memory_space=pltpu.VMEM)
HBM = pl.BlockSpec(memory_space=pltpu.HBM)
NT = (((1,), (1,)), ((), ()))


def up(value, unit):
    return -(-value // unit) * unit


def dot(left, right, dims=None):
    if dims is None:
        return jnp.dot(left, right, preferred_element_type=F32)
    return lax.dot_general(left, right, dims, preferred_element_type=F32)


def both(values):
    high = values.astype(BF16)
    return high, (values - high.astype(F32)).astype(BF16)


def payload_kernel(
    destination, target_block, delay_slot, spikes, weights, total,
    codes, given, held, plain, lagged, sems, part_sems,
):
    steps, trials, neurons = spikes.shape
    unit_count = weights.shape[0]
    delays = lagged.shape[0]
    blocks = neurons // 128
    rows = total.shape[1]
    chunk = held.shape[0] // part_sems.shape[0]
    chunks = unit_count // chunk
    small = [
        pltpu.make_async_copy(destination, codes.at[0], sems.at[0]),
        pltpu.make_async_copy(target_block, codes.at[1], sems.at[1]),
        pltpu.make_async_copy(delay_slot, codes.at[2], sems.at[2]),
        pltpu.make_async_copy(spikes, given, sems.at[3]),
    ]
    for copy in small:
        copy.start()

    def part(index):
        where = pl.ds(index * chunk, chunk)
        return pltpu.make_async_copy(weights.at[where], held.at[where], part_sems.at[index])

    for index in range(chunks):
        part(index).start()
    total[...] = jnp.zeros_like(total)
    plain[...] = jnp.zeros_like(plain)
    lagged[...] = jnp.zeros_like(lagged)
    for copy in small:
        copy.wait()
    front = trials * delays
    for step in range(steps):
        start = front + step * trials
        plain[start : start + trials, :] = given[step].astype(F32)
    for delay in range(delays):
        start = front - trials * (delay + 1)
        lagged[delay, 0:rows, :] = plain[start : start + rows, :].astype(BF16)
    me = lax.axis_index("area")

    def some(index, _):
        part(index).wait()
        units = [index * chunk + inner for inner in range(chunk)]
        values = [
            dot(lagged[codes[2, unit]], held[unit])[0:rows].astype(BF16).astype(F32)
            for unit in units
        ]
        for unit, value in zip(units, values):
            place = lax.bitwise_xor(codes[0, unit], me) * blocks + codes[1, unit]
            total[place] += value
        return 0

    lax.fori_loop(0, chunks, some, 0)


def payload_sums(spikes, weights, destination, target_block, delay_slot, area_count, delays):
    steps, trials, neurons = spikes.shape
    unit_count = weights.shape[0]
    blocks = neurons // 128
    rows = trials * (steps + delays)
    chunk = next(size for size in (16, 12, 8, 6, 4, 3, 2, 1) if unit_count % size == 0)
    return pl.pallas_call(
        payload_kernel,
        out_shape=jax.ShapeDtypeStruct((area_count * blocks, rows, 128), F32),
        in_specs=[HBM, HBM, HBM, HBM, HBM],
        out_specs=VMEM,
        scratch_shapes=[
            pltpu.SMEM((3, unit_count), jnp.int32),
            pltpu.VMEM(spikes.shape, jnp.int32),
            pltpu.VMEM(weights.shape, BF16),
            pltpu.VMEM((trials * delays + rows, neurons), F32),
            pltpu.VMEM((delays, up(rows, 16), neurons), BF16),
            pltpu.SemaphoreType.DMA((4,)),
            pltpu.SemaphoreType.DMA((unit_count // chunk,)),
        ],
        compiler_params=pltpu.CompilerParams(vmem_limit_bytes=32 * 2**20),
        name="payload",
    )(destination, target_block, delay_slot, spikes, weights)


def known_kernel(spikes, population, history, kernel, out, series, fresh, lags):
    steps, trials, neurons = spikes.shape
    pops, kinds, _, taps = history.shape
    group = kinds * trials
    lane = lax.broadcasted_iota(jnp.int32, (pops * group, taps), 1)
    for pop in range(pops):
        for kind in range(kinds):
            start = pop * group + kind * trials
            series[start : start + trials, :] = history[pop, kind]
    flip = lax.broadcasted_iota(jnp.int32, (taps, taps), 0) + lax.broadcasted_iota(
        jnp.int32, (taps, taps), 1
    )
    flip = (flip == taps - 1).astype(F32).astype(BF16)
    back = dot(series[...].astype(BF16), flip)

    which = lax.broadcasted_iota(jnp.int32, (8, neurons), 0)
    member = (which == population[...]).astype(F32).astype(BF16)
    rows = spikes[...].reshape(steps * trials, neurons).astype(F32).astype(BF16)
    rates = (dot(member, rows, NT) / (neurons / pops)).astype(BF16)
    fresh[...] = jnp.zeros_like(fresh)
    row = lax.broadcasted_iota(jnp.int32, (steps * trials, taps), 0)
    column = lax.broadcasted_iota(jnp.int32, (steps * trials, taps), 1)
    for trial in range(trials):
        place = (row == (taps - 1 - column) * trials + trial).astype(F32).astype(BF16)
        placed = dot(rates, place)
        for pop in range(pops):
            fresh[pop * group + trial : pop * group + trial + 1, :] = placed[pop : pop + 1, :]
    lags[...] = jnp.zeros_like(lags)
    recent = fresh[...]
    for step in range(steps):
        shifted = jnp.where(lane >= taps - step, recent, back)
        if step:
            shifted = pltpu.roll(shifted, step, 1)
        for part in range(pops * kinds):
            lags[part, step * trials : (step + 1) * trials, :] = shifted[
                part * trials : (part + 1) * trials, :
            ]
    total = dot(kernel[:, 0:taps], lags[0].astype(BF16), NT)
    for part in range(1, pops * kinds):
        total += dot(kernel[:, part * taps : (part + 1) * taps], lags[part].astype(BF16), NT)
    out[...] = total


def known_lfp(spikes, population, history, kernel):
    pops, kinds, trials, taps = history.shape
    channels = kernel.shape[0]
    return pl.pallas_call(
        known_kernel,
        out_shape=jax.ShapeDtypeStruct((channels, 128), F32),
        in_specs=[VMEM] * 4,
        out_specs=VMEM,
        scratch_shapes=[
            pltpu.VMEM((pops * kinds * trials, taps), F32),
            pltpu.VMEM((pops * kinds * trials, taps), F32),
            pltpu.VMEM((pops * kinds, 128, taps), F32),
        ],
        compiler_params=pltpu.CompilerParams(vmem_limit_bytes=16 * 2**20),
        name="known_lfp",
    )(spikes, population, history, kernel)


class Plan:
    def __init__(self, area_count, trials, steps, delays, neurons, pops, channels):
        self.area_count, self.trials, self.steps, self.delays = area_count, trials, steps, delays
        self.blocks, self.pops = neurons // 128, pops
        self.pop_size = neurons / pops
        self.each = trials * (1 + delays)
        self.main = up(self.blocks * self.each, 16)
        self.share = channels // area_count
        self.groups = up(self.share, 8) // 8
        self.width = trials * steps
        self.slot = self.main + 8
        self.narrow_slot = self.main + 16
        self.signal_rows = up(trials * (steps - 1), 8)
        self.signal_lanes = pops * area_count
        self.parts = up(self.signal_lanes, 128) // 128
        self.wide_lanes = min(self.signal_lanes, 128)
        self.tail = self.parts * self.signal_rows
        self.narrow_tail = up(self.tail, 16) * (2 if 2 * self.wide_lanes > 128 else 1)

    def wide(self, slots):
        return jax.ShapeDtypeStruct((slots * self.slot + self.tail, 128), F32)

    def narrow(self, slots):
        return jax.ShapeDtypeStruct((slots * self.narrow_slot + self.narrow_tail, 128), BF16)


def compress_kernel(plan, total, given, cycle, start, known, keep, send, signal):
    trials, steps, delays, blocks = plan.trials, plan.steps, plan.delays, plan.blocks
    me = lax.axis_index("area")
    signal_rows, lanes = plan.signal_rows, plan.signal_lanes
    signal[...] = jnp.zeros_like(signal)
    owner = lax.broadcasted_iota(jnp.int32, (lanes, 128), 0).astype(F32)

    def pair(index, _):
        sums = jnp.zeros((2 * signal_rows, lanes), F32)
        for bit, out in enumerate((keep, send)):
            device = 2 * index + bit
            own = (device == 0).astype(F32)
            place = lax.bitwise_xor(device, me)
            first = (place * plan.pops).astype(F32)
            base = pl.multiple_of(index * plan.slot, 8)
            tops, members = [], []
            for block in range(blocks):
                arriving = total[device * blocks + block]
                early = arriving[0 : trials * delays] + own * cycle[block]
                arriving = jnp.concatenate([early, arriving[trials * delays :]], axis=0)
                facts = given[device, block * 8 : block * 8 + 8]
                last, leak = facts[0:trials], facts[trials : trials + 1]
                population = facts[trials + 1 : trials + 2]
                membrane = own * start[block]
                for step in range(steps):
                    current = arriving[step * trials : (step + 1) * trials]
                    membrane = jnp.where(last < step, leak * membrane + current, 0.0)
                spot = base + block * plan.each
                out[pl.ds(spot, trials)] = membrane
                out[pl.ds(spot + trials, trials * delays)] = arriving[trials * steps :]
                tops.append(arriving[0:signal_rows])
                members.append((owner == population + first).astype(F32).astype(BF16))
            out[pl.ds(base + blocks * plan.each, plan.main - blocks * plan.each)] = jnp.zeros(
                (plan.main - blocks * plan.each, 128), F32
            )
            top = jnp.concatenate(tops, axis=1)
            high, low = both(top)
            stacked = jnp.concatenate([high.astype(F32), low.astype(F32)], axis=0).astype(BF16)
            sums += dot(stacked, jnp.concatenate(members, axis=1), NT)
            mine = known[place]
            packed = mine[0:8]
            for group in range(1, plan.groups):
                packed += pltpu.roll(mine[group * 8 : group * 8 + 8], group * plan.width, 1)
            out[pl.ds(base + plan.main, 8)] = packed
        signal[...] += sums[:signal_rows] + sums[signal_rows:]
        return 0

    pairs = plan.area_count // 2
    lax.fori_loop(0, pairs, pair, 0, unroll=2)
    for part in range(plan.parts):
        values = signal[:, part * 128 : part * 128 + plan.wide_lanes]
        if plan.wide_lanes < 128:
            values = jnp.concatenate(
                [values, jnp.zeros((signal_rows, 128 - plan.wide_lanes), F32)], axis=1
            )
        spot = pairs * plan.slot + part * signal_rows
        keep[spot : spot + signal_rows] = values
        send[spot : spot + signal_rows] = values


def compress(plan, total, given, cycle, start, known):
    return pl.pallas_call(
        functools.partial(compress_kernel, plan),
        out_shape=(plan.wide(plan.area_count // 2),) * 2,
        in_specs=[VMEM] * 5,
        out_specs=(VMEM, VMEM),
        scratch_shapes=[pltpu.VMEM((plan.signal_rows, plan.signal_lanes), F32)],
        compiler_params=pltpu.CompilerParams(vmem_limit_bytes=32 * 2**20),
        name="compress",
    )(total, given, cycle, start, known)


def narrow_slot(plan, out, slot, main, channels):
    base = slot * plan.narrow_slot
    high, low = both(channels)
    out[base : base + plan.main] = main.astype(BF16)
    out[base + plan.main : base + plan.narrow_slot] = jnp.concatenate(
        [high.astype(F32), low.astype(F32)], axis=0
    ).astype(BF16)


def narrow_tail(plan, out, slots, values):
    base = slots * plan.narrow_slot
    high, low = both(values)
    high, low = high.astype(F32), low.astype(F32)
    if 2 * plan.wide_lanes <= 128:
        rows = high + pltpu.roll(low, plan.wide_lanes, 1)
        pad = plan.narrow_tail - plan.tail
        if pad:
            rows = jnp.concatenate([rows, jnp.zeros((pad, 128), F32)], axis=0)
        out[base : base + plan.narrow_tail] = rows.astype(BF16)
    else:
        half = plan.narrow_tail // 2
        for index, rows in enumerate((high, low)):
            if half > plan.tail:
                rows = jnp.concatenate([rows, jnp.zeros((half - plan.tail, 128), F32)], axis=0)
            out[base + index * half : base + (index + 1) * half] = rows.astype(BF16)


def wide_tail(plan, values):
    values = values.astype(F32)
    if 2 * plan.wide_lanes <= 128:
        lane = lax.broadcasted_iota(jnp.int32, values.shape, 1)
        values = jnp.where(
            lane < plan.wide_lanes, values + pltpu.roll(values, 128 - plan.wide_lanes, 1), 0.0
        )
        return values[: plan.tail]
    half = plan.narrow_tail // 2
    return (values[:half] + values[half:])[: plan.tail]


def received(plan, got, slots, slot):
    if got.dtype == F32:
        rows = got[slot * plan.slot : (slot + 1) * plan.slot]
        return rows[: plan.main], rows[plan.main :]
    rows = got[slot * plan.narrow_slot : (slot + 1) * plan.narrow_slot].astype(F32)
    return rows[: plan.main], rows[plan.main : plan.main + 8] + rows[plan.main + 8 :]


def received_tail(plan, got, slots):
    if got.dtype == F32:
        return got[slots * plan.slot : slots * plan.slot + plan.tail]
    base = slots * plan.narrow_slot
    return wide_tail(plan, got[base : base + plan.narrow_tail])


def fold_kernel(plan, slots, direct, held, got, keep, *sends):
    tail = held[slots * plan.slot : slots * plan.slot + plan.tail] + received_tail(plan, got, slots)
    left = 1 if direct else slots // 2
    for slot in range(slots):
        main, channels = received(plan, got, slots, slot)
        main = main + held[slot * plan.slot : slot * plan.slot + plan.main]
        channels = channels + held[slot * plan.slot + plan.main : (slot + 1) * plan.slot]
        if direct and slot:
            narrow_slot(plan, sends[slot - 1], 0, main, channels)
        elif slot % 2:
            narrow_slot(plan, sends[0], slot // 2, main, channels)
        else:
            base = slot // 2 * plan.slot
            keep[base : base + plan.main] = main
            keep[base + plan.main : base + plan.slot] = channels
    keep[left * plan.slot : left * plan.slot + plan.tail] = tail
    for out in sends:
        narrow_tail(plan, out, left, tail)


def fold(plan, slots, direct, held, got):
    left = 1 if direct else slots // 2
    count = slots - 1 if direct else 1
    return pl.pallas_call(
        functools.partial(fold_kernel, plan, slots, direct),
        out_shape=(plan.wide(left),) + (plan.narrow(left),) * count,
        in_specs=[VMEM] * 2,
        out_specs=(VMEM,) * (1 + count),
        compiler_params=pltpu.CompilerParams(vmem_limit_bytes=32 * 2**20),
        name="fold",
    )(held, got)


def final_kernel(plan, taps_in, held, *refs):
    gots, (membrane, cycle, lfp, late) = refs[:-4], refs[-4:]
    trials, steps, delays = plan.trials, plan.steps, plan.delays
    main, channels = held[0 : plan.main], held[plan.main : plan.slot]
    tail = held[plan.slot : plan.slot + plan.tail]
    for got in gots:
        more, few = received(plan, got, 1, 0)
        main, channels = main + more, channels + few
        tail = tail + received_tail(plan, got, 1)
    for block in range(plan.blocks):
        lanes = slice(block * 128, block * 128 + 128)
        base = block * plan.each
        membrane[:, lanes] = main[base : base + trials]
        for delay in range(delays):
            spot = base + trials * (1 + delay)
            cycle[:, delay, lanes] = main[spot : spot + trials]
    signal = (tail / plan.pop_size).astype(BF16)
    products = None
    for part in range(plan.parts):
        rows = part * 128
        one = dot(
            signal[part * plan.signal_rows : (part + 1) * plan.signal_rows, : plan.wide_lanes],
            taps_in[rows : rows + plan.wide_lanes].astype(BF16),
        )
        products = one if products is None else products + one
    late[...] = jnp.zeros_like(late)
    width = products.shape[1]
    for lag in range(1, steps):
        moved = products
        if lag > 1:
            moved = pltpu.roll(products, width - (lag - 1) * plan.share, 1)
        top = trials * lag
        late[top : plan.width] += moved[0 : plan.width - top, 0:128]
    fresh = jnp.transpose(late[...])
    pieces = [channels]
    for group in range(1, plan.groups):
        pieces.append(pltpu.roll(channels, 128 - group * plan.width, 1))
    known = jnp.concatenate(pieces, axis=0)
    lane = lax.broadcasted_iota(jnp.int32, known.shape, 1)
    value = jnp.where(lane < plan.width, known, 0.0) + fresh[0 : known.shape[0]]
    old = lax.broadcasted_iota(jnp.int32, (128, 128), 0)
    new = lax.broadcasted_iota(jnp.int32, (128, 128), 1)
    swap = (old == (new % steps) * trials + new // steps).astype(F32)
    value = lax.dot_general(
        value, swap, (((1,), (0,)), ((), ())),
        precision=lax.Precision.HIGHEST, preferred_element_type=F32,
    )
    lfp[...] = value[0 : plan.share, 0 : plan.width]


def final(plan, neurons, taps_in, held, gots):
    trials, delays = plan.trials, plan.delays
    return pl.pallas_call(
        functools.partial(final_kernel, plan),
        out_shape=(
            jax.ShapeDtypeStruct((trials, neurons), F32),
            jax.ShapeDtypeStruct((trials, delays, neurons), F32),
            jax.ShapeDtypeStruct((plan.share, plan.width), F32),
        ),
        in_specs=[VMEM] * (2 + len(gots)),
        out_specs=(VMEM,) * 3,
        scratch_shapes=[pltpu.VMEM((128, 128), F32)],
        compiler_params=pltpu.CompilerParams(vmem_limit_bytes=16 * 2**20),
        name="final",
    )(taps_in, held, *gots)


def swap(values, bit, area_count):
    return lax.ppermute(values, "area", [(i, i ^ bit) for i in range(area_count)])


def body(
    spikes,
    weights,
    destination,
    target_block,
    delay_slot,
    population,
    leak_rate,
    membrane_start,
    cycle_start,
    history,
    lfp_kernel,
):
    area_count = lax.axis_size("area")
    neurons = weights.shape[1]
    blocks = neurons // 128
    trials, steps = spikes.shape[:2]
    delays = cycle_start.shape[1]
    channels = lfp_kernel.shape[0]
    pops = history.shape[0]
    me = lax.axis_index("area")
    plan = Plan(area_count, trials, steps, delays, neurons, pops, channels)
    share = plan.share
    spikes = jnp.transpose(spikes, (1, 0, 2))

    order = lax.broadcasted_iota(jnp.int32, spikes.shape, 0)
    last = jnp.max(jnp.where(spikes > 0, order, -1), axis=0)
    facts = jnp.concatenate(
        [
            last.astype(F32),
            leak_rate[None],
            population.astype(F32)[None],
            jnp.zeros((6 - trials, neurons), F32),
        ]
    )
    facts = jnp.transpose(facts.reshape(8, blocks, 128), (1, 0, 2)).reshape(1, blocks * 8, 128)
    reach = steps - 1
    taps_in = lfp_kernel[:, :, 1, :reach].astype(F32).reshape(area_count, share, pops, reach)
    taps_in = jnp.transpose(taps_in, (0, 2, 3, 1)).reshape(area_count, pops, reach * share)
    lanes = up(reach * share, 128)
    taps_in = jnp.pad(taps_in, ((0, 0), (0, 0), (0, lanes - reach * share)))
    taps_in = taps_in.reshape(1, area_count, pops * lanes // 128, 128)
    for level in range(area_count.bit_length() - 2, -1, -1):
        bit = 1 << level
        upper = lax.bitwise_and(lax.shift_right_logical(me, level), 1)
        count, left, rows = taps_in.shape[:3]
        halves = taps_in.reshape(count, 2, left // 2, rows, 128)
        stays = lax.dynamic_index_in_dim(halves, upper, 1, keepdims=False)
        goes = lax.dynamic_index_in_dim(halves, 1 - upper, 1, keepdims=False)
        size = facts.shape[0] * facts.shape[1]
        message = jnp.concatenate([facts.reshape(-1, 128), goes.reshape(-1, 128)])
        message = swap(message, bit, area_count)
        facts = jnp.stack([facts, message[:size].reshape(facts.shape)], axis=1)
        facts = facts.reshape(-1, blocks * 8, 128)
        came = message[size:].reshape(stays.shape)
        taps_in = jnp.stack(
            [jnp.where(upper == 0, stays, came), jnp.where(upper == 0, came, stays)], axis=1
        ).reshape(count * 2, left // 2, rows, 128)
    taps_in = taps_in.reshape(area_count * pops, lanes)

    total = payload_sums(
        spikes, weights, destination[:, 0], target_block, delay_slot, area_count, delays
    )
    known = known_lfp(spikes, population[None], history, lfp_kernel.reshape(channels, -1))
    known = known.reshape(area_count, share, 128)
    known = jnp.pad(known, ((0, 0), (0, plan.groups * 8 - share), (0, 0)))
    cycle = jnp.transpose(cycle_start, (1, 0, 2)).reshape(delays * trials, blocks, 128)
    cycle = jnp.transpose(cycle, (1, 0, 2))
    start = jnp.transpose(membrane_start.reshape(trials, blocks, 128), (1, 0, 2))
    keep, send = compress(plan, total, facts, cycle, start, known)

    slots = area_count // 2
    got = swap(send, 1, area_count)
    bit = 2
    while slots > 4:
        keep, send = fold(plan, slots, False, keep, got)
        got = swap(send, bit, area_count)
        slots, bit = slots // 2, bit * 2
    keep, *sends = fold(plan, slots, True, keep, got)
    gots = [swap(send, bit * index, area_count) for index, send in enumerate(sends, 1)]
    return tuple(final(plan, neurons, taps_in, keep, gots))


def solution(mesh):
    return jax.shard_map(
        body,
        mesh=mesh,
        in_specs=(
            P("runs", None, "area"),
            P("area", None, None),
            P("area", None),
            P("area"),
            P("area"),
            P("area"),
            P("area"),
            P("runs", "area"),
            P("runs", None, "area"),
            P("area", None, "runs", None),
            P(None, "area", None, None),
        ),
        out_specs=(P("runs", "area"), P("runs", None, "area"), P("area", "runs")),
        check_vma=False,
    )
```

```python
import functools

import jax
import jax.numpy as jnp
from jax import lax
from jax.experimental import pallas as pl
from jax.experimental.pallas import tpu as pltpu
from jax.sharding import PartitionSpec as P

BF16, F32 = jnp.bfloat16, jnp.float32
VMEM = pl.BlockSpec(memory_space=pltpu.VMEM)
HBM = pl.BlockSpec(memory_space=pltpu.HBM)
NT = (((1,), (1,)), ((), ()))


def up(value, unit):
    return -(-value // unit) * unit


def dot(left, right, dims=None):
    if dims is None:
        return jnp.dot(left, right, preferred_element_type=F32)
    return lax.dot_general(left, right, dims, preferred_element_type=F32)


def both(values):
    high = values.astype(BF16).astype(F32)
    return high, (values - high).astype(BF16).astype(F32)


def params(megabytes):
    return pltpu.CompilerParams(vmem_limit_bytes=megabytes * 2**20)


def cost(flops, size):
    return pl.CostEstimate(flops=flops, bytes_accessed=size, transcendentals=0)


class Plan:
    def __init__(self, area_count, trials, steps, delays, neurons, pops, channels):
        self.area_count, self.trials, self.steps, self.delays = area_count, trials, steps, delays
        self.lanes = area_count // 2
        self.blocks, self.pops = neurons // 128, pops
        self.pop_size = neurons / pops
        self.arriving = trials * (steps + delays)
        self.each = trials * (1 + delays)
        self.main = self.blocks * self.each
        self.main_up = up(self.main, 16)
        self.share = channels // area_count
        self.groups = up(self.share, 8) // 8
        self.width = trials * steps
        self.taps_lanes = up((steps - 1) * self.share, 128)
        self.taps = up(self.taps_lanes // 128 * pops, 8)
        self.signal = up(trials * (steps - 1), 8)
        self.signal_lanes = pops * self.lanes
        self.tile = min(self.signal_lanes, 128)
        self.tiles = up(self.signal_lanes, 128) // 128
        self.compact = 4 * self.tile <= 128 and self.signal % 2 == 0
        self.packed = self.signal // 2 if self.compact else 2 * self.tiles * self.signal
        self.packed_up = up(self.packed, 16)
        self.held = self.main_up + 16
        self.last = up(self.main + self.packed, 16)

    def keep(self, slots):
        rows = slots * self.held + self.tiles * self.signal
        return jax.ShapeDtypeStruct((rows, 128), F32)

    def slot(self, stage):
        return self.held + (2 * self.taps << stage)

    def send(self, slots, stage):
        return jax.ShapeDtypeStruct((slots * self.slot(stage) + self.packed_up, 128), BF16)

    def direct(self):
        rows = self.last + 16 + self.lanes // 4 * 2 * self.taps
        return jax.ShapeDtypeStruct((rows, 128), BF16)

    def carried(self):
        return jax.ShapeDtypeStruct((self.lanes * 2 * self.taps, 128), BF16)


def payload_kernel(
    destination, target_block, delay_slot, spikes, weights, keep, send, token,
    codes, given, held, plain, lagged, total, sems, part_sems,
):
    steps, trials, neurons = spikes.shape
    unit_count = weights.shape[0]
    delays = lagged.shape[0]
    blocks = neurons // 128
    half, rows = keep.shape[:2]
    chunk = held.shape[0] // part_sems.shape[0]
    chunks = unit_count // chunk
    small = [
        pltpu.make_async_copy(destination, codes.at[0], sems.at[0]),
        pltpu.make_async_copy(target_block, codes.at[1], sems.at[1]),
        pltpu.make_async_copy(delay_slot, codes.at[2], sems.at[2]),
        pltpu.make_async_copy(spikes, given, sems.at[3]),
    ]
    for copy in small:
        copy.start()

    def part(index):
        where = pl.ds(index * chunk, chunk)
        return pltpu.make_async_copy(weights.at[where], held.at[where], part_sems.at[index])

    for index in range(chunks):
        part(index).start()
    total[...] = jnp.zeros_like(total)
    plain[...] = jnp.zeros_like(plain)
    lagged[...] = jnp.zeros_like(lagged)
    token[...] = jnp.zeros_like(token)
    for copy in small:
        copy.wait()
    front = trials * delays
    for step in range(steps):
        start = front + step * trials
        plain[start : start + trials, :] = given[step].astype(F32)
    for delay in range(delays):
        start = front - trials * (delay + 1)
        lagged[delay, 0:rows, :] = plain[start : start + rows, :].astype(BF16)
    me = lax.axis_index("area")

    def some(index, _):
        part(index).wait()
        units = [index * chunk + inner for inner in range(chunk)]
        values = [
            dot(lagged[codes[2, unit]], held[unit])[0:rows].astype(BF16).astype(F32)
            for unit in units
        ]
        for unit, value in zip(units, values):
            device = lax.bitwise_xor(codes[0, unit], me)
            lane = lax.shift_right_logical(device, 1)
            place = lax.bitwise_and(device, 1) * half + lane * blocks + codes[1, unit]
            total[place] += value
        return 0

    lax.fori_loop(0, chunks, some, 0)
    keep[...] = total[0:half]
    send[...] = total[half:]


def payload_sums(plan, spikes, weights, destination, target_block, delay_slot):
    steps, trials, neurons = spikes.shape
    unit_count = weights.shape[0]
    rows, delays = plan.arriving, plan.delays
    chunk = next(size for size in (16, 12, 8, 6, 4, 3, 2, 1) if unit_count % size == 0)
    half = jax.ShapeDtypeStruct((plan.lanes * plan.blocks, rows, 128), F32)
    return pl.pallas_call(
        payload_kernel,
        out_shape=(half, half, jax.ShapeDtypeStruct((8, 128), F32)),
        in_specs=[HBM, HBM, HBM, HBM, HBM],
        out_specs=(VMEM, VMEM, VMEM),
        scratch_shapes=[
            pltpu.SMEM((3, unit_count), jnp.int32),
            pltpu.VMEM(spikes.shape, jnp.int32),
            pltpu.VMEM(weights.shape, BF16),
            pltpu.VMEM((trials * delays + rows, neurons), F32),
            pltpu.VMEM((delays, up(rows, 16), neurons), BF16),
            pltpu.VMEM((2 * plan.lanes * plan.blocks, rows, 128), F32),
            pltpu.SemaphoreType.DMA((4,)),
            pltpu.SemaphoreType.DMA((unit_count // chunk,)),
        ],
        compiler_params=params(52),
        cost_estimate=cost(2 * unit_count * 256 * neurons * 128, 2 * unit_count * neurons * 128),
        name="payload",
    )(destination, target_block, delay_slot, spikes, weights)


def known_kernel(spikes, population, history, kernel, out, series, fresh, lags):
    steps, trials, neurons = spikes.shape
    pops, kinds, _, taps = history.shape
    group = kinds * trials
    lane = lax.broadcasted_iota(jnp.int32, (pops * group, taps), 1)
    for pop in range(pops):
        for kind in range(kinds):
            start = pop * group + kind * trials
            series[start : start + trials, :] = history[pop, kind]
    flip = lax.broadcasted_iota(jnp.int32, (taps, taps), 0) + lax.broadcasted_iota(
        jnp.int32, (taps, taps), 1
    )
    flip = (flip == taps - 1).astype(F32).astype(BF16)
    back = dot(series[...].astype(BF16), flip)

    which = lax.broadcasted_iota(jnp.int32, (8, neurons), 0)
    member = (which == population[...]).astype(F32).astype(BF16)
    rows = spikes[...].reshape(steps * trials, neurons).astype(F32).astype(BF16)
    rates = (dot(member, rows, NT) / (neurons / pops)).astype(BF16)
    fresh[...] = jnp.zeros_like(fresh)
    row = lax.broadcasted_iota(jnp.int32, (steps * trials, taps), 0)
    column = lax.broadcasted_iota(jnp.int32, (steps * trials, taps), 1)
    for trial in range(trials):
        place = (row == (taps - 1 - column) * trials + trial).astype(F32).astype(BF16)
        placed = dot(rates, place)
        for pop in range(pops):
            fresh[pop * group + trial : pop * group + trial + 1, :] = placed[pop : pop + 1, :]
    lags[...] = jnp.zeros_like(lags)
    recent = fresh[...]
    for step in range(steps):
        shifted = jnp.where(lane >= taps - step, recent, back)
        if step:
            shifted = pltpu.roll(shifted, step, 1)
        for part in range(pops * kinds):
            for trial in range(trials):
                row = part * trials + trial
                spot = trial * steps + step
                lags[part, spot : spot + 1, :] = shifted[row : row + 1, :]
    total = dot(kernel[:, 0:taps], lags[0].astype(BF16), NT)
    for part in range(1, pops * kinds):
        total += dot(kernel[:, part * taps : (part + 1) * taps], lags[part].astype(BF16), NT)
    out[...] = total


def known_lfp(spikes, population, history, kernel):
    pops, kinds, trials, taps = history.shape
    channels = kernel.shape[0]
    return pl.pallas_call(
        known_kernel,
        out_shape=jax.ShapeDtypeStruct((channels, 128), F32),
        in_specs=[VMEM] * 4,
        out_specs=VMEM,
        scratch_shapes=[
            pltpu.VMEM((pops * kinds * trials, taps), F32),
            pltpu.VMEM((pops * kinds * trials, taps), F32),
            pltpu.VMEM((pops * kinds, 128, taps), F32),
        ],
        compiler_params=params(16),
        cost_estimate=cost(2 * channels * 128 * pops * kinds * taps * 4, 2 * kernel.size),
        name="known_lfp",
    )(spikes, population, history, kernel)


def pack_signal(plan, values):
    high, low = both(values)
    if not plan.compact:
        return jnp.concatenate([high, low], axis=0)
    half = plan.signal // 2
    out = high[:half]
    for index, piece in enumerate((high[half:], low[:half], low[half:]), 1):
        out = out + pltpu.roll(piece, index * plan.tile, 1)
    return out


def unpack_signal(plan, rows):
    if not plan.compact:
        half = plan.packed // 2
        return rows[:half] + rows[half:]
    lane = lax.broadcasted_iota(jnp.int32, rows.shape, 1)
    pieces = [rows] + [pltpu.roll(rows, 128 - index * plan.tile, 1) for index in (1, 2, 3)]
    value = jnp.concatenate([pieces[0] + pieces[2], pieces[1] + pieces[3]], axis=0)
    lane = lax.broadcasted_iota(jnp.int32, value.shape, 1)
    return jnp.where(lane < plan.tile, value, 0.0)


def compress_kernel(
    plan, mine, got, given, cycle, start, known, taps, keep, send, carried, signal, room
):
    trials, steps, delays, blocks = plan.trials, plan.steps, plan.delays, plan.blocks
    me = lax.axis_index("area")
    signal[...] = jnp.zeros_like(signal)
    room[...] = jnp.zeros_like(room)
    owner = lax.broadcasted_iota(jnp.int32, (plan.signal_lanes, 128), 0).astype(F32)

    def pair(index, _):
        sums = jnp.zeros((2 * plan.signal, plan.signal_lanes), F32)
        for bit in range(2):
            lane = 2 * index + bit
            own = (lane == 0).astype(F32)
            place = lax.bitwise_xor(2 * lane, me)
            first = (lax.shift_right_logical(place, 1) * plan.pops).astype(F32)
            tops, members = [], []
            for block in range(blocks):
                arriving = mine[lane * blocks + block] + got[lane * blocks + block]
                early = arriving[0 : trials * delays] + own * cycle[block]
                arriving = jnp.concatenate([early, arriving[trials * delays :]], axis=0)
                facts = given[lane, block * 8 : block * 8 + 8]
                last = facts[0:trials]
                leak = facts[trials : trials + 1] + facts[trials + 1 : trials + 2]
                population = facts[trials + 2 : trials + 3]
                membrane = own * start[block]
                for step in range(steps):
                    current = arriving[step * trials : (step + 1) * trials]
                    membrane = jnp.where(last < step, leak * membrane + current, 0.0)
                spot = block * plan.each
                room[bit, spot : spot + trials] = membrane
                room[bit, spot + trials : spot + plan.each] = arriving[trials * steps :]
                tops.append(arriving[0 : plan.signal])
                members.append((owner == population + first).astype(F32).astype(BF16))
            high, low = both(jnp.concatenate(tops, axis=1))
            stacked = jnp.concatenate([high, low], axis=0).astype(BF16)
            sums += dot(stacked, jnp.concatenate(members, axis=1), NT)
            channels, reach = [], []
            for core in range(2):
                there = lax.bitwise_xor(place, core)
                rows = known[there]
                packed = rows[0:8]
                for group in range(1, plan.groups):
                    packed += pltpu.roll(rows[group * 8 : group * 8 + 8], group * plan.width, 1)
                channels.append(packed)
                reach.append(taps[there])
            reach = jnp.concatenate(reach, axis=0).astype(BF16)
            spot = pl.multiple_of(lane * 2 * plan.taps, 16)
            carried[pl.ds(spot, 2 * plan.taps)] = reach
            if bit:
                base = pl.multiple_of(index * plan.slot(0), 16)
                send[pl.ds(base, plan.main_up)] = room[bit].astype(BF16)
                spot = pl.multiple_of(base + plan.main_up, 16)
                send[pl.ds(spot, 16)] = jnp.concatenate(channels, axis=0).astype(BF16)
                spot = pl.multiple_of(base + plan.held, 16)
                send[pl.ds(spot, 2 * plan.taps)] = reach
            else:
                base = pl.multiple_of(index * plan.held, 8)
                keep[pl.ds(base, plan.main_up)] = room[bit]
                keep[pl.ds(base + plan.main_up, 8)] = channels[0]
                keep[pl.ds(base + plan.main_up + 8, 8)] = channels[1]
        signal[...] += sums[: plan.signal] + sums[plan.signal :]
        return 0

    pairs = plan.lanes // 2
    lax.fori_loop(0, pairs, pair, 0, unroll=min(pairs, 4))
    pieces = []
    for tile in range(plan.tiles):
        values = signal[:, tile * 128 : tile * 128 + plan.tile]
        if plan.tile < 128:
            blank = jnp.zeros((plan.signal, 128 - plan.tile), F32)
            values = jnp.concatenate([values, blank], axis=1)
        pieces.append(values)
    values = jnp.concatenate(pieces, axis=0) if plan.tiles > 1 else pieces[0]
    keep[pairs * plan.held :] = values
    put_signal(plan, send, pairs * plan.slot(0), values)


def put_signal(plan, out, base, values):
    rows = pack_signal(plan, values)
    if plan.packed_up > plan.packed:
        blank = jnp.zeros((plan.packed_up - plan.packed, 128), F32)
        rows = jnp.concatenate([rows, blank], axis=0)
    out[base:] = rows.astype(BF16)


def compress(plan, mine, got, given, cycle, start, known, taps):
    return pl.pallas_call(
        functools.partial(compress_kernel, plan),
        out_shape=(plan.keep(plan.lanes // 2), plan.send(plan.lanes // 2, 0), plan.carried()),
        in_specs=[VMEM] * 7,
        out_specs=(VMEM,) * 3,
        scratch_shapes=[
            pltpu.VMEM((plan.signal, plan.signal_lanes), F32),
            pltpu.VMEM((2, plan.main_up, 128), F32),
        ],
        compiler_params=params(32),
        name="compress",
    )(mine, got, given, cycle, start, known, taps)


def fold_kernel(plan, slots, stage, direct, held, got, carried, keep, *refs):
    taps = 2 * plan.taps
    if direct:
        sends, (now, room) = refs[:-2], refs[-2:]
    else:
        sends, (now,) = refs[:1], refs[1:]
    def spot_of(lane, stage):
        rest = lane & ((1 << stage) - 1)
        return (lane >> (stage + 1)) * plan.slot(stage) + plan.held + rest * taps

    for lane in range(plan.lanes):
        rows = slice(lane * taps, (lane + 1) * taps)
        if lane >> stage & 1:
            spot = spot_of(lane, stage)
            now[rows] = got[spot : spot + taps]
        else:
            now[rows] = carried[rows]
    size = plan.slot(stage)
    tail = got[slots * size : slots * size + plan.packed_up].astype(F32)[: plan.packed]
    tail = unpack_signal(plan, tail)
    tail = tail + held[slots * plan.held :]
    left = 1 if direct else slots // 2
    for slot in range(slots):
        rows = got[slot * size : slot * size + plan.held].astype(F32)
        rows = rows + held[slot * plan.held : (slot + 1) * plan.held]
        if direct and slot:
            out = sends[slot - 1]
            room[0 : plan.main] = rows[: plan.main]
            room[plan.main : plan.main + plan.packed] = pack_signal(plan, tail)
            out[0 : plan.last] = room[...].astype(BF16)
            out[plan.last : plan.last + 16] = rows[plan.main_up :].astype(BF16)
            span = plan.lanes // 4 * taps
            out[plan.last + 16 :] = now[slot * span : (slot + 1) * span]
        elif slot % 2:
            base = slot // 2 * plan.slot(stage + 1)
            sends[0][base : base + plan.held] = rows.astype(BF16)
        else:
            keep[slot // 2 * plan.held : (slot // 2 + 1) * plan.held] = rows
    keep[left * plan.held :] = tail
    if not direct:
        for lane in range(plan.lanes):
            if lane >> (stage + 1) & 1:
                spot = spot_of(lane, stage + 1)
                sends[0][spot : spot + taps] = now[lane * taps : (lane + 1) * taps]
        put_signal(plan, sends[0], left * plan.slot(stage + 1), tail)


def fold(plan, slots, stage, direct, held, got, carried):
    left = 1 if direct else slots // 2
    scratch = []
    sends = (plan.send(left, stage + 1),)
    if direct:
        sends = (plan.direct(),) * (slots - 1)
        scratch = [pltpu.VMEM((plan.last, 128), F32)]
    return pl.pallas_call(
        functools.partial(fold_kernel, plan, slots, stage, direct),
        out_shape=(plan.keep(left),) + sends + (plan.carried(),),
        in_specs=[VMEM] * 3,
        out_specs=(VMEM,) * (2 + len(sends)),
        scratch_shapes=scratch,
        compiler_params=params(32),
        name="fold",
    )(held, got, carried)


def finish_kernel(plan, held, carried, *refs):
    gots, (membrane, cycle, own, other, mixed, reach, late, parts) = refs[:3], refs[3:]
    trials, steps, delays = plan.trials, plan.steps, plan.delays
    taps = 2 * plan.taps
    rows = held[0 : plan.held]
    main, channels = rows[: plan.main_up], rows[plan.main_up :]
    tail = held[plan.held :]
    parts[0 : plan.main] = main[: plan.main]
    for got in gots:
        arrived = got[0 : plan.last].astype(F32)
        parts[0 : plan.main] += arrived[: plan.main]
        channels = channels + got[plan.last : plan.last + 16].astype(F32)
        tail = tail + unpack_signal(plan, arrived[plan.main : plan.main + plan.packed])
    for block in range(plan.blocks):
        lanes = slice(block * 128, block * 128 + 128)
        base = block * plan.each
        membrane[:, lanes] = parts[base : base + trials]
        for delay in range(delays):
            spot = base + trials * (1 + delay)
            cycle[:, delay, lanes] = parts[spot : spot + trials]

    me = lax.shift_right_logical(lax.axis_index("area"), 1)
    span = plan.lanes // 4
    pops, wide = plan.pops, plan.taps_lanes // 128
    for lane in range(plan.lanes):
        far, near = divmod(lane, span)
        if far:
            spot = plan.last + 16 + near * taps
            slot = gots[far - 1][spot : spot + taps]
        else:
            slot = carried[lane * taps : (lane + 1) * taps]
        slot = slot.astype(F32)
        spot = lax.bitwise_xor(me, lane)
        for core in range(2):
            for tile in range(wide):
                top = core * plan.taps + tile * pops
                mixed[core, spot, 0:pops, tile * 128 : tile * 128 + 128] = slot[top : top + pops]
    for core in range(2):
        for lane in range(plan.lanes):
            reach[core, lane * pops : (lane + 1) * pops] = mixed[core, lane, 0:pops]
    new = lax.broadcasted_iota(jnp.int32, (plan.width, plan.signal), 0)
    old = lax.broadcasted_iota(jnp.int32, (plan.width, plan.signal), 1)
    order = (old == (new % steps) * trials + new // steps).astype(F32).astype(BF16)
    signal = (tail / plan.pop_size).astype(BF16)
    signal = [
        dot(order, signal[tile * plan.signal : (tile + 1) * plan.signal]).astype(BF16)
        for tile in range(plan.tiles)
    ]
    step_of = lax.broadcasted_iota(jnp.int32, (plan.width, 128), 0) % steps
    late[...] = jnp.zeros_like(late)
    sums = []
    for core in range(2):
        products = None
        for tile in range(plan.tiles):
            right = reach[core, tile * 128 : tile * 128 + plan.tile].astype(BF16)
            one = dot(signal[tile][:, : plan.tile], right)
            products = one if products is None else products + one
        value = jnp.zeros((plan.width, 128), F32)
        width = products.shape[1]
        for lag in range(1, steps):
            moved = products
            if lag > 1:
                moved = pltpu.roll(products, width - (lag - 1) * plan.share, 1)
            moved = pltpu.roll(moved[:, 0:128], lag, 0)
            value = value + jnp.where(step_of >= lag, moved, 0.0)
        sums.append(value)
    lane = lax.broadcasted_iota(jnp.int32, (plan.width, 128), 1)
    late[0 : plan.width] = jnp.where(lane < 64, sums[0], pltpu.roll(sums[1], 64, 1))
    fresh = jnp.transpose(late[...])
    lane = lax.broadcasted_iota(jnp.int32, (8, 128), 1)
    row = lax.broadcasted_iota(jnp.int32, (8, 128), 0)
    for core, out in enumerate((own, other)):
        value = channels[core * 8 : core * 8 + 8]
        for group in range(plan.groups):
            piece = fresh[core * 64 + group * 8 : core * 64 + group * 8 + 8]
            piece = jnp.where(lane < plan.width, piece, 0.0)
            if group:
                piece = pltpu.roll(piece, group * plan.width, 1)
            value = value + piece
        out[...] = value


def finish(plan, neurons, held, carried, gots):
    trials, delays = plan.trials, plan.delays
    part = jax.ShapeDtypeStruct((8, 128), F32)
    return pl.pallas_call(
        functools.partial(finish_kernel, plan),
        out_shape=(
            jax.ShapeDtypeStruct((trials, neurons), F32),
            jax.ShapeDtypeStruct((trials, delays, neurons), F32),
            part,
            part,
        ),
        in_specs=[VMEM] * (2 + len(gots)),
        out_specs=(VMEM,) * 4,
        scratch_shapes=[
            pltpu.VMEM((2, plan.lanes, 8, plan.taps_lanes), F32),
            pltpu.VMEM((2, plan.signal_lanes, plan.taps_lanes), F32),
            pltpu.VMEM((128, 128), F32),
            pltpu.VMEM((plan.main_up, 128), F32),
        ],
        compiler_params=params(16),
        name="finish",
    )(held, carried, *gots)


def lfp_kernel_body(plan, own, got, out):
    value = own[...] + got[...]
    pieces = [value]
    for group in range(1, plan.groups):
        pieces.append(pltpu.roll(value, 128 - group * plan.width, 1))
    value = jnp.concatenate(pieces, axis=0) if plan.groups > 1 else value
    out[...] = value[0 : plan.share, 0 : plan.width]


def lfp_sum(plan, own, got):
    return pl.pallas_call(
        functools.partial(lfp_kernel_body, plan),
        out_shape=jax.ShapeDtypeStruct((plan.share, plan.width), F32),
        in_specs=[VMEM] * 2,
        out_specs=VMEM,
        name="lfp_sum",
    )(own, got)


def swap(values, bit, area_count):
    return lax.ppermute(values, "area", [(i, i ^ bit) for i in range(area_count)])


def body(
    spikes,
    weights,
    destination,
    target_block,
    delay_slot,
    population,
    leak_rate,
    membrane_start,
    cycle_start,
    history,
    lfp_kernel,
):
    area_count = lax.axis_size("area")
    neurons = weights.shape[1]
    blocks = neurons // 128
    trials, steps = spikes.shape[:2]
    delays = cycle_start.shape[1]
    channels = lfp_kernel.shape[0]
    pops, kinds, _, taps = history.shape
    plan = Plan(area_count, trials, steps, delays, neurons, pops, channels)
    share = plan.share
    spikes = jnp.transpose(spikes, (1, 0, 2))
    top = area_count // 4
    far = [top, 2 * top, 3 * top]

    order = lax.broadcasted_iota(jnp.int32, spikes.shape, 0)
    last = jnp.max(jnp.where(spikes > 0, order, -1), axis=0)
    leak = lax.reduce_precision(leak_rate, 8, 7)
    facts = jnp.concatenate(
        [
            last.astype(F32),
            leak[None],
            (leak_rate - leak)[None],
            population.astype(F32)[None],
            jnp.zeros((5 - trials, neurons), F32),
        ]
    ).astype(BF16)
    facts = jnp.transpose(facts.reshape(8, blocks, 128), (1, 0, 2)).reshape(blocks * 8, 128)
    facts = jnp.stack([facts] + [swap(facts, bit, area_count) for bit in far])

    mine, goes, token = payload_sums(
        plan, spikes, weights, destination[:, 0], target_block, delay_slot
    )
    facts = facts + token[0, 0].astype(BF16)
    got = swap(goes, 1, area_count)
    bit = top // 2
    while bit > 1:
        more = swap(facts.reshape(-1, 128), bit, area_count).reshape(facts.shape)
        facts = jnp.stack([facts, more], axis=1).reshape(-1, blocks * 8, 128)
        bit //= 2
    facts = facts.astype(F32)

    flat = lax.optimization_barrier(lfp_kernel.reshape(channels, -1))
    known = known_lfp(spikes, population[None], history, flat)
    known = known.reshape(area_count, share, 128)
    known = jnp.pad(known, ((0, 0), (0, plan.groups * 8 - share), (0, 0)))
    reach = steps - 1
    first = [flat[:, (pop * kinds + 1) * taps :][:, :reach] for pop in range(pops)]
    first = jnp.stack(first, axis=1).astype(F32).reshape(area_count, share, pops, reach)
    first = jnp.transpose(first, (0, 2, 3, 1)).reshape(area_count, pops, reach * share)
    first = jnp.pad(first, ((0, 0), (0, 0), (0, plan.taps_lanes - reach * share)))
    first = first.reshape(area_count, pops, plan.taps_lanes // 128, 128)
    first = jnp.transpose(first, (0, 2, 1, 3)).reshape(area_count, -1, 128)
    first = jnp.pad(first, ((0, 0), (0, plan.taps - first.shape[1]), (0, 0)))

    cycle = jnp.transpose(cycle_start, (1, 0, 2)).reshape(delays * trials, blocks, 128)
    cycle = jnp.transpose(cycle, (1, 0, 2))
    start = jnp.transpose(membrane_start.reshape(trials, blocks, 128), (1, 0, 2))
    keep, send, carried = compress(plan, mine, got, facts, cycle, start, known, first)

    slots, stage = plan.lanes // 2, 0
    got = swap(send, 2, area_count)
    while slots > 4:
        keep, send, carried = fold(plan, slots, stage, False, keep, got, carried)
        slots, stage = slots // 2, stage + 1
        got = swap(send, 2 << stage, area_count)
    keep, *sends, carried = fold(plan, slots, stage, True, keep, got, carried)
    gots = [swap(send, bit, area_count) for send, bit in zip(sends, far)]
    membrane, cycle_out, own, other = finish(plan, neurons, keep, carried, gots)
    lfp = lfp_sum(plan, own, swap(other, 1, area_count))
    return membrane, cycle_out, lfp


def solution(mesh):
    return jax.shard_map(
        body,
        mesh=mesh,
        in_specs=(
            P("runs", None, "area"),
            P("area", None, None),
            P("area", None),
            P("area"),
            P("area"),
            P("area"),
            P("area"),
            P("runs", "area"),
            P("runs", None, "area"),
            P("area", None, "runs", None),
            P(None, "area", None, None),
        ),
        out_specs=(P("runs", "area"), P("runs", None, "area"), P("area", "runs")),
        check_vma=False,
    )
```

```python
import functools

import jax
import jax.numpy as jnp
from jax import lax
from jax.experimental import pallas as pl
from jax.experimental.pallas import tpu as pltpu
from jax.sharding import PartitionSpec as P

BF16, F32 = jnp.bfloat16, jnp.float32
VMEM = pl.BlockSpec(memory_space=pltpu.VMEM)
HBM = pl.BlockSpec(memory_space=pltpu.HBM)
NT = (((1,), (1,)), ((), ()))


def up(value, unit):
    return -(-value // unit) * unit


def dot(left, right, dims=None):
    if dims is None:
        return jnp.dot(left, right, preferred_element_type=F32)
    return lax.dot_general(left, right, dims, preferred_element_type=F32)


def both(values):
    high = values.astype(BF16).astype(F32)
    return high, (values - high).astype(BF16).astype(F32)


def params(megabytes):
    return pltpu.CompilerParams(vmem_limit_bytes=megabytes * 2**20)


class Plan:
    def __init__(self, area_count, trials, steps, delays, neurons, pops, channels):
        self.area_count, self.trials, self.steps, self.delays = area_count, trials, steps, delays
        self.lanes = area_count // 2
        self.top = self.lanes.bit_length() - 2
        self.blocks, self.pops = neurons // 128, pops
        self.pop_size = neurons / pops
        self.arriving = trials * (steps + delays)
        self.each = trials * (1 + delays)
        self.main = self.blocks * self.each
        self.main_up = up(self.main, 16)
        self.share = channels // area_count
        self.groups = up(self.share, 8) // 8
        self.width = trials * steps
        self.taps_lanes = up((steps - 1) * self.share, 128)
        self.taps = up(self.taps_lanes // 128 * pops, 8)
        self.signal = up(trials * (steps - 1), 8)
        self.signal_lanes = pops * self.lanes
        self.tile = min(self.signal_lanes, 128)
        self.tiles = up(self.signal_lanes, 128) // 128
        self.compact = 4 * self.tile <= 128 and self.signal % 2 == 0
        self.packed = self.signal // 2 if self.compact else 2 * self.tiles * self.signal
        self.packed_up = up(self.packed, 16)
        self.held = self.main_up + 16
        self.last = up(self.main + self.packed, 16)

    def mask(self, lane):
        return (2 * lane) ^ (lane >> self.top)

    def keep(self, slots):
        rows = slots * self.held + self.tiles * self.signal
        return jax.ShapeDtypeStruct((rows, 128), F32)

    def slot(self, stage):
        return self.held + (2 * self.taps << stage)

    def send(self, slots, stage):
        return jax.ShapeDtypeStruct((slots * self.slot(stage) + self.packed_up, 128), BF16)

    def direct(self):
        rows = self.last + 16 + self.lanes // 4 * 2 * self.taps
        return jax.ShapeDtypeStruct((rows, 128), BF16)

    def carried(self):
        return jax.ShapeDtypeStruct((self.lanes * 2 * self.taps, 128), BF16)


def facts_kernel(plan, spikes, leak, population, destination, target_block, delay_slot, out, codes):
    trials, steps = plan.trials, plan.steps
    last = jnp.full(spikes.shape[1:], -1, jnp.int32)
    for step in range(steps):
        last = jnp.where(spikes[step] > 0, step, last)
    high, low = both(leak[...].reshape(1, -1))
    blank = jnp.zeros((5 - trials, last.shape[1]), F32)
    rows = jnp.concatenate(
        [last.astype(F32), high, low, population[...].reshape(1, -1).astype(F32), blank], axis=0
    )
    rows = [rows[:, block * 128 : block * 128 + 128] for block in range(plan.blocks)]
    out[...] = jnp.concatenate(rows, axis=0).astype(BF16)
    for row, values in enumerate((destination, target_block, delay_slot)):
        codes[row : row + 1] = values[...].reshape(1, -1)


def facts_of(plan, spikes, leak, population, destination, target_block, delay_slot):
    codes = jax.ShapeDtypeStruct((3, destination.shape[0]), jnp.int32)
    return pl.pallas_call(
        functools.partial(facts_kernel, plan),
        out_shape=(jax.ShapeDtypeStruct((plan.blocks * 8, 128), BF16), codes),
        in_specs=[VMEM] * 6,
        out_specs=(VMEM, VMEM),
        name="facts",
    )(spikes, leak, population, destination, target_block, delay_slot)


def payload_kernel(
    plan, listed, spikes, weights, keep, send, token,
    codes, given, held, plain, lagged, total, sems, part_sems,
):
    steps, trials, neurons = spikes.shape
    unit_count = weights.shape[0]
    delays = lagged.shape[0]
    blocks = neurons // 128
    half, rows = keep.shape[:2]
    chunk = held.shape[0] // part_sems.shape[0]
    chunks = unit_count // chunk
    small = [
        pltpu.make_async_copy(listed, codes, sems.at[0]),
        pltpu.make_async_copy(spikes, given, sems.at[1]),
    ]
    for copy in small:
        copy.start()

    def part(index):
        where = pl.ds(index * chunk, chunk)
        return pltpu.make_async_copy(weights.at[where], held.at[where], part_sems.at[index])

    for index in range(chunks):
        part(index).start()
    total[...] = jnp.zeros_like(total)
    plain[...] = jnp.zeros_like(plain)
    lagged[...] = jnp.zeros_like(lagged)
    token[...] = jnp.zeros_like(token)
    for copy in small:
        copy.wait()
    front = trials * delays
    for step in range(steps):
        start = front + step * trials
        plain[start : start + trials, :] = given[step].astype(F32)
    for delay in range(delays):
        start = front - trials * (delay + 1)
        lagged[delay, 0:rows, :] = plain[start : start + rows, :].astype(BF16)
    me = lax.axis_index("area")

    def some(index, _):
        part(index).wait()
        units = [index * chunk + inner for inner in range(chunk)]
        values = [
            dot(lagged[codes[2, unit]], held[unit])[0:rows].astype(BF16).astype(F32)
            for unit in units
        ]
        for unit, value in zip(units, values):
            device = lax.bitwise_xor(codes[0, unit], me)
            lane = lax.shift_right_logical(device, 1)
            bit = lax.bitwise_and(lax.bitwise_xor(device, lane >> plan.top), 1)
            place = bit * half + lane * blocks + codes[1, unit]
            total[place] += value
        return 0

    lax.fori_loop(0, chunks, some, 0)
    keep[...] = total[0:half]
    send[...] = total[half:]


def payload_sums(plan, spikes, weights, codes):
    steps, trials, neurons = spikes.shape
    unit_count = weights.shape[0]
    rows, delays = plan.arriving, plan.delays
    chunk = next(size for size in (16, 12, 8, 6, 4, 3, 2, 1) if unit_count % size == 0)
    half = jax.ShapeDtypeStruct((plan.lanes * plan.blocks, rows, 128), F32)
    return pl.pallas_call(
        functools.partial(payload_kernel, plan),
        out_shape=(half, half, jax.ShapeDtypeStruct((16, 128), BF16)),
        in_specs=[HBM] * 3,
        out_specs=(VMEM,) * 3,
        scratch_shapes=[
            pltpu.SMEM((3, unit_count), jnp.int32),
            pltpu.VMEM(spikes.shape, jnp.int32),
            pltpu.VMEM(weights.shape, BF16),
            pltpu.VMEM((trials * delays + rows, neurons), F32),
            pltpu.VMEM((delays, up(rows, 16), neurons), BF16),
            pltpu.VMEM((2 * plan.lanes * plan.blocks, rows, 128), F32),
            pltpu.SemaphoreType.DMA((2,)),
            pltpu.SemaphoreType.DMA((unit_count // chunk,)),
        ],
        compiler_params=params(62),
        name="payload",
    )(codes, spikes, weights)


def known_kernel(plan, spikes, population, history, kernel, out, reach, series, fresh, lags):
    steps, trials, neurons = spikes.shape
    pops, kinds, _, taps = history.shape
    group = kinds * trials
    lane = lax.broadcasted_iota(jnp.int32, (pops * group, taps), 1)
    for pop in range(pops):
        for kind in range(kinds):
            start = pop * group + kind * trials
            series[start : start + trials, :] = history[pop, kind]
    flip = lax.broadcasted_iota(jnp.int32, (taps, taps), 0) + lax.broadcasted_iota(
        jnp.int32, (taps, taps), 1
    )
    flip = (flip == taps - 1).astype(F32).astype(BF16)
    back = dot(series[...].astype(BF16), flip)

    which = lax.broadcasted_iota(jnp.int32, (8, neurons), 0)
    member = (which == population[...].reshape(1, -1)).astype(F32).astype(BF16)
    rows = spikes[...].reshape(steps * trials, neurons).astype(F32).astype(BF16)
    rates = (dot(member, rows, NT) / (neurons / pops)).astype(BF16)
    fresh[...] = jnp.zeros_like(fresh)
    row = lax.broadcasted_iota(jnp.int32, (steps * trials, taps), 0)
    column = lax.broadcasted_iota(jnp.int32, (steps * trials, taps), 1)
    for trial in range(trials):
        place = (row == (taps - 1 - column) * trials + trial).astype(F32).astype(BF16)
        placed = dot(rates, place)
        for pop in range(pops):
            fresh[pop * group + trial : pop * group + trial + 1, :] = placed[pop : pop + 1, :]
    lags[...] = jnp.zeros_like(lags)
    recent = fresh[...]
    for step in range(steps):
        shifted = jnp.where(lane >= taps - step, recent, back)
        if step:
            shifted = pltpu.roll(shifted, step, 1)
        for part in range(pops * kinds):
            for trial in range(trials):
                row = part * trials + trial
                spot = trial * steps + step
                lags[part, spot : spot + 1, :] = shifted[row : row + 1, :]
    total = dot(kernel[:, 0:taps], lags[0].astype(BF16), NT)
    for part in range(1, pops * kinds):
        total += dot(kernel[:, part * taps : (part + 1) * taps], lags[part].astype(BF16), NT)
    out[...] = total

    channels, share, wide = kernel.shape[0], plan.share, plan.taps_lanes
    row = lax.broadcasted_iota(jnp.int32, (128, wide), 0)
    column = lax.broadcasted_iota(jnp.int32, (128, wide), 1)
    spread = (row == column // share).astype(F32).astype(BF16)
    row = lax.broadcasted_iota(jnp.int32, (channels, wide), 0)
    column = lax.broadcasted_iota(jnp.int32, (channels, wide), 1)
    same = (row % share == column % share) & (column < (steps - 1) * share)
    row = lax.broadcasted_iota(jnp.int32, (plan.area_count, channels), 0)
    column = lax.broadcasted_iota(jnp.int32, (plan.area_count, channels), 1)
    gather = (row == column // share).astype(F32).astype(BF16)
    reach[...] = jnp.zeros_like(reach)
    for pop in range(pops):
        start = (pop * kinds + 1) * taps
        wider = jnp.where(same, dot(kernel[:, start : start + 128], spread), 0.0)
        packed = dot(gather, wider.astype(BF16))
        for tile in range(wide // 128):
            reach[:, tile * pops + pop, :] = packed[:, tile * 128 : tile * 128 + 128]


def known_lfp(plan, spikes, population, history, kernel):
    pops, kinds, trials, taps = history.shape
    channels = kernel.shape[0]
    return pl.pallas_call(
        functools.partial(known_kernel, plan),
        out_shape=(
            jax.ShapeDtypeStruct((channels, 128), F32),
            jax.ShapeDtypeStruct((plan.area_count, plan.taps, 128), F32),
        ),
        in_specs=[VMEM] * 4,
        out_specs=(VMEM, VMEM),
        scratch_shapes=[
            pltpu.VMEM((pops * kinds * trials, taps), F32),
            pltpu.VMEM((pops * kinds * trials, taps), F32),
            pltpu.VMEM((pops * kinds, 128, taps), F32),
        ],
        compiler_params=params(16),
        name="known_lfp",
    )(spikes, population, history, kernel)


def pack_signal(plan, values):
    high, low = both(values)
    if not plan.compact:
        return jnp.concatenate([high, low], axis=0)
    half = plan.signal // 2
    out = high[:half]
    for index, piece in enumerate((high[half:], low[:half], low[half:]), 1):
        out = out + pltpu.roll(piece, index * plan.tile, 1)
    return out


def unpack_signal(plan, rows):
    if not plan.compact:
        half = plan.packed // 2
        return rows[:half] + rows[half:]
    lane = lax.broadcasted_iota(jnp.int32, rows.shape, 1)
    pieces = [rows] + [pltpu.roll(rows, 128 - index * plan.tile, 1) for index in (1, 2, 3)]
    value = jnp.concatenate([pieces[0] + pieces[2], pieces[1] + pieces[3]], axis=0)
    lane = lax.broadcasted_iota(jnp.int32, value.shape, 1)
    return jnp.where(lane < plan.tile, value, 0.0)


def compress_kernel(
    plan, mine, got, given, cycle, start, known, taps, keep, send, carried, signal, room
):
    trials, steps, delays, blocks = plan.trials, plan.steps, plan.delays, plan.blocks
    me = lax.axis_index("area")
    signal[...] = jnp.zeros_like(signal)
    room[...] = jnp.zeros_like(room)
    owner = lax.broadcasted_iota(jnp.int32, (plan.signal_lanes, 128), 0).astype(F32)

    def pair(index, _):
        sums = jnp.zeros((2 * plan.signal, plan.signal_lanes), F32)
        for bit in range(2):
            lane = 2 * index + bit
            own = (lane == 0).astype(F32)
            place = lax.bitwise_xor(plan.mask(lane), me)
            first = (lax.shift_right_logical(place, 1) * plan.pops).astype(F32)
            tops, members = [], []
            for block in range(blocks):
                arriving = mine[lane * blocks + block] + got[lane * blocks + block]
                early = arriving[0 : trials * delays] + own * cycle[block]
                arriving = jnp.concatenate([early, arriving[trials * delays :]], axis=0)
                facts = given[lane, block * 8 : block * 8 + 8]
                last = facts[0:trials]
                leak = facts[trials : trials + 1] + facts[trials + 1 : trials + 2]
                population = facts[trials + 2 : trials + 3]
                membrane = own * start[block]
                for step in range(steps):
                    current = arriving[step * trials : (step + 1) * trials]
                    membrane = jnp.where(last < step, leak * membrane + current, 0.0)
                spot = block * plan.each
                room[bit, spot : spot + trials] = membrane
                room[bit, spot + trials : spot + plan.each] = arriving[trials * steps :]
                tops.append(arriving[0 : plan.signal])
                members.append((owner == population + first).astype(F32).astype(BF16))
            high, low = both(jnp.concatenate(tops, axis=1))
            stacked = jnp.concatenate([high, low], axis=0).astype(BF16)
            sums += dot(stacked, jnp.concatenate(members, axis=1), NT)
            channels, reach = [], []
            for core in range(2):
                there = lax.bitwise_xor(place, core)
                rows = known[there]
                packed = rows[0:8]
                for group in range(1, plan.groups):
                    packed += pltpu.roll(rows[group * 8 : group * 8 + 8], group * plan.width, 1)
                channels.append(packed)
                reach.append(taps[there])
            reach = jnp.concatenate(reach, axis=0).astype(BF16)
            spot = pl.multiple_of(lane * 2 * plan.taps, 16)
            carried[pl.ds(spot, 2 * plan.taps)] = reach
            if bit:
                base = pl.multiple_of(index * plan.slot(0), 16)
                send[pl.ds(base, plan.main_up)] = room[bit].astype(BF16)
                spot = pl.multiple_of(base + plan.main_up, 16)
                send[pl.ds(spot, 16)] = jnp.concatenate(channels, axis=0).astype(BF16)
                spot = pl.multiple_of(base + plan.held, 16)
                send[pl.ds(spot, 2 * plan.taps)] = reach
            else:
                base = pl.multiple_of(index * plan.held, 8)
                keep[pl.ds(base, plan.main_up)] = room[bit]
                keep[pl.ds(base + plan.main_up, 8)] = channels[0]
                keep[pl.ds(base + plan.main_up + 8, 8)] = channels[1]
        signal[...] += sums[: plan.signal] + sums[plan.signal :]
        return 0

    pairs = plan.lanes // 2
    lax.fori_loop(0, pairs, pair, 0, unroll=min(pairs, 4))
    pieces = []
    for tile in range(plan.tiles):
        values = signal[:, tile * 128 : tile * 128 + plan.tile]
        if plan.tile < 128:
            blank = jnp.zeros((plan.signal, 128 - plan.tile), F32)
            values = jnp.concatenate([values, blank], axis=1)
        pieces.append(values)
    values = jnp.concatenate(pieces, axis=0) if plan.tiles > 1 else pieces[0]
    keep[pairs * plan.held :] = values
    put_signal(plan, send, pairs * plan.slot(0), values)


def put_signal(plan, out, base, values):
    rows = pack_signal(plan, values)
    if plan.packed_up > plan.packed:
        blank = jnp.zeros((plan.packed_up - plan.packed, 128), F32)
        rows = jnp.concatenate([rows, blank], axis=0)
    out[base:] = rows.astype(BF16)


def compress(plan, mine, got, given, cycle, start, known, taps):
    return pl.pallas_call(
        functools.partial(compress_kernel, plan),
        out_shape=(plan.keep(plan.lanes // 2), plan.send(plan.lanes // 2, 0), plan.carried()),
        in_specs=[VMEM] * 7,
        out_specs=(VMEM,) * 3,
        scratch_shapes=[
            pltpu.VMEM((plan.signal, plan.signal_lanes), F32),
            pltpu.VMEM((2, plan.main_up, 128), F32),
        ],
        compiler_params=params(32),
        name="compress",
    )(mine, got, given, cycle, start, known, taps)


def fold_kernel(plan, slots, stage, direct, held, got, carried, keep, *refs):
    taps = 2 * plan.taps
    if direct:
        sends, (now, room) = refs[:-2], refs[-2:]
    else:
        sends, (now,) = refs[:1], refs[1:]
    def spot_of(lane, stage):
        rest = lane & ((1 << stage) - 1)
        return (lane >> (stage + 1)) * plan.slot(stage) + plan.held + rest * taps

    for lane in range(plan.lanes):
        rows = slice(lane * taps, (lane + 1) * taps)
        if lane >> stage & 1:
            spot = spot_of(lane, stage)
            now[rows] = got[spot : spot + taps]
        else:
            now[rows] = carried[rows]
    size = plan.slot(stage)
    tail = got[slots * size : slots * size + plan.packed_up].astype(F32)[: plan.packed]
    tail = unpack_signal(plan, tail)
    tail = tail + held[slots * plan.held :]
    left = 1 if direct else slots // 2
    for slot in range(slots):
        rows = got[slot * size : slot * size + plan.held].astype(F32)
        rows = rows + held[slot * plan.held : (slot + 1) * plan.held]
        if direct and slot:
            out = sends[slot - 1]
            room[0 : plan.main] = rows[: plan.main]
            room[plan.main : plan.main + plan.packed] = pack_signal(plan, tail)
            out[0 : plan.last] = room[...].astype(BF16)
            out[plan.last : plan.last + 16] = rows[plan.main_up :].astype(BF16)
            span = plan.lanes // 4 * taps
            out[plan.last + 16 :] = now[slot * span : (slot + 1) * span]
        elif slot % 2:
            base = slot // 2 * plan.slot(stage + 1)
            sends[0][base : base + plan.held] = rows.astype(BF16)
        else:
            keep[slot // 2 * plan.held : (slot // 2 + 1) * plan.held] = rows
    keep[left * plan.held :] = tail
    if not direct:
        for lane in range(plan.lanes):
            if lane >> (stage + 1) & 1:
                spot = spot_of(lane, stage + 1)
                sends[0][spot : spot + taps] = now[lane * taps : (lane + 1) * taps]
        put_signal(plan, sends[0], left * plan.slot(stage + 1), tail)


def fold(plan, slots, stage, direct, held, got, carried):
    left = 1 if direct else slots // 2
    scratch = []
    sends = (plan.send(left, stage + 1),)
    if direct:
        sends = (plan.direct(),) * (slots - 1)
        scratch = [pltpu.VMEM((plan.last, 128), F32)]
    return pl.pallas_call(
        functools.partial(fold_kernel, plan, slots, stage, direct),
        out_shape=(plan.keep(left),) + sends + (plan.carried(),),
        in_specs=[VMEM] * 3,
        out_specs=(VMEM,) * (2 + len(sends)),
        scratch_shapes=scratch,
        compiler_params=params(32),
        name="fold",
    )(held, got, carried)


def finish_kernel(plan, held, carried, *refs):
    gots, (membrane, cycle, own, other, mixed, reach, late, parts) = refs[:3], refs[3:]
    trials, steps, delays = plan.trials, plan.steps, plan.delays
    taps = 2 * plan.taps
    rows = held[0 : plan.held]
    main, channels = rows[: plan.main_up], rows[plan.main_up :]
    tail = held[plan.held :]
    parts[0 : plan.main] = main[: plan.main]
    for got in gots:
        arrived = got[0 : plan.last].astype(F32)
        parts[0 : plan.main] += arrived[: plan.main]
        channels = channels + got[plan.last : plan.last + 16].astype(F32)
        tail = tail + unpack_signal(plan, arrived[plan.main : plan.main + plan.packed])
    for block in range(plan.blocks):
        lanes = slice(block * 128, block * 128 + 128)
        base = block * plan.each
        membrane[:, lanes] = parts[base : base + trials]
        for delay in range(delays):
            spot = base + trials * (1 + delay)
            cycle[:, delay, lanes] = parts[spot : spot + trials]

    me = lax.shift_right_logical(lax.axis_index("area"), 1)
    span = plan.lanes // 4
    pops, wide = plan.pops, plan.taps_lanes // 128
    for lane in range(plan.lanes):
        far, near = divmod(lane, span)
        if far:
            spot = plan.last + 16 + near * taps
            slot = gots[far - 1][spot : spot + taps]
        else:
            slot = carried[lane * taps : (lane + 1) * taps]
        slot = slot.astype(F32)
        spot = lax.bitwise_xor(me, lane)
        for core in range(2):
            for tile in range(wide):
                top = core * plan.taps + tile * pops
                mixed[core, spot, 0:pops, tile * 128 : tile * 128 + 128] = slot[top : top + pops]
    for core in range(2):
        for lane in range(plan.lanes):
            reach[core, lane * pops : (lane + 1) * pops] = mixed[core, lane, 0:pops]
    new = lax.broadcasted_iota(jnp.int32, (plan.width, plan.signal), 0)
    old = lax.broadcasted_iota(jnp.int32, (plan.width, plan.signal), 1)
    order = (old == (new % steps) * trials + new // steps).astype(F32).astype(BF16)
    signal = (tail / plan.pop_size).astype(BF16)
    signal = [
        dot(order, signal[tile * plan.signal : (tile + 1) * plan.signal]).astype(BF16)
        for tile in range(plan.tiles)
    ]
    step_of = lax.broadcasted_iota(jnp.int32, (plan.width, 128), 0) % steps
    late[...] = jnp.zeros_like(late)
    sums = []
    for core in range(2):
        products = None
        for tile in range(plan.tiles):
            right = reach[core, tile * 128 : tile * 128 + plan.tile].astype(BF16)
            one = dot(signal[tile][:, : plan.tile], right)
            products = one if products is None else products + one
        value = jnp.zeros((plan.width, 128), F32)
        width = products.shape[1]
        for lag in range(1, steps):
            moved = products
            if lag > 1:
                moved = pltpu.roll(products, width - (lag - 1) * plan.share, 1)
            moved = pltpu.roll(moved[:, 0:128], lag, 0)
            value = value + jnp.where(step_of >= lag, moved, 0.0)
        sums.append(value)
    lane = lax.broadcasted_iota(jnp.int32, (plan.width, 128), 1)
    late[0 : plan.width] = jnp.where(lane < 64, sums[0], pltpu.roll(sums[1], 64, 1))
    fresh = jnp.transpose(late[...])
    lane = lax.broadcasted_iota(jnp.int32, (8, 128), 1)
    row = lax.broadcasted_iota(jnp.int32, (8, 128), 0)
    for core, out in enumerate((own, other)):
        value = channels[core * 8 : core * 8 + 8]
        for group in range(plan.groups):
            piece = fresh[core * 64 + group * 8 : core * 64 + group * 8 + 8]
            piece = jnp.where(lane < plan.width, piece, 0.0)
            if group:
                piece = pltpu.roll(piece, group * plan.width, 1)
            value = value + piece
        out[...] = value


def finish(plan, neurons, held, carried, gots):
    trials, delays = plan.trials, plan.delays
    part = jax.ShapeDtypeStruct((8, 128), F32)
    return pl.pallas_call(
        functools.partial(finish_kernel, plan),
        out_shape=(
            jax.ShapeDtypeStruct((trials, neurons), F32),
            jax.ShapeDtypeStruct((trials, delays, neurons), F32),
            part,
            part,
        ),
        in_specs=[VMEM] * (2 + len(gots)),
        out_specs=(VMEM,) * 4,
        scratch_shapes=[
            pltpu.VMEM((2, plan.lanes, 8, plan.taps_lanes), F32),
            pltpu.VMEM((2, plan.signal_lanes, plan.taps_lanes), F32),
            pltpu.VMEM((128, 128), F32),
            pltpu.VMEM((plan.main_up, 128), F32),
        ],
        compiler_params=params(16),
        name="finish",
    )(held, carried, *gots)


def swap(values, bit, area_count):
    return lax.ppermute(values, "area", [(i, i ^ bit) for i in range(area_count)])


def body(
    spikes,
    weights,
    destination,
    target_block,
    delay_slot,
    population,
    leak_rate,
    membrane_start,
    cycle_start,
    history,
    lfp_kernel,
):
    area_count = lax.axis_size("area")
    neurons = weights.shape[1]
    blocks = neurons // 128
    trials, steps = spikes.shape[:2]
    delays = cycle_start.shape[1]
    channels = lfp_kernel.shape[0]
    pops = history.shape[0]
    plan = Plan(area_count, trials, steps, delays, neurons, pops, channels)
    share = plan.share
    spikes = jnp.transpose(spikes, (1, 0, 2))
    quarter = plan.lanes // 4
    far = [plan.mask(index * quarter) for index in (1, 2, 3)]

    facts, codes = facts_of(
        plan, spikes, leak_rate, population, destination[:, 0], target_block, delay_slot
    )
    facts = [facts] + [swap(facts, mask, area_count) for mask in far]
    mine, goes, token = payload_sums(plan, spikes, weights, codes)
    got = swap(goes, 1, area_count)
    size = blocks * 8
    facts = jnp.concatenate(facts)
    lane = quarter // 2
    while lane:
        count = facts.shape[0]
        message = facts
        if lane == quarter // 2:
            blank = jnp.zeros((max(0, 512 - count - token.shape[0]), 128), BF16)
            message = jnp.concatenate([facts, token, blank])
        more = swap(message, plan.mask(lane), area_count)[:count]
        facts = jnp.stack([facts.reshape(-1, size, 128), more.reshape(-1, size, 128)], axis=1)
        facts = facts.reshape(-1, 128)
        lane //= 2
    facts = facts.astype(F32).reshape(-1, size, 128)

    flat = lfp_kernel.reshape(channels, -1)
    known, first = known_lfp(plan, spikes, population, history, flat)
    known = known.reshape(area_count, share, 128)
    known = jnp.pad(known, ((0, 0), (0, plan.groups * 8 - share), (0, 0)))

    cycle = jnp.transpose(cycle_start, (1, 0, 2)).reshape(delays * trials, blocks, 128)
    cycle = jnp.transpose(cycle, (1, 0, 2))
    start = jnp.transpose(membrane_start.reshape(trials, blocks, 128), (1, 0, 2))
    keep, send, carried = compress(plan, mine, got, facts, cycle, start, known, first)

    slots, stage = plan.lanes // 2, 0
    got = swap(send, plan.mask(1), area_count)
    while slots > 4:
        keep, send, carried = fold(plan, slots, stage, False, keep, got, carried)
        slots, stage = slots // 2, stage + 1
        got = swap(send, plan.mask(1 << stage), area_count)
    keep, *sends, carried = fold(plan, slots, stage, True, keep, got, carried)
    gots = [swap(send, mask, area_count) for send, mask in zip(sends, far)]
    membrane, cycle_out, own, other = finish(plan, neurons, keep, carried, gots)
    lfp = own + swap(other, 1, area_count)
    width = plan.width
    lfp = [lfp[:, group * width : (group + 1) * width] for group in range(plan.groups)]
    lfp = jnp.concatenate(lfp, axis=0)[:share]
    return membrane, cycle_out, lfp


def solution(mesh):
    return jax.shard_map(
        body,
        mesh=mesh,
        in_specs=(
            P("runs", None, "area"),
            P("area", None, None),
            P("area", None),
            P("area"),
            P("area"),
            P("area"),
            P("area"),
            P("runs", "area"),
            P("runs", None, "area"),
            P("area", None, "runs", None),
            P(None, "area", None, None),
        ),
        out_specs=(P("runs", "area"), P("runs", None, "area"), P("area", "runs")),
        check_vma=False,
    )
```

```python
import functools

import jax
import jax.numpy as jnp
from jax import lax
from jax.experimental import pallas as pl
from jax.experimental.pallas import tpu as pltpu
from jax.sharding import PartitionSpec as P

BF16, F32 = jnp.bfloat16, jnp.float32
PAD = 112
VMEM = pl.BlockSpec(memory_space=pltpu.VMEM)
HBM = pl.BlockSpec(memory_space=pltpu.HBM)
NT = (((1,), (1,)), ((), ()))


def up(value, unit):
    return -(-value // unit) * unit


def dot(left, right, dims=None):
    if dims is None:
        return jnp.dot(left, right, preferred_element_type=F32)
    return lax.dot_general(left, right, dims, preferred_element_type=F32)


def both(values):
    high = values.astype(BF16).astype(F32)
    return high, (values - high).astype(BF16).astype(F32)


def params(megabytes):
    return pltpu.CompilerParams(vmem_limit_bytes=megabytes * 2**20)


class Plan:
    def __init__(self, area_count, trials, steps, delays, neurons, pops, channels):
        self.area_count, self.trials, self.steps, self.delays = area_count, trials, steps, delays
        self.lanes = area_count // 2
        self.top = self.lanes.bit_length() - 2
        self.blocks, self.pops = neurons // 128, pops
        self.pop_size = neurons / pops
        self.arriving = trials * (steps + delays)
        self.each = trials * (1 + delays)
        self.main = self.blocks * self.each
        self.main_up = up(self.main, 16)
        self.share = channels // area_count
        self.groups = up(self.share, 8) // 8
        self.width = trials * steps
        self.taps_lanes = up((steps - 1) * self.share, 128)
        self.taps = up(self.taps_lanes // 128 * pops, 8)
        self.signal = up(trials * (steps - 1), 8)
        self.signal_lanes = pops * self.lanes
        self.tile = min(self.signal_lanes, 128)
        self.tiles = up(self.signal_lanes, 128) // 128
        self.compact = 4 * self.tile <= 128 and self.signal % 2 == 0
        self.packed = self.signal // 2 if self.compact else 2 * self.tiles * self.signal
        self.packed_up = up(self.packed, 16)
        self.held = self.main_up + 16
        self.last = up(self.main + self.packed, 16)

    def mask(self, lane):
        return (2 * lane) ^ (lane >> self.top)

    def keep(self, slots):
        rows = slots * self.held + self.tiles * self.signal
        return jax.ShapeDtypeStruct((rows, 128), F32)

    def slot(self, stage):
        return self.held + (2 * self.taps << stage)

    def send(self, slots, stage):
        return jax.ShapeDtypeStruct((slots * self.slot(stage) + self.packed_up, 128), BF16)

    def direct(self):
        rows = self.last + 16 + self.lanes // 4 * 2 * self.taps
        return jax.ShapeDtypeStruct((rows, 128), BF16)

    def carried(self):
        return jax.ShapeDtypeStruct((self.lanes * 2 * self.taps, 128), BF16)


def facts_kernel(plan, spikes, leak, population, destination, target_block, delay_slot, out, given):
    trials, steps = plan.trials, plan.steps
    last = jnp.full(spikes.shape[1:], -1, jnp.int32)
    for step in range(steps):
        last = jnp.where(spikes[step] > 0, step, last)
        given[step * trials : (step + 1) * trials] = spikes[step]
    blank = jnp.zeros((6 - trials, last.shape[1]), F32)
    rows = [last.astype(F32), leak[...].reshape(1, -1), population[...].astype(F32).reshape(1, -1)]
    rows = jnp.concatenate(rows + [blank], axis=0)
    for block in range(plan.blocks):
        out[block * 8 : block * 8 + 8] = rows[:, block * 128 : block * 128 + 128]
    given[plan.width :] = jnp.zeros((given.shape[0] - plan.width, given.shape[1]), jnp.int32)
    for row, values in enumerate((destination, target_block, delay_slot)):
        row += up(plan.width, 8)
        given[row : row + 1, 0 : values.shape[0]] = values[...].reshape(1, -1)


def facts_of(plan, spikes, leak, population, destination, target_block, delay_slot):
    rows = up(plan.width, 8) + 8
    return pl.pallas_call(
        functools.partial(facts_kernel, plan),
        out_shape=(
            jax.ShapeDtypeStruct((plan.blocks * 8, 128), F32),
            jax.ShapeDtypeStruct((rows, spikes.shape[2]), jnp.int32),
        ),
        in_specs=[VMEM] * 6,
        out_specs=(VMEM, VMEM),
        name="facts",
    )(spikes, leak, population, destination, target_block, delay_slot)


def payload_kernel(
    plan, given, weights, keep, send, token, codes, held, plain, lagged, total, sem, part_sems
):
    steps, trials = plan.steps, plan.trials
    unit_count = weights.shape[0]
    delays = lagged.shape[0]
    blocks = plan.blocks
    half, rows = keep.shape[:2]
    chunk = held.shape[0] // part_sems.shape[0]
    chunks = unit_count // chunk
    listed = pltpu.make_async_copy(given.at[pl.ds(up(plan.width, 8), 8)], codes, sem)
    listed.start()

    def part(index):
        where = pl.ds(index * chunk, chunk)
        return pltpu.make_async_copy(weights.at[where], held.at[where], part_sems.at[index])

    for index in range(chunks):
        part(index).start()
    total[...] = jnp.zeros_like(total)
    plain[...] = jnp.zeros_like(plain)
    lagged[...] = jnp.zeros_like(lagged)
    token[...] = jnp.zeros_like(token)
    front = trials * delays
    for step in range(steps):
        start = front + step * trials
        plain[start : start + trials, :] = given[step * trials : (step + 1) * trials].astype(F32)
    for delay in range(delays):
        start = front - trials * (delay + 1)
        lagged[delay, 0:rows, :] = plain[start : start + rows, :].astype(BF16)
    listed.wait()
    me = lax.axis_index("area")

    def some(index, _):
        part(index).wait()
        units = [index * chunk + inner for inner in range(chunk)]
        values = [
            dot(lagged[codes[2, unit]], held[unit])[0:rows].astype(BF16).astype(F32)
            for unit in units
        ]
        for unit, value in zip(units, values):
            device = lax.bitwise_xor(codes[0, unit], me)
            lane = lax.shift_right_logical(device, 1)
            bit = lax.bitwise_and(lax.bitwise_xor(device, lane >> plan.top), 1)
            place = bit * half + lane * blocks + codes[1, unit]
            total[place] += value
        return 0

    lax.fori_loop(0, chunks, some, 0)
    keep[...] = total[0:half]
    send[...] = total[half:]


def payload_sums(plan, given, weights):
    unit_count, neurons = weights.shape[:2]
    rows, delays = plan.arriving, plan.delays
    chunk = next(size for size in (16, 12, 8, 6, 4, 3, 2, 1) if unit_count % size == 0)
    half = jax.ShapeDtypeStruct((plan.lanes * plan.blocks, rows, 128), F32)
    return pl.pallas_call(
        functools.partial(payload_kernel, plan),
        out_shape=(half, half, jax.ShapeDtypeStruct((8, 128), F32)),
        in_specs=[VMEM, HBM],
        out_specs=(VMEM,) * 3,
        scratch_shapes=[
            pltpu.SMEM((8, neurons), jnp.int32),
            pltpu.VMEM(weights.shape, BF16),
            pltpu.VMEM((plan.trials * delays + rows, neurons), F32),
            pltpu.VMEM((delays, up(rows, 16), neurons), BF16),
            pltpu.VMEM((2 * plan.lanes * plan.blocks, rows, 128), F32),
            pltpu.SemaphoreType.DMA,
            pltpu.SemaphoreType.DMA((unit_count // chunk,)),
        ],
        compiler_params=params(52),
        name="payload",
    )(given, weights)


def known_kernel(plan, given, population, history, kernel, out, reach, series, fresh, lags, sorted_):
    steps, trials, neurons = plan.steps, plan.trials, given.shape[1]
    pops, kinds, _, taps = history.shape
    channels, parts = kernel.shape[0], pops * kinds
    some = 256 // parts
    row = lax.broadcasted_iota(jnp.int32, (256, 256), 0)
    column = lax.broadcasted_iota(jnp.int32, (256, 256), 1)
    order = (column == row % some * parts + row // some).astype(F32).astype(BF16)
    for index in range(channels // some):
        rows = kernel[index * some : (index + 1) * some].reshape(256, taps)
        rows = dot(order, rows).astype(BF16)
        for part in range(parts):
            sorted_[part, index * some : (index + 1) * some] = rows[part * some : (part + 1) * some]
    group = kinds * trials
    lane = lax.broadcasted_iota(jnp.int32, (pops * group, taps), 1)
    for pop in range(pops):
        for kind in range(kinds):
            start = pop * group + kind * trials
            series[start : start + trials, :] = history[pop, kind]
    flip = lax.broadcasted_iota(jnp.int32, (taps, taps), 0) + lax.broadcasted_iota(
        jnp.int32, (taps, taps), 1
    )
    flip = (flip == taps - 1).astype(F32).astype(BF16)
    back = dot(series[...].astype(BF16), flip)

    which = lax.broadcasted_iota(jnp.int32, (8, neurons), 0)
    member = (which == population[...].reshape(1, -1)).astype(F32).astype(BF16)
    rows = given[0 : steps * trials].astype(F32).astype(BF16)
    rates = (dot(member, rows, NT) / (neurons / pops)).astype(BF16)
    fresh[...] = jnp.zeros_like(fresh)
    row = lax.broadcasted_iota(jnp.int32, (steps * trials, taps), 0)
    column = lax.broadcasted_iota(jnp.int32, (steps * trials, taps), 1)
    for trial in range(trials):
        place = (row == (taps - 1 - column) * trials + trial).astype(F32).astype(BF16)
        placed = dot(rates, place)
        for pop in range(pops):
            fresh[pop * group + trial : pop * group + trial + 1, :] = placed[pop : pop + 1, :]
    lags[...] = jnp.zeros_like(lags)
    recent = fresh[...]
    for step in range(steps):
        shifted = jnp.where(lane >= taps - step, recent, back)
        if step:
            shifted = pltpu.roll(shifted, step, 1)
        for part in range(pops * kinds):
            for trial in range(trials):
                row = part * trials + trial
                spot = trial * steps + step
                lags[part, spot : spot + 1, :] = shifted[row : row + 1, :]
    total = dot(sorted_[0], lags[0].astype(BF16), NT)
    for part in range(1, parts):
        total += dot(sorted_[part], lags[part].astype(BF16), NT)
    out[...] = total

    share, wide = plan.share, plan.taps_lanes
    row = lax.broadcasted_iota(jnp.int32, (128, wide), 0)
    column = lax.broadcasted_iota(jnp.int32, (128, wide), 1)
    spread = (row == column // share).astype(F32).astype(BF16)
    row = lax.broadcasted_iota(jnp.int32, (channels, wide), 0)
    column = lax.broadcasted_iota(jnp.int32, (channels, wide), 1)
    same = (row % share == column % share) & (column < (steps - 1) * share)
    row = lax.broadcasted_iota(jnp.int32, (plan.area_count, channels), 0)
    column = lax.broadcasted_iota(jnp.int32, (plan.area_count, channels), 1)
    gather = (row == column // share).astype(F32).astype(BF16)
    reach[...] = jnp.zeros_like(reach)
    for pop in range(pops):
        wider = jnp.where(same, dot(sorted_[pop * kinds + 1, :, 0:128], spread), 0.0)
        packed = dot(gather, wider.astype(BF16))
        for tile in range(wide // 128):
            reach[:, tile * pops + pop, :] = packed[:, tile * 128 : tile * 128 + 128]


def known_lfp(plan, given, population, history, kernel):
    pops, kinds, trials, taps = history.shape
    channels = kernel.shape[0]
    return pl.pallas_call(
        functools.partial(known_kernel, plan),
        out_shape=(
            jax.ShapeDtypeStruct((channels, 128), F32),
            jax.ShapeDtypeStruct((plan.area_count, plan.taps, 128), F32),
        ),
        in_specs=[VMEM] * 4,
        out_specs=(VMEM, VMEM),
        scratch_shapes=[
            pltpu.VMEM((pops * kinds * trials, taps), F32),
            pltpu.VMEM((pops * kinds * trials, taps), F32),
            pltpu.VMEM((pops * kinds, 128, taps), F32),
            pltpu.VMEM((pops * kinds, channels, taps), BF16),
        ],
        compiler_params=params(16),
        name="known_lfp",
    )(given, population, history, kernel)


def pack_signal(plan, values):
    high, low = both(values)
    if not plan.compact:
        return jnp.concatenate([high, low], axis=0)
    half = plan.signal // 2
    out = high[:half]
    for index, piece in enumerate((high[half:], low[:half], low[half:]), 1):
        out = out + pltpu.roll(piece, index * plan.tile, 1)
    return out


def unpack_signal(plan, rows):
    if not plan.compact:
        half = plan.packed // 2
        return rows[:half] + rows[half:]
    lane = lax.broadcasted_iota(jnp.int32, rows.shape, 1)
    pieces = [rows] + [pltpu.roll(rows, 128 - index * plan.tile, 1) for index in (1, 2, 3)]
    value = jnp.concatenate([pieces[0] + pieces[2], pieces[1] + pieces[3]], axis=0)
    lane = lax.broadcasted_iota(jnp.int32, value.shape, 1)
    return jnp.where(lane < plan.tile, value, 0.0)


def compress_kernel(
    plan, mine, got, near, far, cycle, start, known, taps, keep, send, carried, signal, room
):
    trials, steps, delays, blocks = plan.trials, plan.steps, plan.delays, plan.blocks
    me = lax.axis_index("area")
    signal[...] = jnp.zeros_like(signal)
    room[...] = jnp.zeros_like(room)
    owner = lax.broadcasted_iota(jnp.int32, (plan.signal_lanes, 128), 0).astype(F32)

    def pair(index, _):
        sums = jnp.zeros((2 * plan.signal, plan.signal_lanes), F32)
        for bit in range(2):
            lane = 2 * index + bit
            own = (lane == 0).astype(F32)
            place = lax.bitwise_xor(plan.mask(lane), me)
            first = (lax.shift_right_logical(place, 1) * plan.pops).astype(F32)
            tops, members = [], []
            for block in range(blocks):
                arriving = mine[lane * blocks + block] + got[lane * blocks + block]
                early = arriving[0 : trials * delays] + own * cycle[block]
                arriving = jnp.concatenate([early, arriving[trials * delays :]], axis=0)
                spot = pl.multiple_of((index * blocks + block) * 8, 8)
                facts = (far if bit else near)[pl.ds(spot, 8)]
                last = facts[0:trials]
                leak = facts[trials : trials + 1]
                population = facts[trials + 1 : trials + 2]
                membrane = own * start[block]
                for step in range(steps):
                    current = arriving[step * trials : (step + 1) * trials]
                    membrane = jnp.where(last < step, leak * membrane + current, 0.0)
                spot = block * plan.each
                room[bit, spot : spot + trials] = membrane
                room[bit, spot + trials : spot + plan.each] = arriving[trials * steps :]
                tops.append(arriving[0 : plan.signal])
                members.append((owner == population + first).astype(F32).astype(BF16))
            high, low = both(jnp.concatenate(tops, axis=1))
            stacked = jnp.concatenate([high, low], axis=0).astype(BF16)
            sums += dot(stacked, jnp.concatenate(members, axis=1), NT)
            channels, reach = [], []
            for core in range(2):
                there = lax.bitwise_xor(place, core)
                rows = known[there]
                packed = rows[0:8]
                for group in range(1, plan.groups):
                    packed += pltpu.roll(rows[group * 8 : group * 8 + 8], group * plan.width, 1)
                channels.append(packed)
                reach.append(taps[there])
            reach = jnp.concatenate(reach, axis=0).astype(BF16)
            spot = pl.multiple_of(lane * 2 * plan.taps, 16)
            carried[pl.ds(spot, 2 * plan.taps)] = reach
            if bit:
                base = pl.multiple_of(index * plan.slot(0), 16)
                send[pl.ds(base, plan.main_up)] = room[bit].astype(BF16)
                spot = pl.multiple_of(base + plan.main_up, 16)
                send[pl.ds(spot, 16)] = jnp.concatenate(channels, axis=0).astype(BF16)
                spot = pl.multiple_of(base + plan.held, 16)
                send[pl.ds(spot, 2 * plan.taps)] = reach
            else:
                base = pl.multiple_of(index * plan.held, 8)
                keep[pl.ds(base, plan.main_up)] = room[bit]
                keep[pl.ds(base + plan.main_up, 8)] = channels[0]
                keep[pl.ds(base + plan.main_up + 8, 8)] = channels[1]
        signal[...] += sums[: plan.signal] + sums[plan.signal :]
        return 0

    pairs = plan.lanes // 2
    lax.fori_loop(0, pairs, pair, 0, unroll=min(pairs, 4))
    pieces = []
    for tile in range(plan.tiles):
        values = signal[:, tile * 128 : tile * 128 + plan.tile]
        if plan.tile < 128:
            blank = jnp.zeros((plan.signal, 128 - plan.tile), F32)
            values = jnp.concatenate([values, blank], axis=1)
        pieces.append(values)
    values = jnp.concatenate(pieces, axis=0) if plan.tiles > 1 else pieces[0]
    keep[pairs * plan.held :] = values
    put_signal(plan, send, pairs * plan.slot(0), values)


def put_signal(plan, out, base, values):
    rows = pack_signal(plan, values)
    if plan.packed_up > plan.packed:
        blank = jnp.zeros((plan.packed_up - plan.packed, 128), F32)
        rows = jnp.concatenate([rows, blank], axis=0)
    out[base:] = rows.astype(BF16)


def compress(plan, mine, got, near, far, cycle, start, known, taps):
    return pl.pallas_call(
        functools.partial(compress_kernel, plan),
        out_shape=(plan.keep(plan.lanes // 2), plan.send(plan.lanes // 2, 0), plan.carried()),
        in_specs=[VMEM] * 8,
        out_specs=(VMEM,) * 3,
        scratch_shapes=[
            pltpu.VMEM((plan.signal, plan.signal_lanes), F32),
            pltpu.VMEM((2, plan.main_up, 128), F32),
        ],
        compiler_params=params(32),
        name="compress",
    )(mine, got, near, far, cycle, start, known, taps)


def fold_kernel(plan, slots, stage, direct, held, got, carried, keep, *refs):
    taps = 2 * plan.taps
    if direct:
        sends, (now, room) = refs[:-2], refs[-2:]
    else:
        sends, (now,) = refs[:1], refs[1:]
    def spot_of(lane, stage):
        rest = lane & ((1 << stage) - 1)
        return (lane >> (stage + 1)) * plan.slot(stage) + plan.held + rest * taps

    for lane in range(plan.lanes):
        rows = slice(lane * taps, (lane + 1) * taps)
        if lane >> stage & 1:
            spot = spot_of(lane, stage)
            now[rows] = got[spot : spot + taps]
        else:
            now[rows] = carried[rows]
    size = plan.slot(stage)
    tail = got[slots * size : slots * size + plan.packed_up].astype(F32)[: plan.packed]
    tail = unpack_signal(plan, tail)
    tail = tail + held[slots * plan.held :]
    left = 1 if direct else slots // 2
    for slot in range(slots):
        rows = got[slot * size : slot * size + plan.held].astype(F32)
        rows = rows + held[slot * plan.held : (slot + 1) * plan.held]
        if direct and slot:
            out = sends[slot - 1]
            room[0 : plan.main] = rows[: plan.main]
            room[plan.main : plan.main + plan.packed] = pack_signal(plan, tail)
            out[0 : plan.last] = room[...].astype(BF16)
            out[plan.last : plan.last + 16] = rows[plan.main_up :].astype(BF16)
            span = plan.lanes // 4 * taps
            out[plan.last + 16 :] = now[slot * span : (slot + 1) * span]
        elif slot % 2:
            base = slot // 2 * plan.slot(stage + 1)
            sends[0][base : base + plan.held] = rows.astype(BF16)
        else:
            keep[slot // 2 * plan.held : (slot // 2 + 1) * plan.held] = rows
    keep[left * plan.held :] = tail
    if not direct:
        for lane in range(plan.lanes):
            if lane >> (stage + 1) & 1:
                spot = spot_of(lane, stage + 1)
                sends[0][spot : spot + taps] = now[lane * taps : (lane + 1) * taps]
        put_signal(plan, sends[0], left * plan.slot(stage + 1), tail)


def fold(plan, slots, stage, direct, held, got, carried):
    left = 1 if direct else slots // 2
    scratch = []
    sends = (plan.send(left, stage + 1),)
    if direct:
        sends = (plan.direct(),) * (slots - 1)
        scratch = [pltpu.VMEM((plan.last, 128), F32)]
    return pl.pallas_call(
        functools.partial(fold_kernel, plan, slots, stage, direct),
        out_shape=(plan.keep(left),) + sends + (plan.carried(),),
        in_specs=[VMEM] * 3,
        out_specs=(VMEM,) * (2 + len(sends)),
        scratch_shapes=scratch,
        compiler_params=params(32),
        name="fold",
    )(held, got, carried)


def finish_kernel(plan, held, carried, *refs):
    gots, (membrane, cycle, own, other, mixed, reach, late, parts) = refs[:3], refs[3:]
    trials, steps, delays = plan.trials, plan.steps, plan.delays
    taps = 2 * plan.taps
    rows = held[0 : plan.held]
    main, channels = rows[: plan.main_up], rows[plan.main_up :]
    tail = held[plan.held :]
    parts[0 : plan.main] = main[: plan.main]
    for got in gots:
        arrived = got[0 : plan.last].astype(F32)
        parts[0 : plan.main] += arrived[: plan.main]
        channels = channels + got[plan.last : plan.last + 16].astype(F32)
        tail = tail + unpack_signal(plan, arrived[plan.main : plan.main + plan.packed])
    for block in range(plan.blocks):
        lanes = slice(block * 128, block * 128 + 128)
        base = block * plan.each
        membrane[:, lanes] = parts[base : base + trials]
        for delay in range(delays):
            spot = base + trials * (1 + delay)
            cycle[:, delay, lanes] = parts[spot : spot + trials]

    me = lax.shift_right_logical(lax.axis_index("area"), 1)
    span = plan.lanes // 4
    pops, wide = plan.pops, plan.taps_lanes // 128
    for lane in range(plan.lanes):
        far, near = divmod(lane, span)
        if far:
            spot = plan.last + 16 + near * taps
            slot = gots[far - 1][spot : spot + taps]
        else:
            slot = carried[lane * taps : (lane + 1) * taps]
        slot = slot.astype(F32)
        spot = lax.bitwise_xor(me, lane)
        for core in range(2):
            for tile in range(wide):
                top = core * plan.taps + tile * pops
                mixed[core, spot, 0:pops, tile * 128 : tile * 128 + 128] = slot[top : top + pops]
    for core in range(2):
        for lane in range(plan.lanes):
            reach[core, lane * pops : (lane + 1) * pops] = mixed[core, lane, 0:pops]
    new = lax.broadcasted_iota(jnp.int32, (plan.width, plan.signal), 0)
    old = lax.broadcasted_iota(jnp.int32, (plan.width, plan.signal), 1)
    order = (old == (new % steps) * trials + new // steps).astype(F32).astype(BF16)
    signal = (tail / plan.pop_size).astype(BF16)
    signal = [
        dot(order, signal[tile * plan.signal : (tile + 1) * plan.signal]).astype(BF16)
        for tile in range(plan.tiles)
    ]
    step_of = lax.broadcasted_iota(jnp.int32, (plan.width, 128), 0) % steps
    late[...] = jnp.zeros_like(late)
    sums = []
    for core in range(2):
        products = None
        for tile in range(plan.tiles):
            right = reach[core, tile * 128 : tile * 128 + plan.tile].astype(BF16)
            one = dot(signal[tile][:, : plan.tile], right)
            products = one if products is None else products + one
        value = jnp.zeros((plan.width, 128), F32)
        width = products.shape[1]
        for lag in range(1, steps):
            moved = products
            if lag > 1:
                moved = pltpu.roll(products, width - (lag - 1) * plan.share, 1)
            moved = pltpu.roll(moved[:, 0:128], lag, 0)
            value = value + jnp.where(step_of >= lag, moved, 0.0)
        sums.append(value)
    lane = lax.broadcasted_iota(jnp.int32, (plan.width, 128), 1)
    late[0 : plan.width] = jnp.where(lane < 64, sums[0], pltpu.roll(sums[1], 64, 1))
    fresh = jnp.transpose(late[...])
    lane = lax.broadcasted_iota(jnp.int32, (8, 128), 1)
    row = lax.broadcasted_iota(jnp.int32, (8, 128), 0)
    for core, out in enumerate((own, other)):
        value = channels[core * 8 : core * 8 + 8]
        for group in range(plan.groups):
            piece = fresh[core * 64 + group * 8 : core * 64 + group * 8 + 8]
            piece = jnp.where(lane < plan.width, piece, 0.0)
            if group:
                piece = pltpu.roll(piece, group * plan.width, 1)
            value = value + piece
        out[...] = value


def finish(plan, neurons, held, carried, gots):
    trials, delays = plan.trials, plan.delays
    part = jax.ShapeDtypeStruct((8, 128), F32)
    return pl.pallas_call(
        functools.partial(finish_kernel, plan),
        out_shape=(
            jax.ShapeDtypeStruct((trials, neurons), F32),
            jax.ShapeDtypeStruct((trials, delays, neurons), F32),
            part,
            part,
        ),
        in_specs=[VMEM] * (2 + len(gots)),
        out_specs=(VMEM,) * 4,
        scratch_shapes=[
            pltpu.VMEM((2, plan.lanes, 8, plan.taps_lanes), F32),
            pltpu.VMEM((2, plan.signal_lanes, plan.taps_lanes), F32),
            pltpu.VMEM((128, 128), F32),
            pltpu.VMEM((plan.main_up, 128), F32),
        ],
        compiler_params=params(16),
        name="finish",
    )(held, carried, *gots)


def swap(values, bit, area_count):
    return lax.ppermute(values, "area", [(i, i ^ bit) for i in range(area_count)])


def body(
    spikes,
    weights,
    destination,
    target_block,
    delay_slot,
    population,
    leak_rate,
    membrane_start,
    cycle_start,
    history,
    lfp_kernel,
):
    area_count = lax.axis_size("area")
    neurons = weights.shape[1]
    blocks = neurons // 128
    trials, steps = spikes.shape[:2]
    delays = cycle_start.shape[1]
    channels = lfp_kernel.shape[0]
    pops = history.shape[0]
    plan = Plan(area_count, trials, steps, delays, neurons, pops, channels)
    share = plan.share
    spikes = jnp.transpose(spikes, (1, 0, 2))
    quarter = plan.lanes // 4
    far = [plan.mask(index * quarter) for index in (1, 2, 3)]

    facts, given = facts_of(
        plan, spikes, leak_rate, population, destination[:, 0], target_block, delay_slot
    )
    size = facts.shape[0]
    facts = [facts] + [swap(facts, mask, area_count) for mask in far]
    mine, goes, token = payload_sums(plan, given, weights)
    got = swap(goes, 1, area_count)
    blank = jnp.zeros((max(0, PAD - 4 * size - token.shape[0]), 128), F32)
    near = jnp.concatenate(facts + [token, blank])
    count, lane = 4 * size, quarter // 2
    while True:
        more = swap(near, plan.mask(lane), area_count)
        if lane == 1:
            break
        near = jnp.stack(
            [near[:count].reshape(-1, size, 128), more[:count].reshape(-1, size, 128)], axis=1
        ).reshape(-1, 128)
        count, lane = 2 * count, lane // 2

    known, first = known_lfp(plan, given, population, history, lfp_kernel)
    known = known.reshape(area_count, share, 128)
    known = jnp.pad(known, ((0, 0), (0, plan.groups * 8 - share), (0, 0)))

    cycle = jnp.transpose(cycle_start, (1, 0, 2)).reshape(delays * trials, blocks, 128)
    cycle = jnp.transpose(cycle, (1, 0, 2))
    start = jnp.transpose(membrane_start.reshape(trials, blocks, 128), (1, 0, 2))
    keep, send, carried = compress(plan, mine, got, near, more, cycle, start, known, first)

    slots, stage = plan.lanes // 2, 0
    got = swap(send, plan.mask(1), area_count)
    while slots > 4:
        keep, send, carried = fold(plan, slots, stage, False, keep, got, carried)
        slots, stage = slots // 2, stage + 1
        got = swap(send, plan.mask(1 << stage), area_count)
    keep, *sends, carried = fold(plan, slots, stage, True, keep, got, carried)
    gots = [swap(send, mask, area_count) for send, mask in zip(sends, far)]
    membrane, cycle_out, own, other = finish(plan, neurons, keep, carried, gots)
    lfp = own + swap(other, 1, area_count)
    width = plan.width
    lfp = [lfp[:, group * width : (group + 1) * width] for group in range(plan.groups)]
    lfp = jnp.concatenate(lfp, axis=0)[:share]
    return membrane, cycle_out, lfp


def solution(mesh):
    return jax.shard_map(
        body,
        mesh=mesh,
        in_specs=(
            P("runs", None, "area"),
            P("area", None, None),
            P("area", None),
            P("area"),
            P("area"),
            P("area"),
            P("area"),
            P("runs", "area"),
            P("runs", None, "area"),
            P("area", None, "runs", None),
            P(None, "area", None, None),
        ),
        out_specs=(P("runs", "area"), P("runs", None, "area"), P("area", "runs")),
        check_vma=False,
    )
```

```python
import functools

import jax
import jax.numpy as jnp
from jax import lax
from jax.experimental import pallas as pl
from jax.experimental.pallas import tpu as pltpu
from jax.sharding import PartitionSpec as P

BF16, F32 = jnp.bfloat16, jnp.float32
PAD = 112
LATE = (2, 3, 1)
VMEM = pl.BlockSpec(memory_space=pltpu.VMEM)
HBM = pl.BlockSpec(memory_space=pltpu.HBM)
NT = (((1,), (1,)), ((), ()))


def up(value, unit):
    return -(-value // unit) * unit


def dot(left, right, dims=None):
    if dims is None:
        return jnp.dot(left, right, preferred_element_type=F32)
    return lax.dot_general(left, right, dims, preferred_element_type=F32)


def both(values):
    high = values.astype(BF16).astype(F32)
    return high, (values - high).astype(BF16).astype(F32)


def params(megabytes):
    return pltpu.CompilerParams(vmem_limit_bytes=megabytes * 2**20)


class Plan:
    def __init__(self, area_count, trials, steps, delays, neurons, pops, channels):
        self.area_count, self.trials, self.steps, self.delays = area_count, trials, steps, delays
        self.lanes = area_count // 2
        self.top = self.lanes.bit_length() - 2
        self.blocks, self.pops = neurons // 128, pops
        self.pop_size = neurons / pops
        self.arriving = trials * (steps + delays)
        self.each = trials * (1 + delays)
        self.main = self.blocks * self.each
        self.main_up = up(self.main, 16)
        self.share = channels // area_count
        self.groups = up(self.share, 8) // 8
        self.width = trials * steps
        self.taps_lanes = up((steps - 1) * self.share, 128)
        self.taps = up(self.taps_lanes // 128 * pops, 8)
        self.signal = up(trials * (steps - 1), 8)
        self.signal_lanes = pops * self.lanes
        self.tile = min(self.signal_lanes, 128)
        self.tiles = up(self.signal_lanes, 128) // 128
        self.compact = 4 * self.tile <= 128 and self.signal % 2 == 0
        self.packed = self.signal // 2 if self.compact else 2 * self.tiles * self.signal
        self.packed_up = up(self.packed, 16)
        self.held = self.main_up + 16
        self.last = up(self.main + self.packed, 16)

    def mask(self, lane):
        return (2 * lane) ^ (lane >> self.top)

    def keep(self, slots):
        rows = slots * self.held + self.tiles * self.signal
        return jax.ShapeDtypeStruct((rows, 128), F32)

    def slot(self, stage):
        return self.held + (2 * self.taps << stage)

    def send(self, slots, stage):
        return jax.ShapeDtypeStruct((slots * self.slot(stage) + self.packed_up, 128), BF16)

    def direct(self):
        rows = self.last + 16 + self.lanes // 4 * 2 * self.taps
        return jax.ShapeDtypeStruct((rows, 128), BF16)

    def carried(self):
        return jax.ShapeDtypeStruct((self.lanes * 2 * self.taps, 128), BF16)


def facts_kernel(plan, spikes, leak, population, destination, target_block, delay_slot, out, given):
    trials, steps = plan.trials, plan.steps
    last = jnp.full(spikes.shape[1:], -1, jnp.int32)
    for step in range(steps):
        last = jnp.where(spikes[step] > 0, step, last)
        given[step * trials : (step + 1) * trials] = spikes[step]
    blank = jnp.zeros((6 - trials, last.shape[1]), F32)
    rows = [last.astype(F32), leak[...].reshape(1, -1), population[...].astype(F32).reshape(1, -1)]
    rows = jnp.concatenate(rows + [blank], axis=0)
    for block in range(plan.blocks):
        out[block * 8 : block * 8 + 8] = rows[:, block * 128 : block * 128 + 128]
    given[plan.width :] = jnp.zeros((given.shape[0] - plan.width, given.shape[1]), jnp.int32)
    for row, values in enumerate((destination, target_block, delay_slot)):
        row += up(plan.width, 8)
        given[row : row + 1, 0 : values.shape[0]] = values[...].reshape(1, -1)


def facts_of(plan, spikes, leak, population, destination, target_block, delay_slot):
    rows = up(plan.width, 8) + 8
    return pl.pallas_call(
        functools.partial(facts_kernel, plan),
        out_shape=(
            jax.ShapeDtypeStruct((plan.blocks * 8, 128), F32),
            jax.ShapeDtypeStruct((rows, spikes.shape[2]), jnp.int32),
        ),
        in_specs=[VMEM] * 6,
        out_specs=(VMEM, VMEM),
        name="facts",
    )(spikes, leak, population, destination, target_block, delay_slot)


def payload_kernel(
    plan, given, weights, keep, send, token, codes, held, plain, lagged, total, sem, part_sems
):
    steps, trials = plan.steps, plan.trials
    unit_count = weights.shape[0]
    delays = lagged.shape[0]
    blocks = plan.blocks
    half, rows = keep.shape[:2]
    chunk = held.shape[0] // part_sems.shape[0]
    chunks = unit_count // chunk
    listed = pltpu.make_async_copy(given.at[pl.ds(up(plan.width, 8), 8)], codes, sem)
    listed.start()

    def part(index):
        where = pl.ds(index * chunk, chunk)
        return pltpu.make_async_copy(weights.at[where], held.at[where], part_sems.at[index])

    for index in range(chunks):
        part(index).start()
    total[...] = jnp.zeros_like(total)
    plain[...] = jnp.zeros_like(plain)
    lagged[...] = jnp.zeros_like(lagged)
    token[...] = jnp.zeros_like(token)
    front = trials * delays
    for step in range(steps):
        start = front + step * trials
        plain[start : start + trials, :] = given[step * trials : (step + 1) * trials].astype(F32)
    for delay in range(delays):
        start = front - trials * (delay + 1)
        lagged[delay, 0:rows, :] = plain[start : start + rows, :].astype(BF16)
    listed.wait()
    me = lax.axis_index("area")

    def some(index, _):
        part(index).wait()
        units = [index * chunk + inner for inner in range(chunk)]
        values = [
            dot(lagged[codes[2, unit]], held[unit])[0:rows].astype(BF16).astype(F32)
            for unit in units
        ]
        for unit, value in zip(units, values):
            device = lax.bitwise_xor(codes[0, unit], me)
            lane = lax.shift_right_logical(device, 1)
            bit = lax.bitwise_and(lax.bitwise_xor(device, lane >> plan.top), 1)
            place = bit * half + lane * blocks + codes[1, unit]
            total[place] += value
        return 0

    lax.fori_loop(0, chunks, some, 0)
    keep[...] = total[0:half]
    send[...] = total[half:]


def payload_sums(plan, given, weights):
    unit_count, neurons = weights.shape[:2]
    rows, delays = plan.arriving, plan.delays
    chunk = next(size for size in (16, 12, 8, 6, 4, 3, 2, 1) if unit_count % size == 0)
    half = jax.ShapeDtypeStruct((plan.lanes * plan.blocks, rows, 128), F32)
    return pl.pallas_call(
        functools.partial(payload_kernel, plan),
        out_shape=(half, half, jax.ShapeDtypeStruct((8, 128), F32)),
        in_specs=[VMEM, HBM],
        out_specs=(VMEM,) * 3,
        scratch_shapes=[
            pltpu.SMEM((8, neurons), jnp.int32),
            pltpu.VMEM(weights.shape, BF16),
            pltpu.VMEM((plan.trials * delays + rows, neurons), F32),
            pltpu.VMEM((delays, up(rows, 16), neurons), BF16),
            pltpu.VMEM((2 * plan.lanes * plan.blocks, rows, 128), F32),
            pltpu.SemaphoreType.DMA,
            pltpu.SemaphoreType.DMA((unit_count // chunk,)),
        ],
        compiler_params=params(52),
        name="payload",
    )(given, weights)


def known_kernel(plan, given, population, history, kernel, out, reach, series, fresh, lags, sorted_):
    steps, trials, neurons = plan.steps, plan.trials, given.shape[1]
    pops, kinds, _, taps = history.shape
    channels, parts = kernel.shape[0], pops * kinds
    some = 256 // parts
    row = lax.broadcasted_iota(jnp.int32, (256, 256), 0)
    column = lax.broadcasted_iota(jnp.int32, (256, 256), 1)
    order = (column == row % some * parts + row // some).astype(F32).astype(BF16)
    for index in range(channels // some):
        rows = kernel[index * some : (index + 1) * some].reshape(256, taps)
        rows = dot(order, rows).astype(BF16)
        for part in range(parts):
            sorted_[part, index * some : (index + 1) * some] = rows[part * some : (part + 1) * some]
    group = kinds * trials
    lane = lax.broadcasted_iota(jnp.int32, (pops * group, taps), 1)
    for pop in range(pops):
        for kind in range(kinds):
            start = pop * group + kind * trials
            series[start : start + trials, :] = history[pop, kind]
    flip = lax.broadcasted_iota(jnp.int32, (taps, taps), 0) + lax.broadcasted_iota(
        jnp.int32, (taps, taps), 1
    )
    flip = (flip == taps - 1).astype(F32).astype(BF16)
    back = dot(series[...].astype(BF16), flip)

    which = lax.broadcasted_iota(jnp.int32, (8, neurons), 0)
    member = (which == population[...].reshape(1, -1)).astype(F32).astype(BF16)
    rows = given[0 : steps * trials].astype(F32).astype(BF16)
    rates = (dot(member, rows, NT) / (neurons / pops)).astype(BF16)
    fresh[...] = jnp.zeros_like(fresh)
    row = lax.broadcasted_iota(jnp.int32, (steps * trials, taps), 0)
    column = lax.broadcasted_iota(jnp.int32, (steps * trials, taps), 1)
    for trial in range(trials):
        place = (row == (taps - 1 - column) * trials + trial).astype(F32).astype(BF16)
        placed = dot(rates, place)
        for pop in range(pops):
            fresh[pop * group + trial : pop * group + trial + 1, :] = placed[pop : pop + 1, :]
    lags[...] = jnp.zeros_like(lags)
    recent = fresh[...]
    for step in range(steps):
        shifted = jnp.where(lane >= taps - step, recent, back)
        if step:
            shifted = pltpu.roll(shifted, step, 1)
        for part in range(pops * kinds):
            for trial in range(trials):
                row = part * trials + trial
                spot = trial * steps + step
                lags[part, spot : spot + 1, :] = shifted[row : row + 1, :]
    total = dot(sorted_[0], lags[0].astype(BF16), NT)
    for part in range(1, parts):
        total += dot(sorted_[part], lags[part].astype(BF16), NT)
    out[...] = total

    share, wide = plan.share, plan.taps_lanes
    row = lax.broadcasted_iota(jnp.int32, (128, wide), 0)
    column = lax.broadcasted_iota(jnp.int32, (128, wide), 1)
    spread = (row == column // share).astype(F32).astype(BF16)
    row = lax.broadcasted_iota(jnp.int32, (channels, wide), 0)
    column = lax.broadcasted_iota(jnp.int32, (channels, wide), 1)
    same = (row % share == column % share) & (column < (steps - 1) * share)
    row = lax.broadcasted_iota(jnp.int32, (plan.area_count, channels), 0)
    column = lax.broadcasted_iota(jnp.int32, (plan.area_count, channels), 1)
    gather = (row == column // share).astype(F32).astype(BF16)
    reach[...] = jnp.zeros_like(reach)
    for pop in range(pops):
        wider = jnp.where(same, dot(sorted_[pop * kinds + 1, :, 0:128], spread), 0.0)
        packed = dot(gather, wider.astype(BF16))
        for tile in range(wide // 128):
            reach[:, tile * pops + pop, :] = packed[:, tile * 128 : tile * 128 + 128]


def known_lfp(plan, given, population, history, kernel):
    pops, kinds, trials, taps = history.shape
    channels = kernel.shape[0]
    return pl.pallas_call(
        functools.partial(known_kernel, plan),
        out_shape=(
            jax.ShapeDtypeStruct((channels, 128), F32),
            jax.ShapeDtypeStruct((plan.area_count, plan.taps, 128), F32),
        ),
        in_specs=[VMEM] * 4,
        out_specs=(VMEM, VMEM),
        scratch_shapes=[
            pltpu.VMEM((pops * kinds * trials, taps), F32),
            pltpu.VMEM((pops * kinds * trials, taps), F32),
            pltpu.VMEM((pops * kinds, 128, taps), F32),
            pltpu.VMEM((pops * kinds, channels, taps), BF16),
        ],
        compiler_params=params(16),
        name="known_lfp",
    )(given, population, history, kernel)


def pack_signal(plan, values):
    high, low = both(values)
    if not plan.compact:
        return jnp.concatenate([high, low], axis=0)
    half = plan.signal // 2
    out = high[:half]
    for index, piece in enumerate((high[half:], low[:half], low[half:]), 1):
        out = out + pltpu.roll(piece, index * plan.tile, 1)
    return out


def unpack_signal(plan, rows):
    if not plan.compact:
        half = plan.packed // 2
        return rows[:half] + rows[half:]
    lane = lax.broadcasted_iota(jnp.int32, rows.shape, 1)
    pieces = [rows] + [pltpu.roll(rows, 128 - index * plan.tile, 1) for index in (1, 2, 3)]
    value = jnp.concatenate([pieces[0] + pieces[2], pieces[1] + pieces[3]], axis=0)
    lane = lax.broadcasted_iota(jnp.int32, value.shape, 1)
    return jnp.where(lane < plan.tile, value, 0.0)


def compress_kernel(
    plan, mine, got, near, far, cycle, start, known, taps, keep, send, carried, signal, room
):
    trials, steps, delays, blocks = plan.trials, plan.steps, plan.delays, plan.blocks
    me = lax.axis_index("area")
    signal[...] = jnp.zeros_like(signal)
    room[...] = jnp.zeros_like(room)
    owner = lax.broadcasted_iota(jnp.int32, (plan.signal_lanes, 128), 0).astype(F32)

    def pair(index, _):
        sums = jnp.zeros((2 * plan.signal, plan.signal_lanes), F32)
        for bit in range(2):
            lane = 2 * index + bit
            own = (lane == 0).astype(F32)
            place = lax.bitwise_xor(plan.mask(lane), me)
            first = (lax.shift_right_logical(place, 1) * plan.pops).astype(F32)
            tops, members = [], []
            for block in range(blocks):
                arriving = mine[lane * blocks + block] + got[lane * blocks + block]
                early = arriving[0 : trials * delays] + own * cycle[block]
                arriving = jnp.concatenate([early, arriving[trials * delays :]], axis=0)
                spot = pl.multiple_of((index * blocks + block) * 8, 8)
                facts = (far if bit else near)[pl.ds(spot, 8)]
                last = facts[0:trials]
                leak = facts[trials : trials + 1]
                population = facts[trials + 1 : trials + 2]
                membrane = own * start[block]
                for step in range(steps):
                    current = arriving[step * trials : (step + 1) * trials]
                    membrane = jnp.where(last < step, leak * membrane + current, 0.0)
                spot = block * plan.each
                room[bit, spot : spot + trials] = membrane
                room[bit, spot + trials : spot + plan.each] = arriving[trials * steps :]
                tops.append(arriving[0 : plan.signal])
                members.append((owner == population + first).astype(F32).astype(BF16))
            high, low = both(jnp.concatenate(tops, axis=1))
            stacked = jnp.concatenate([high, low], axis=0).astype(BF16)
            sums += dot(stacked, jnp.concatenate(members, axis=1), NT)
            channels, reach = [], []
            for core in range(2):
                there = lax.bitwise_xor(place, core)
                rows = known[there]
                packed = rows[0:8]
                for group in range(1, plan.groups):
                    packed += pltpu.roll(rows[group * 8 : group * 8 + 8], group * plan.width, 1)
                channels.append(packed)
                reach.append(taps[there])
            reach = jnp.concatenate(reach, axis=0).astype(BF16)
            spot = pl.multiple_of(lane * 2 * plan.taps, 16)
            carried[pl.ds(spot, 2 * plan.taps)] = reach
            if bit:
                base = pl.multiple_of(index * plan.slot(0), 16)
                send[pl.ds(base, plan.main_up)] = room[bit].astype(BF16)
                spot = pl.multiple_of(base + plan.main_up, 16)
                send[pl.ds(spot, 16)] = jnp.concatenate(channels, axis=0).astype(BF16)
                spot = pl.multiple_of(base + plan.held, 16)
                send[pl.ds(spot, 2 * plan.taps)] = reach
            else:
                base = pl.multiple_of(index * plan.held, 8)
                keep[pl.ds(base, plan.main_up)] = room[bit]
                keep[pl.ds(base + plan.main_up, 8)] = channels[0]
                keep[pl.ds(base + plan.main_up + 8, 8)] = channels[1]
        signal[...] += sums[: plan.signal] + sums[plan.signal :]
        return 0

    pairs = plan.lanes // 2
    lax.fori_loop(0, pairs, pair, 0, unroll=min(pairs, 4))
    pieces = []
    for tile in range(plan.tiles):
        values = signal[:, tile * 128 : tile * 128 + plan.tile]
        if plan.tile < 128:
            blank = jnp.zeros((plan.signal, 128 - plan.tile), F32)
            values = jnp.concatenate([values, blank], axis=1)
        pieces.append(values)
    values = jnp.concatenate(pieces, axis=0) if plan.tiles > 1 else pieces[0]
    keep[pairs * plan.held :] = values
    put_signal(plan, send, pairs * plan.slot(0), values)


def put_signal(plan, out, base, values):
    rows = pack_signal(plan, values)
    if plan.packed_up > plan.packed:
        blank = jnp.zeros((plan.packed_up - plan.packed, 128), F32)
        rows = jnp.concatenate([rows, blank], axis=0)
    out[base:] = rows.astype(BF16)


def compress(plan, mine, got, near, far, cycle, start, known, taps):
    return pl.pallas_call(
        functools.partial(compress_kernel, plan),
        out_shape=(plan.keep(plan.lanes // 2), plan.send(plan.lanes // 2, 0), plan.carried()),
        in_specs=[VMEM] * 8,
        out_specs=(VMEM,) * 3,
        scratch_shapes=[
            pltpu.VMEM((plan.signal, plan.signal_lanes), F32),
            pltpu.VMEM((2, plan.main_up, 128), F32),
        ],
        compiler_params=params(32),
        name="compress",
    )(mine, got, near, far, cycle, start, known, taps)


def fold_kernel(plan, slots, stage, direct, held, got, carried, keep, *refs):
    taps = 2 * plan.taps
    if direct:
        sends, (now, room) = refs[:-2], refs[-2:]
    else:
        sends, (now,) = refs[:1], refs[1:]
    def spot_of(lane, stage):
        rest = lane & ((1 << stage) - 1)
        return (lane >> (stage + 1)) * plan.slot(stage) + plan.held + rest * taps

    for lane in range(plan.lanes):
        rows = slice(lane * taps, (lane + 1) * taps)
        if lane >> stage & 1:
            spot = spot_of(lane, stage)
            now[rows] = got[spot : spot + taps]
        else:
            now[rows] = carried[rows]
    size = plan.slot(stage)
    tail = got[slots * size : slots * size + plan.packed_up].astype(F32)[: plan.packed]
    tail = unpack_signal(plan, tail)
    tail = tail + held[slots * plan.held :]
    left = 1 if direct else slots // 2
    for slot in range(slots):
        rows = got[slot * size : slot * size + plan.held].astype(F32)
        rows = rows + held[slot * plan.held : (slot + 1) * plan.held]
        if direct and slot:
            out = sends[LATE.index(slot)]
            room[0 : plan.main] = rows[: plan.main]
            room[plan.main : plan.main + plan.packed] = pack_signal(plan, tail)
            out[0 : plan.last] = room[...].astype(BF16)
            out[plan.last : plan.last + 16] = rows[plan.main_up :].astype(BF16)
            span = plan.lanes // 4 * taps
            out[plan.last + 16 :] = now[slot * span : (slot + 1) * span]
        elif slot % 2:
            base = slot // 2 * plan.slot(stage + 1)
            sends[0][base : base + plan.held] = rows.astype(BF16)
        else:
            keep[slot // 2 * plan.held : (slot // 2 + 1) * plan.held] = rows
    keep[left * plan.held :] = tail
    if not direct:
        for lane in range(plan.lanes):
            if lane >> (stage + 1) & 1:
                spot = spot_of(lane, stage + 1)
                sends[0][spot : spot + taps] = now[lane * taps : (lane + 1) * taps]
        put_signal(plan, sends[0], left * plan.slot(stage + 1), tail)


def fold(plan, slots, stage, direct, held, got, carried):
    left = 1 if direct else slots // 2
    scratch = []
    sends = (plan.send(left, stage + 1),)
    if direct:
        sends = (plan.direct(),) * (slots - 1)
        scratch = [pltpu.VMEM((plan.last, 128), F32)]
    return pl.pallas_call(
        functools.partial(fold_kernel, plan, slots, stage, direct),
        out_shape=(plan.keep(left),) + sends + (plan.carried(),),
        in_specs=[VMEM] * 3,
        out_specs=(VMEM,) * (2 + len(sends)),
        scratch_shapes=scratch,
        compiler_params=params(32),
        name="fold",
    )(held, got, carried)


def finish_kernel(plan, held, carried, *refs):
    gots, (membrane, cycle, own, other, mixed, reach, late, parts) = refs[:3], refs[3:]
    trials, steps, delays = plan.trials, plan.steps, plan.delays
    taps = 2 * plan.taps
    rows = held[0 : plan.held]
    main, channels = rows[: plan.main_up], rows[plan.main_up :]
    tail = held[plan.held :]
    parts[0 : plan.main] = main[: plan.main]
    for got in gots:
        arrived = got[0 : plan.last].astype(F32)
        parts[0 : plan.main] += arrived[: plan.main]
        channels = channels + got[plan.last : plan.last + 16].astype(F32)
        tail = tail + unpack_signal(plan, arrived[plan.main : plan.main + plan.packed])
    for block in range(plan.blocks):
        lanes = slice(block * 128, block * 128 + 128)
        base = block * plan.each
        membrane[:, lanes] = parts[base : base + trials]
        for delay in range(delays):
            spot = base + trials * (1 + delay)
            cycle[:, delay, lanes] = parts[spot : spot + trials]

    me = lax.shift_right_logical(lax.axis_index("area"), 1)
    span = plan.lanes // 4
    pops, wide = plan.pops, plan.taps_lanes // 128
    for lane in range(plan.lanes):
        far, near = divmod(lane, span)
        if far:
            spot = plan.last + 16 + near * taps
            slot = gots[LATE.index(far)][spot : spot + taps]
        else:
            slot = carried[lane * taps : (lane + 1) * taps]
        slot = slot.astype(F32)
        spot = lax.bitwise_xor(me, lane)
        for core in range(2):
            for tile in range(wide):
                top = core * plan.taps + tile * pops
                mixed[core, spot, 0:pops, tile * 128 : tile * 128 + 128] = slot[top : top + pops]
    for core in range(2):
        for lane in range(plan.lanes):
            reach[core, lane * pops : (lane + 1) * pops] = mixed[core, lane, 0:pops]
    new = lax.broadcasted_iota(jnp.int32, (plan.width, plan.signal), 0)
    old = lax.broadcasted_iota(jnp.int32, (plan.width, plan.signal), 1)
    order = (old == (new % steps) * trials + new // steps).astype(F32).astype(BF16)
    signal = (tail / plan.pop_size).astype(BF16)
    signal = [
        dot(order, signal[tile * plan.signal : (tile + 1) * plan.signal]).astype(BF16)
        for tile in range(plan.tiles)
    ]
    step_of = lax.broadcasted_iota(jnp.int32, (plan.width, 128), 0) % steps
    late[...] = jnp.zeros_like(late)
    sums = []
    for core in range(2):
        products = None
        for tile in range(plan.tiles):
            right = reach[core, tile * 128 : tile * 128 + plan.tile].astype(BF16)
            one = dot(signal[tile][:, : plan.tile], right)
            products = one if products is None else products + one
        value = jnp.zeros((plan.width, 128), F32)
        width = products.shape[1]
        for lag in range(1, steps):
            moved = products
            if lag > 1:
                moved = pltpu.roll(products, width - (lag - 1) * plan.share, 1)
            moved = pltpu.roll(moved[:, 0:128], lag, 0)
            value = value + jnp.where(step_of >= lag, moved, 0.0)
        sums.append(value)
    lane = lax.broadcasted_iota(jnp.int32, (plan.width, 128), 1)
    late[0 : plan.width] = jnp.where(lane < 64, sums[0], pltpu.roll(sums[1], 64, 1))
    fresh = jnp.transpose(late[...])
    lane = lax.broadcasted_iota(jnp.int32, (8, 128), 1)
    row = lax.broadcasted_iota(jnp.int32, (8, 128), 0)
    for core, out in enumerate((own, other)):
        value = channels[core * 8 : core * 8 + 8]
        for group in range(plan.groups):
            piece = fresh[core * 64 + group * 8 : core * 64 + group * 8 + 8]
            piece = jnp.where(lane < plan.width, piece, 0.0)
            if group:
                piece = pltpu.roll(piece, group * plan.width, 1)
            value = value + piece
        out[...] = value


def finish(plan, neurons, held, carried, gots):
    trials, delays = plan.trials, plan.delays
    part = jax.ShapeDtypeStruct((8, 128), F32)
    return pl.pallas_call(
        functools.partial(finish_kernel, plan),
        out_shape=(
            jax.ShapeDtypeStruct((trials, neurons), F32),
            jax.ShapeDtypeStruct((trials, delays, neurons), F32),
            part,
            part,
        ),
        in_specs=[VMEM] * (2 + len(gots)),
        out_specs=(VMEM,) * 4,
        scratch_shapes=[
            pltpu.VMEM((2, plan.lanes, 8, plan.taps_lanes), F32),
            pltpu.VMEM((2, plan.signal_lanes, plan.taps_lanes), F32),
            pltpu.VMEM((128, 128), F32),
            pltpu.VMEM((plan.main_up, 128), F32),
        ],
        compiler_params=params(16),
        name="finish",
    )(held, carried, *gots)


def swap(values, bit, area_count):
    return lax.ppermute(values, "area", [(i, i ^ bit) for i in range(area_count)])


def body(
    spikes,
    weights,
    destination,
    target_block,
    delay_slot,
    population,
    leak_rate,
    membrane_start,
    cycle_start,
    history,
    lfp_kernel,
):
    area_count = lax.axis_size("area")
    neurons = weights.shape[1]
    blocks = neurons // 128
    trials, steps = spikes.shape[:2]
    delays = cycle_start.shape[1]
    channels = lfp_kernel.shape[0]
    pops = history.shape[0]
    plan = Plan(area_count, trials, steps, delays, neurons, pops, channels)
    share = plan.share
    spikes = jnp.transpose(spikes, (1, 0, 2))
    quarter = plan.lanes // 4

    facts, given = facts_of(
        plan, spikes, leak_rate, population, destination[:, 0], target_block, delay_slot
    )
    size = facts.shape[0]
    came = {index: swap(facts, plan.mask(index * quarter), area_count) for index in (1, 2, 3)}
    facts = [facts] + [came[index] for index in (1, 2, 3)]
    mine, goes, token = payload_sums(plan, given, weights)
    got = swap(goes, 1, area_count)
    blank = jnp.zeros((max(0, PAD - 4 * size - token.shape[0]), 128), F32)
    near = jnp.concatenate(facts + [token, blank])
    count, lane = 4 * size, quarter // 2
    while True:
        more = swap(near, plan.mask(lane), area_count)
        if lane == 1:
            break
        near = jnp.stack(
            [near[:count].reshape(-1, size, 128), more[:count].reshape(-1, size, 128)], axis=1
        ).reshape(-1, 128)
        count, lane = 2 * count, lane // 2

    known, first = known_lfp(plan, given, population, history, lfp_kernel)
    known = known.reshape(area_count, share, 128)
    known = jnp.pad(known, ((0, 0), (0, plan.groups * 8 - share), (0, 0)))

    cycle = jnp.transpose(cycle_start, (1, 0, 2)).reshape(delays * trials, blocks, 128)
    cycle = jnp.transpose(cycle, (1, 0, 2))
    start = jnp.transpose(membrane_start.reshape(trials, blocks, 128), (1, 0, 2))
    keep, send, carried = compress(plan, mine, got, near, more, cycle, start, known, first)

    slots, stage = plan.lanes // 2, 0
    got = swap(send, plan.mask(1), area_count)
    while slots > 4:
        keep, send, carried = fold(plan, slots, stage, False, keep, got, carried)
        slots, stage = slots // 2, stage + 1
        got = swap(send, plan.mask(1 << stage), area_count)
    keep, *sends, carried = fold(plan, slots, stage, True, keep, got, carried)
    gots = [
        swap(send, plan.mask(index * quarter), area_count) for send, index in zip(sends, LATE)
    ]
    membrane, cycle_out, own, other = finish(plan, neurons, keep, carried, gots)
    lfp = own + swap(other, 1, area_count)
    width = plan.width
    lfp = [lfp[:, group * width : (group + 1) * width] for group in range(plan.groups)]
    lfp = jnp.concatenate(lfp, axis=0)[:share]
    return membrane, cycle_out, lfp


def solution(mesh):
    return jax.shard_map(
        body,
        mesh=mesh,
        in_specs=(
            P("runs", None, "area"),
            P("area", None, None),
            P("area", None),
            P("area"),
            P("area"),
            P("area"),
            P("area"),
            P("runs", "area"),
            P("runs", None, "area"),
            P("area", None, "runs", None),
            P(None, "area", None, None),
        ),
        out_specs=(P("runs", "area"), P("runs", None, "area"), P("area", "runs")),
        check_vma=False,
    )
```

```python
import functools

import jax
import jax.numpy as jnp
from jax import lax
from jax.experimental import pallas as pl
from jax.experimental.pallas import tpu as pltpu
from jax.sharding import PartitionSpec as P

BF16, F32 = jnp.bfloat16, jnp.float32
PAD = 112
LATE = (2, 3, 1)
VMEM = pl.BlockSpec(memory_space=pltpu.VMEM)
HBM = pl.BlockSpec(memory_space=pltpu.HBM)
NT = (((1,), (1,)), ((), ()))


def up(value, unit):
    return -(-value // unit) * unit


def dot(left, right, dims=None):
    if dims is None:
        return jnp.dot(left, right, preferred_element_type=F32)
    return lax.dot_general(left, right, dims, preferred_element_type=F32)


def both(values):
    high = values.astype(BF16).astype(F32)
    return high, (values - high).astype(BF16).astype(F32)


def params(megabytes):
    return pltpu.CompilerParams(vmem_limit_bytes=megabytes * 2**20)


class Plan:
    def __init__(self, area_count, trials, steps, delays, neurons, pops, channels):
        self.area_count, self.trials, self.steps, self.delays = area_count, trials, steps, delays
        self.lanes = area_count // 2
        self.top = self.lanes.bit_length() - 2
        self.blocks, self.pops = neurons // 128, pops
        self.pop_size = neurons / pops
        self.arriving = trials * (steps + delays)
        self.each = trials * (1 + delays)
        self.main = self.blocks * self.each
        self.main_up = up(self.main, 16)
        self.share = channels // area_count
        self.groups = up(self.share, 8) // 8
        self.width = trials * steps
        self.taps_lanes = up((steps - 1) * self.share, 128)
        self.taps = up(self.taps_lanes // 128 * pops, 8)
        self.signal = up(trials * (steps - 1), 8)
        self.signal_lanes = pops * self.lanes
        self.tile = min(self.signal_lanes, 128)
        self.tiles = up(self.signal_lanes, 128) // 128
        self.compact = 4 * self.tile <= 128 and self.signal % 2 == 0
        self.packed = self.signal // 2 if self.compact else 2 * self.tiles * self.signal
        self.packed_up = up(self.packed, 16)
        self.held = self.main_up + 16
        self.last = up(self.main + self.packed, 16)

    def mask(self, lane):
        return (2 * lane) ^ (lane >> self.top)

    def keep(self, slots):
        rows = slots * self.held + self.tiles * self.signal
        return jax.ShapeDtypeStruct((rows, 128), F32)

    def slot(self, stage):
        return self.held + (2 * self.taps << stage)

    def send(self, slots, stage):
        return jax.ShapeDtypeStruct((slots * self.slot(stage) + self.packed_up, 128), BF16)

    def direct(self):
        rows = self.last + 16 + self.lanes // 4 * 2 * self.taps
        return jax.ShapeDtypeStruct((rows, 128), BF16)

    def carried(self):
        return jax.ShapeDtypeStruct((self.lanes * 2 * self.taps, 128), BF16)


def facts_kernel(plan, spikes, leak, population, destination, target_block, delay_slot, out, given):
    trials, steps = plan.trials, plan.steps
    last = jnp.full(spikes.shape[1:], -1, jnp.int32)
    for step in range(steps):
        last = jnp.where(spikes[step] > 0, step, last)
        given[step * trials : (step + 1) * trials] = spikes[step]
    blank = jnp.zeros((6 - trials, last.shape[1]), F32)
    rows = [last.astype(F32), leak[...].reshape(1, -1), population[...].astype(F32).reshape(1, -1)]
    rows = jnp.concatenate(rows + [blank], axis=0)
    for block in range(plan.blocks):
        out[block * 8 : block * 8 + 8] = rows[:, block * 128 : block * 128 + 128]
    given[plan.width :] = jnp.zeros((given.shape[0] - plan.width, given.shape[1]), jnp.int32)
    for row, values in enumerate((destination, target_block, delay_slot)):
        row += up(plan.width, 8)
        given[row : row + 1, 0 : values.shape[0]] = values[...].reshape(1, -1)


def facts_of(plan, spikes, leak, population, destination, target_block, delay_slot):
    rows = up(plan.width, 8) + 8
    return pl.pallas_call(
        functools.partial(facts_kernel, plan),
        out_shape=(
            pltpu.VMEM((plan.blocks * 8, 128), F32),
            pltpu.VMEM((rows, spikes.shape[2]), jnp.int32),
        ),
        in_specs=[VMEM] * 6,
        out_specs=(VMEM, VMEM),
        name="facts",
    )(spikes, leak, population, destination, target_block, delay_slot)


def payload_kernel(
    plan, given, weights, keep, send, token, codes, held, plain, lagged, total, sem, part_sems
):
    steps, trials = plan.steps, plan.trials
    unit_count = weights.shape[0]
    delays = lagged.shape[0]
    blocks = plan.blocks
    half, rows = keep.shape[:2]
    chunk = held.shape[0] // part_sems.shape[0]
    chunks = unit_count // chunk
    listed = pltpu.make_async_copy(given.at[pl.ds(up(plan.width, 8), 8)], codes, sem)
    listed.start()

    def part(index):
        where = pl.ds(index * chunk, chunk)
        return pltpu.make_async_copy(weights.at[where], held.at[where], part_sems.at[index])

    for index in range(chunks):
        part(index).start()
    total[...] = jnp.zeros_like(total)
    plain[...] = jnp.zeros_like(plain)
    lagged[...] = jnp.zeros_like(lagged)
    token[...] = jnp.zeros_like(token)
    front = trials * delays
    for step in range(steps):
        start = front + step * trials
        plain[start : start + trials, :] = given[step * trials : (step + 1) * trials].astype(F32)
    for delay in range(delays):
        start = front - trials * (delay + 1)
        lagged[delay, 0:rows, :] = plain[start : start + rows, :].astype(BF16)
    listed.wait()
    me = lax.axis_index("area")

    def some(index, _):
        part(index).wait()
        units = [index * chunk + inner for inner in range(chunk)]
        values = [
            dot(lagged[codes[2, unit]], held[unit])[0:rows].astype(BF16).astype(F32)
            for unit in units
        ]
        for unit, value in zip(units, values):
            device = lax.bitwise_xor(codes[0, unit], me)
            lane = lax.shift_right_logical(device, 1)
            bit = lax.bitwise_and(lax.bitwise_xor(device, lane >> plan.top), 1)
            place = bit * half + lane * blocks + codes[1, unit]
            total[place] += value
        return 0

    lax.fori_loop(0, chunks, some, 0)
    keep[...] = total[0:half]
    send[...] = total[half:]


def payload_sums(plan, given, weights):
    unit_count, neurons = weights.shape[:2]
    rows, delays = plan.arriving, plan.delays
    chunk = next(size for size in (16, 12, 8, 6, 4, 3, 2, 1) if unit_count % size == 0)
    half = jax.ShapeDtypeStruct((plan.lanes * plan.blocks, rows, 128), F32)
    return pl.pallas_call(
        functools.partial(payload_kernel, plan),
        out_shape=(half, half, jax.ShapeDtypeStruct((8, 128), F32)),
        in_specs=[VMEM, HBM],
        out_specs=(VMEM,) * 3,
        scratch_shapes=[
            pltpu.SMEM((8, neurons), jnp.int32),
            pltpu.VMEM(weights.shape, BF16),
            pltpu.VMEM((plan.trials * delays + rows, neurons), F32),
            pltpu.VMEM((delays, up(rows, 16), neurons), BF16),
            pltpu.VMEM((2 * plan.lanes * plan.blocks, rows, 128), F32),
            pltpu.SemaphoreType.DMA,
            pltpu.SemaphoreType.DMA((unit_count // chunk,)),
        ],
        compiler_params=params(24),
        name="payload",
    )(given, pltpu.with_memory_space_constraint(weights, pltpu.HBM))


def known_kernel(plan, given, population, history, kernel, out, reach, series, fresh, lags, sorted_):
    steps, trials, neurons = plan.steps, plan.trials, given.shape[1]
    pops, kinds, _, taps = history.shape
    channels, parts = kernel.shape[0], pops * kinds
    some = 256 // parts
    row = lax.broadcasted_iota(jnp.int32, (256, 256), 0)
    column = lax.broadcasted_iota(jnp.int32, (256, 256), 1)
    order = (column == row % some * parts + row // some).astype(F32).astype(BF16)
    for index in range(channels // some):
        rows = kernel[index * some : (index + 1) * some].reshape(256, taps)
        rows = dot(order, rows).astype(BF16)
        for part in range(parts):
            sorted_[part, index * some : (index + 1) * some] = rows[part * some : (part + 1) * some]
    group = kinds * trials
    lane = lax.broadcasted_iota(jnp.int32, (pops * group, taps), 1)
    for pop in range(pops):
        for kind in range(kinds):
            start = pop * group + kind * trials
            series[start : start + trials, :] = history[pop, kind]
    flip = lax.broadcasted_iota(jnp.int32, (taps, taps), 0) + lax.broadcasted_iota(
        jnp.int32, (taps, taps), 1
    )
    flip = (flip == taps - 1).astype(F32).astype(BF16)
    back = dot(series[...].astype(BF16), flip)

    which = lax.broadcasted_iota(jnp.int32, (8, neurons), 0)
    member = (which == population[...].reshape(1, -1)).astype(F32).astype(BF16)
    rows = given[0 : steps * trials].astype(F32).astype(BF16)
    rates = (dot(member, rows, NT) / (neurons / pops)).astype(BF16)
    fresh[...] = jnp.zeros_like(fresh)
    row = lax.broadcasted_iota(jnp.int32, (steps * trials, taps), 0)
    column = lax.broadcasted_iota(jnp.int32, (steps * trials, taps), 1)
    for trial in range(trials):
        place = (row == (taps - 1 - column) * trials + trial).astype(F32).astype(BF16)
        placed = dot(rates, place)
        for pop in range(pops):
            fresh[pop * group + trial : pop * group + trial + 1, :] = placed[pop : pop + 1, :]
    lags[...] = jnp.zeros_like(lags)
    recent = fresh[...]
    for step in range(steps):
        shifted = jnp.where(lane >= taps - step, recent, back)
        if step:
            shifted = pltpu.roll(shifted, step, 1)
        for part in range(pops * kinds):
            for trial in range(trials):
                row = part * trials + trial
                spot = trial * steps + step
                lags[part, spot : spot + 1, :] = shifted[row : row + 1, :]
    total = dot(sorted_[0], lags[0].astype(BF16), NT)
    for part in range(1, parts):
        total += dot(sorted_[part], lags[part].astype(BF16), NT)
    out[...] = total

    share, wide = plan.share, plan.taps_lanes
    row = lax.broadcasted_iota(jnp.int32, (128, wide), 0)
    column = lax.broadcasted_iota(jnp.int32, (128, wide), 1)
    spread = (row == column // share).astype(F32).astype(BF16)
    row = lax.broadcasted_iota(jnp.int32, (channels, wide), 0)
    column = lax.broadcasted_iota(jnp.int32, (channels, wide), 1)
    same = (row % share == column % share) & (column < (steps - 1) * share)
    row = lax.broadcasted_iota(jnp.int32, (plan.area_count, channels), 0)
    column = lax.broadcasted_iota(jnp.int32, (plan.area_count, channels), 1)
    gather = (row == column // share).astype(F32).astype(BF16)
    reach[...] = jnp.zeros_like(reach)
    for pop in range(pops):
        wider = jnp.where(same, dot(sorted_[pop * kinds + 1, :, 0:128], spread), 0.0)
        packed = dot(gather, wider.astype(BF16))
        for tile in range(wide // 128):
            reach[:, tile * pops + pop, :] = packed[:, tile * 128 : tile * 128 + 128]


def known_lfp(plan, given, population, history, kernel):
    pops, kinds, trials, taps = history.shape
    channels = kernel.shape[0]
    return pl.pallas_call(
        functools.partial(known_kernel, plan),
        out_shape=(
            jax.ShapeDtypeStruct((channels, 128), F32),
            jax.ShapeDtypeStruct((plan.area_count, plan.taps, 128), F32),
        ),
        in_specs=[VMEM] * 4,
        out_specs=(VMEM, VMEM),
        scratch_shapes=[
            pltpu.VMEM((pops * kinds * trials, taps), F32),
            pltpu.VMEM((pops * kinds * trials, taps), F32),
            pltpu.VMEM((pops * kinds, 128, taps), F32),
            pltpu.VMEM((pops * kinds, channels, taps), BF16),
        ],
        compiler_params=params(16),
        name="known_lfp",
    )(given, population, history, kernel)


def pack_signal(plan, values):
    high, low = both(values)
    if not plan.compact:
        return jnp.concatenate([high, low], axis=0)
    half = plan.signal // 2
    out = high[:half]
    for index, piece in enumerate((high[half:], low[:half], low[half:]), 1):
        out = out + pltpu.roll(piece, index * plan.tile, 1)
    return out


def unpack_signal(plan, rows):
    if not plan.compact:
        half = plan.packed // 2
        return rows[:half] + rows[half:]
    lane = lax.broadcasted_iota(jnp.int32, rows.shape, 1)
    pieces = [rows] + [pltpu.roll(rows, 128 - index * plan.tile, 1) for index in (1, 2, 3)]
    value = jnp.concatenate([pieces[0] + pieces[2], pieces[1] + pieces[3]], axis=0)
    lane = lax.broadcasted_iota(jnp.int32, value.shape, 1)
    return jnp.where(lane < plan.tile, value, 0.0)


def compress_kernel(
    plan, mine, got, near, far, cycle, start, known, taps, keep, send, carried, signal, room
):
    trials, steps, delays, blocks = plan.trials, plan.steps, plan.delays, plan.blocks
    me = lax.axis_index("area")
    signal[...] = jnp.zeros_like(signal)
    room[...] = jnp.zeros_like(room)
    owner = lax.broadcasted_iota(jnp.int32, (plan.signal_lanes, 128), 0).astype(F32)

    def pair(index, _):
        sums = jnp.zeros((2 * plan.signal, plan.signal_lanes), F32)
        for bit in range(2):
            lane = 2 * index + bit
            own = (lane == 0).astype(F32)
            place = lax.bitwise_xor(plan.mask(lane), me)
            first = (lax.shift_right_logical(place, 1) * plan.pops).astype(F32)
            tops, members = [], []
            for block in range(blocks):
                arriving = mine[lane * blocks + block] + got[lane * blocks + block]
                early = arriving[0 : trials * delays] + own * cycle[block]
                arriving = jnp.concatenate([early, arriving[trials * delays :]], axis=0)
                spot = pl.multiple_of((index * blocks + block) * 8, 8)
                facts = (far if bit else near)[pl.ds(spot, 8)]
                last = facts[0:trials]
                leak = facts[trials : trials + 1]
                population = facts[trials + 1 : trials + 2]
                membrane = own * start[block]
                for step in range(steps):
                    current = arriving[step * trials : (step + 1) * trials]
                    membrane = jnp.where(last < step, leak * membrane + current, 0.0)
                spot = block * plan.each
                room[bit, spot : spot + trials] = membrane
                room[bit, spot + trials : spot + plan.each] = arriving[trials * steps :]
                tops.append(arriving[0 : plan.signal])
                members.append((owner == population + first).astype(F32).astype(BF16))
            high, low = both(jnp.concatenate(tops, axis=1))
            stacked = jnp.concatenate([high, low], axis=0).astype(BF16)
            sums += dot(stacked, jnp.concatenate(members, axis=1), NT)
            channels, reach = [], []
            for core in range(2):
                there = lax.bitwise_xor(place, core)
                rows = known[there]
                packed = rows[0:8]
                for group in range(1, plan.groups):
                    packed += pltpu.roll(rows[group * 8 : group * 8 + 8], group * plan.width, 1)
                channels.append(packed)
                reach.append(taps[there])
            reach = jnp.concatenate(reach, axis=0).astype(BF16)
            spot = pl.multiple_of(lane * 2 * plan.taps, 16)
            carried[pl.ds(spot, 2 * plan.taps)] = reach
            if bit:
                base = pl.multiple_of(index * plan.slot(0), 16)
                send[pl.ds(base, plan.main_up)] = room[bit].astype(BF16)
                spot = pl.multiple_of(base + plan.main_up, 16)
                send[pl.ds(spot, 16)] = jnp.concatenate(channels, axis=0).astype(BF16)
                spot = pl.multiple_of(base + plan.held, 16)
                send[pl.ds(spot, 2 * plan.taps)] = reach
            else:
                base = pl.multiple_of(index * plan.held, 8)
                keep[pl.ds(base, plan.main_up)] = room[bit]
                keep[pl.ds(base + plan.main_up, 8)] = channels[0]
                keep[pl.ds(base + plan.main_up + 8, 8)] = channels[1]
        signal[...] += sums[: plan.signal] + sums[plan.signal :]
        return 0

    pairs = plan.lanes // 2
    lax.fori_loop(0, pairs, pair, 0, unroll=min(pairs, 4))
    pieces = []
    for tile in range(plan.tiles):
        values = signal[:, tile * 128 : tile * 128 + plan.tile]
        if plan.tile < 128:
            blank = jnp.zeros((plan.signal, 128 - plan.tile), F32)
            values = jnp.concatenate([values, blank], axis=1)
        pieces.append(values)
    values = jnp.concatenate(pieces, axis=0) if plan.tiles > 1 else pieces[0]
    keep[pairs * plan.held :] = values
    put_signal(plan, send, pairs * plan.slot(0), values)


def put_signal(plan, out, base, values):
    rows = pack_signal(plan, values)
    if plan.packed_up > plan.packed:
        blank = jnp.zeros((plan.packed_up - plan.packed, 128), F32)
        rows = jnp.concatenate([rows, blank], axis=0)
    out[base:] = rows.astype(BF16)


def compress(plan, mine, got, near, far, cycle, start, known, taps):
    return pl.pallas_call(
        functools.partial(compress_kernel, plan),
        out_shape=(plan.keep(plan.lanes // 2), plan.send(plan.lanes // 2, 0), plan.carried()),
        in_specs=[VMEM] * 8,
        out_specs=(VMEM,) * 3,
        scratch_shapes=[
            pltpu.VMEM((plan.signal, plan.signal_lanes), F32),
            pltpu.VMEM((2, plan.main_up, 128), F32),
        ],
        compiler_params=params(32),
        name="compress",
    )(mine, got, near, far, cycle, start, known, taps)


def fold_kernel(plan, slots, stage, direct, held, got, carried, keep, *refs):
    taps = 2 * plan.taps
    if direct:
        sends, (now, room) = refs[:-2], refs[-2:]
    else:
        sends, (now,) = refs[:1], refs[1:]
    def spot_of(lane, stage):
        rest = lane & ((1 << stage) - 1)
        return (lane >> (stage + 1)) * plan.slot(stage) + plan.held + rest * taps

    for lane in range(plan.lanes):
        rows = slice(lane * taps, (lane + 1) * taps)
        if lane >> stage & 1:
            spot = spot_of(lane, stage)
            now[rows] = got[spot : spot + taps]
        else:
            now[rows] = carried[rows]
    size = plan.slot(stage)
    tail = got[slots * size : slots * size + plan.packed_up].astype(F32)[: plan.packed]
    tail = unpack_signal(plan, tail)
    tail = tail + held[slots * plan.held :]
    left = 1 if direct else slots // 2
    for slot in range(slots):
        rows = got[slot * size : slot * size + plan.held].astype(F32)
        rows = rows + held[slot * plan.held : (slot + 1) * plan.held]
        if direct and slot:
            out = sends[LATE.index(slot)]
            room[0 : plan.main] = rows[: plan.main]
            room[plan.main : plan.main + plan.packed] = pack_signal(plan, tail)
            out[0 : plan.last] = room[...].astype(BF16)
            out[plan.last : plan.last + 16] = rows[plan.main_up :].astype(BF16)
            span = plan.lanes // 4 * taps
            out[plan.last + 16 :] = now[slot * span : (slot + 1) * span]
        elif slot % 2:
            base = slot // 2 * plan.slot(stage + 1)
            sends[0][base : base + plan.held] = rows.astype(BF16)
        else:
            keep[slot // 2 * plan.held : (slot // 2 + 1) * plan.held] = rows
    keep[left * plan.held :] = tail
    if not direct:
        for lane in range(plan.lanes):
            if lane >> (stage + 1) & 1:
                spot = spot_of(lane, stage + 1)
                sends[0][spot : spot + taps] = now[lane * taps : (lane + 1) * taps]
        put_signal(plan, sends[0], left * plan.slot(stage + 1), tail)


def fold(plan, slots, stage, direct, held, got, carried):
    left = 1 if direct else slots // 2
    scratch = []
    sends = (plan.send(left, stage + 1),)
    if direct:
        sends = (plan.direct(),) * (slots - 1)
        scratch = [pltpu.VMEM((plan.last, 128), F32)]
    return pl.pallas_call(
        functools.partial(fold_kernel, plan, slots, stage, direct),
        out_shape=(plan.keep(left),) + sends + (plan.carried(),),
        in_specs=[VMEM] * 3,
        out_specs=(VMEM,) * (2 + len(sends)),
        scratch_shapes=scratch,
        compiler_params=params(32),
        name="fold",
    )(held, got, carried)


def finish_kernel(plan, held, carried, *refs):
    gots, (membrane, cycle, own, other, mixed, reach, late, parts) = refs[:3], refs[3:]
    trials, steps, delays = plan.trials, plan.steps, plan.delays
    taps = 2 * plan.taps
    rows = held[0 : plan.held]
    main, channels = rows[: plan.main_up], rows[plan.main_up :]
    tail = held[plan.held :]
    parts[0 : plan.main] = main[: plan.main]
    for got in gots:
        arrived = got[0 : plan.last].astype(F32)
        parts[0 : plan.main] += arrived[: plan.main]
        channels = channels + got[plan.last : plan.last + 16].astype(F32)
        tail = tail + unpack_signal(plan, arrived[plan.main : plan.main + plan.packed])
    for block in range(plan.blocks):
        lanes = slice(block * 128, block * 128 + 128)
        base = block * plan.each
        membrane[:, lanes] = parts[base : base + trials]
        for delay in range(delays):
            spot = base + trials * (1 + delay)
            cycle[:, delay, lanes] = parts[spot : spot + trials]

    me = lax.shift_right_logical(lax.axis_index("area"), 1)
    span = plan.lanes // 4
    pops, wide = plan.pops, plan.taps_lanes // 128
    for lane in range(plan.lanes):
        far, near = divmod(lane, span)
        if far:
            spot = plan.last + 16 + near * taps
            slot = gots[LATE.index(far)][spot : spot + taps]
        else:
            slot = carried[lane * taps : (lane + 1) * taps]
        slot = slot.astype(F32)
        spot = lax.bitwise_xor(me, lane)
        for core in range(2):
            for tile in range(wide):
                top = core * plan.taps + tile * pops
                mixed[core, spot, 0:pops, tile * 128 : tile * 128 + 128] = slot[top : top + pops]
    for core in range(2):
        for lane in range(plan.lanes):
            reach[core, lane * pops : (lane + 1) * pops] = mixed[core, lane, 0:pops]
    new = lax.broadcasted_iota(jnp.int32, (plan.width, plan.signal), 0)
    old = lax.broadcasted_iota(jnp.int32, (plan.width, plan.signal), 1)
    order = (old == (new % steps) * trials + new // steps).astype(F32).astype(BF16)
    signal = (tail / plan.pop_size).astype(BF16)
    signal = [
        dot(order, signal[tile * plan.signal : (tile + 1) * plan.signal]).astype(BF16)
        for tile in range(plan.tiles)
    ]
    step_of = lax.broadcasted_iota(jnp.int32, (plan.width, 128), 0) % steps
    late[...] = jnp.zeros_like(late)
    sums = []
    for core in range(2):
        products = None
        for tile in range(plan.tiles):
            right = reach[core, tile * 128 : tile * 128 + plan.tile].astype(BF16)
            one = dot(signal[tile][:, : plan.tile], right)
            products = one if products is None else products + one
        value = jnp.zeros((plan.width, 128), F32)
        width = products.shape[1]
        for lag in range(1, steps):
            moved = products
            if lag > 1:
                moved = pltpu.roll(products, width - (lag - 1) * plan.share, 1)
            moved = pltpu.roll(moved[:, 0:128], lag, 0)
            value = value + jnp.where(step_of >= lag, moved, 0.0)
        sums.append(value)
    lane = lax.broadcasted_iota(jnp.int32, (plan.width, 128), 1)
    late[0 : plan.width] = jnp.where(lane < 64, sums[0], pltpu.roll(sums[1], 64, 1))
    fresh = jnp.transpose(late[...])
    lane = lax.broadcasted_iota(jnp.int32, (8, 128), 1)
    row = lax.broadcasted_iota(jnp.int32, (8, 128), 0)
    for core, out in enumerate((own, other)):
        value = channels[core * 8 : core * 8 + 8]
        for group in range(plan.groups):
            piece = fresh[core * 64 + group * 8 : core * 64 + group * 8 + 8]
            piece = jnp.where(lane < plan.width, piece, 0.0)
            if group:
                piece = pltpu.roll(piece, group * plan.width, 1)
            value = value + piece
        out[...] = value


def finish(plan, neurons, held, carried, gots):
    trials, delays = plan.trials, plan.delays
    part = jax.ShapeDtypeStruct((8, 128), F32)
    return pl.pallas_call(
        functools.partial(finish_kernel, plan),
        out_shape=(
            jax.ShapeDtypeStruct((trials, neurons), F32),
            jax.ShapeDtypeStruct((trials, delays, neurons), F32),
            part,
            part,
        ),
        in_specs=[VMEM] * (2 + len(gots)),
        out_specs=(VMEM,) * 4,
        scratch_shapes=[
            pltpu.VMEM((2, plan.lanes, 8, plan.taps_lanes), F32),
            pltpu.VMEM((2, plan.signal_lanes, plan.taps_lanes), F32),
            pltpu.VMEM((128, 128), F32),
            pltpu.VMEM((plan.main_up, 128), F32),
        ],
        compiler_params=params(16),
        name="finish",
    )(held, carried, *gots)


def swap(values, bit, area_count):
    return lax.ppermute(values, "area", [(i, i ^ bit) for i in range(area_count)])


def body(
    spikes,
    weights,
    destination,
    target_block,
    delay_slot,
    population,
    leak_rate,
    membrane_start,
    cycle_start,
    history,
    lfp_kernel,
):
    area_count = lax.axis_size("area")
    neurons = weights.shape[1]
    blocks = neurons // 128
    trials, steps = spikes.shape[:2]
    delays = cycle_start.shape[1]
    channels = lfp_kernel.shape[0]
    pops = history.shape[0]
    plan = Plan(area_count, trials, steps, delays, neurons, pops, channels)
    share = plan.share
    spikes = jnp.transpose(spikes, (1, 0, 2))
    quarter = plan.lanes // 4

    facts, given = facts_of(
        plan, spikes, leak_rate, population, destination[:, 0], target_block, delay_slot
    )
    size = facts.shape[0]
    came = {index: swap(facts, plan.mask(index * quarter), area_count) for index in (1, 2, 3)}
    facts = [facts] + [came[index] for index in (1, 2, 3)]
    mine, goes, token = payload_sums(plan, given, weights)
    got = swap(goes, 1, area_count)
    blank = jnp.zeros((max(0, PAD - 4 * size - token.shape[0]), 128), F32)
    near = jnp.concatenate(facts + [token, blank])
    count, lane = 4 * size, quarter // 2
    while True:
        more = swap(near, plan.mask(lane), area_count)
        if lane == 1:
            break
        near = jnp.stack(
            [near[:count].reshape(-1, size, 128), more[:count].reshape(-1, size, 128)], axis=1
        ).reshape(-1, 128)
        count, lane = 2 * count, lane // 2

    known, first = known_lfp(plan, given, population, history, lfp_kernel)
    known = known.reshape(area_count, share, 128)
    known = jnp.pad(known, ((0, 0), (0, plan.groups * 8 - share), (0, 0)))

    cycle = jnp.transpose(cycle_start, (1, 0, 2)).reshape(delays * trials, blocks, 128)
    cycle = jnp.transpose(cycle, (1, 0, 2))
    start = jnp.transpose(membrane_start.reshape(trials, blocks, 128), (1, 0, 2))
    keep, send, carried = compress(plan, mine, got, near, more, cycle, start, known, first)

    slots, stage = plan.lanes // 2, 0
    got = swap(send, plan.mask(1), area_count)
    while slots > 4:
        keep, send, carried = fold(plan, slots, stage, False, keep, got, carried)
        slots, stage = slots // 2, stage + 1
        got = swap(send, plan.mask(1 << stage), area_count)
    keep, *sends, carried = fold(plan, slots, stage, True, keep, got, carried)
    gots = [
        swap(send, plan.mask(index * quarter), area_count) for send, index in zip(sends, LATE)
    ]
    membrane, cycle_out, own, other = finish(plan, neurons, keep, carried, gots)
    lfp = own + swap(other, 1, area_count)
    width = plan.width
    lfp = [lfp[:, group * width : (group + 1) * width] for group in range(plan.groups)]
    lfp = jnp.concatenate(lfp, axis=0)[:share]
    return membrane, cycle_out, lfp


def solution(mesh):
    return jax.shard_map(
        body,
        mesh=mesh,
        in_specs=(
            P("runs", None, "area"),
            P("area", None, None),
            P("area", None),
            P("area"),
            P("area"),
            P("area"),
            P("area"),
            P("runs", "area"),
            P("runs", None, "area"),
            P("area", None, "runs", None),
            P(None, "area", None, None),
        ),
        out_specs=(P("runs", "area"), P("runs", None, "area"), P("area", "runs")),
        check_vma=False,
    )
```

```python
import functools

import jax
import jax.numpy as jnp
from jax import lax
from jax.experimental import pallas as pl
from jax.experimental.pallas import tpu as pltpu
from jax.sharding import PartitionSpec as P

BF16, F32 = jnp.bfloat16, jnp.float32
PAD = 112
LATE = (2, 3, 1)
RING = (1, 2, 3)
VMEM = pl.BlockSpec(memory_space=pltpu.VMEM)
HBM = pl.BlockSpec(memory_space=pltpu.HBM)
NT = (((1,), (1,)), ((), ()))


def up(value, unit):
    return -(-value // unit) * unit


def dot(left, right, dims=None):
    if dims is None:
        return jnp.dot(left, right, preferred_element_type=F32)
    return lax.dot_general(left, right, dims, preferred_element_type=F32)


def both(values):
    high = values.astype(BF16).astype(F32)
    return high, (values - high).astype(BF16).astype(F32)


def params(megabytes):
    return pltpu.CompilerParams(vmem_limit_bytes=megabytes * 2**20)


class Plan:
    def __init__(self, area_count, trials, steps, delays, neurons, pops, channels):
        self.area_count, self.trials, self.steps, self.delays = area_count, trials, steps, delays
        self.lanes = area_count // 2
        self.top = self.lanes.bit_length() - 2
        self.blocks, self.pops = neurons // 128, pops
        self.pop_size = neurons / pops
        self.arriving = trials * (steps + delays)
        self.each = trials * (1 + delays)
        self.main = self.blocks * self.each
        self.main_up = up(self.main, 16)
        self.share = channels // area_count
        self.groups = up(self.share, 8) // 8
        self.width = trials * steps
        self.taps_lanes = up((steps - 1) * self.share, 128)
        self.taps = up(self.taps_lanes // 128 * pops, 8)
        self.signal = up(trials * (steps - 1), 8)
        self.signal_lanes = pops * self.lanes
        self.tile = min(self.signal_lanes, 128)
        self.tiles = up(self.signal_lanes, 128) // 128
        self.compact = 4 * self.tile <= 128 and self.signal % 2 == 0
        self.packed = self.signal // 2 if self.compact else 2 * self.tiles * self.signal
        self.packed_up = up(self.packed, 16)
        self.held = self.main_up + 16
        self.last = up(self.main + self.packed, 16)

    def mask(self, lane):
        return (2 * lane) ^ ((lane >> self.top) ^ (lane >> (self.top - 1) & 1))

    def quarter(self, device):
        return (device >> 1) // (self.lanes // 4)

    def ring(self, shift):
        pairs = []
        for device in range(self.area_count):
            here = self.quarter(device)
            apart = here ^ (here + shift) % 4
            pairs.append((device, device ^ self.mask(apart * (self.lanes // 4))))
        return pairs

    def ring_place(self, pair, me):
        size = self.lanes // 8
        apart, rest = pair // size, pair % size
        turned = (apart % 2 == 1) & (self.quarter(me) % 2 == 0)
        shift = jnp.where(turned, 4 - apart, apart)
        place = jnp.int32(0)
        for index, value in enumerate(RING, 1):
            place = jnp.where(shift == value, index, place)
        return place * size + rest

    def keep(self, slots):
        rows = slots * self.held + self.tiles * self.signal
        return jax.ShapeDtypeStruct((rows, 128), F32)

    def slot(self, stage):
        return self.held + (2 * self.taps << stage)

    def send(self, slots, stage):
        return jax.ShapeDtypeStruct((slots * self.slot(stage) + self.packed_up, 128), BF16)

    def direct(self):
        rows = self.last + 16 + self.lanes // 4 * 2 * self.taps
        return jax.ShapeDtypeStruct((rows, 128), BF16)

    def carried(self):
        return jax.ShapeDtypeStruct((self.lanes * 2 * self.taps, 128), BF16)


def facts_kernel(plan, spikes, leak, population, destination, target_block, delay_slot, out, given):
    trials, steps = plan.trials, plan.steps
    last = jnp.full(spikes.shape[1:], -1, jnp.int32)
    for step in range(steps):
        last = jnp.where(spikes[step] > 0, step, last)
        given[step * trials : (step + 1) * trials] = spikes[step]
    blank = jnp.zeros((6 - trials, last.shape[1]), F32)
    rows = [last.astype(F32), leak[...].reshape(1, -1), population[...].astype(F32).reshape(1, -1)]
    rows = jnp.concatenate(rows + [blank], axis=0)
    for block in range(plan.blocks):
        out[block * 8 : block * 8 + 8] = rows[:, block * 128 : block * 128 + 128]
    given[plan.width :] = jnp.zeros((given.shape[0] - plan.width, given.shape[1]), jnp.int32)
    for row, values in enumerate((destination, target_block, delay_slot)):
        row += up(plan.width, 8)
        given[row : row + 1, 0 : values.shape[0]] = values[...].reshape(1, -1)


def facts_of(plan, spikes, leak, population, destination, target_block, delay_slot):
    rows = up(plan.width, 8) + 8
    return pl.pallas_call(
        functools.partial(facts_kernel, plan),
        out_shape=(
            pltpu.VMEM((plan.blocks * 8, 128), F32),
            pltpu.VMEM((rows, spikes.shape[2]), jnp.int32),
        ),
        in_specs=[VMEM] * 6,
        out_specs=(VMEM, VMEM),
        name="facts",
    )(spikes, leak, population, destination, target_block, delay_slot)


def payload_kernel(
    plan, given, weights, keep, send, token, codes, held, plain, lagged, total, sem, part_sems
):
    steps, trials = plan.steps, plan.trials
    unit_count = weights.shape[0]
    delays = lagged.shape[0]
    blocks = plan.blocks
    half, rows = keep.shape[:2]
    chunk = held.shape[0] // part_sems.shape[0]
    chunks = unit_count // chunk
    listed = pltpu.make_async_copy(given.at[pl.ds(up(plan.width, 8), 8)], codes, sem)
    listed.start()

    def part(index):
        where = pl.ds(index * chunk, chunk)
        return pltpu.make_async_copy(weights.at[where], held.at[where], part_sems.at[index])

    for index in range(chunks):
        part(index).start()
    total[...] = jnp.zeros_like(total)
    plain[...] = jnp.zeros_like(plain)
    lagged[...] = jnp.zeros_like(lagged)
    token[...] = jnp.zeros_like(token)
    front = trials * delays
    for step in range(steps):
        start = front + step * trials
        plain[start : start + trials, :] = given[step * trials : (step + 1) * trials].astype(F32)
    for delay in range(delays):
        start = front - trials * (delay + 1)
        lagged[delay, 0:rows, :] = plain[start : start + rows, :].astype(BF16)
    listed.wait()
    me = lax.axis_index("area")

    def some(index, _):
        part(index).wait()
        units = [index * chunk + inner for inner in range(chunk)]
        values = [
            dot(lagged[codes[2, unit]], held[unit])[0:rows].astype(BF16).astype(F32)
            for unit in units
        ]
        for unit, value in zip(units, values):
            device = lax.bitwise_xor(codes[0, unit], me)
            lane = lax.shift_right_logical(device, 1)
            bit = lax.bitwise_and(device ^ (lane >> plan.top) ^ (lane >> (plan.top - 1)), 1)
            place = bit * half + lane * blocks + codes[1, unit]
            total[place] += value
        return 0

    lax.fori_loop(0, chunks, some, 0)
    keep[...] = total[0:half]
    send[...] = total[half:]


def payload_sums(plan, given, weights):
    unit_count, neurons = weights.shape[:2]
    rows, delays = plan.arriving, plan.delays
    chunk = next(size for size in (16, 12, 8, 6, 4, 3, 2, 1) if unit_count % size == 0)
    half = jax.ShapeDtypeStruct((plan.lanes * plan.blocks, rows, 128), F32)
    return pl.pallas_call(
        functools.partial(payload_kernel, plan),
        out_shape=(half, half, jax.ShapeDtypeStruct((8, 128), F32)),
        in_specs=[VMEM, HBM],
        out_specs=(VMEM,) * 3,
        scratch_shapes=[
            pltpu.SMEM((8, neurons), jnp.int32),
            pltpu.VMEM(weights.shape, BF16),
            pltpu.VMEM((plan.trials * delays + rows, neurons), F32),
            pltpu.VMEM((delays, up(rows, 16), neurons), BF16),
            pltpu.VMEM((2 * plan.lanes * plan.blocks, rows, 128), F32),
            pltpu.SemaphoreType.DMA,
            pltpu.SemaphoreType.DMA((unit_count // chunk,)),
        ],
        compiler_params=params(24),
        name="payload",
    )(given, pltpu.with_memory_space_constraint(weights, pltpu.HBM))


def known_kernel(plan, given, population, history, kernel, out, reach, series, fresh, lags, sorted_):
    steps, trials, neurons = plan.steps, plan.trials, given.shape[1]
    pops, kinds, _, taps = history.shape
    channels, parts = kernel.shape[0], pops * kinds
    some = 256 // parts
    row = lax.broadcasted_iota(jnp.int32, (256, 256), 0)
    column = lax.broadcasted_iota(jnp.int32, (256, 256), 1)
    order = (column == row % some * parts + row // some).astype(F32).astype(BF16)
    for index in range(channels // some):
        rows = kernel[index * some : (index + 1) * some].reshape(256, taps)
        rows = dot(order, rows).astype(BF16)
        for part in range(parts):
            sorted_[part, index * some : (index + 1) * some] = rows[part * some : (part + 1) * some]
    group = kinds * trials
    lane = lax.broadcasted_iota(jnp.int32, (pops * group, taps), 1)
    for pop in range(pops):
        for kind in range(kinds):
            start = pop * group + kind * trials
            series[start : start + trials, :] = history[pop, kind]
    flip = lax.broadcasted_iota(jnp.int32, (taps, taps), 0) + lax.broadcasted_iota(
        jnp.int32, (taps, taps), 1
    )
    flip = (flip == taps - 1).astype(F32).astype(BF16)
    back = dot(series[...].astype(BF16), flip)

    which = lax.broadcasted_iota(jnp.int32, (8, neurons), 0)
    member = (which == population[...].reshape(1, -1)).astype(F32).astype(BF16)
    rows = given[0 : steps * trials].astype(F32).astype(BF16)
    rates = (dot(member, rows, NT) / (neurons / pops)).astype(BF16)
    fresh[...] = jnp.zeros_like(fresh)
    row = lax.broadcasted_iota(jnp.int32, (steps * trials, taps), 0)
    column = lax.broadcasted_iota(jnp.int32, (steps * trials, taps), 1)
    for trial in range(trials):
        place = (row == (taps - 1 - column) * trials + trial).astype(F32).astype(BF16)
        placed = dot(rates, place)
        for pop in range(pops):
            fresh[pop * group + trial : pop * group + trial + 1, :] = placed[pop : pop + 1, :]
    lags[...] = jnp.zeros_like(lags)
    recent = fresh[...]
    for step in range(steps):
        shifted = jnp.where(lane >= taps - step, recent, back)
        if step:
            shifted = pltpu.roll(shifted, step, 1)
        for part in range(pops * kinds):
            for trial in range(trials):
                row = part * trials + trial
                spot = trial * steps + step
                lags[part, spot : spot + 1, :] = shifted[row : row + 1, :]
    total = dot(sorted_[0], lags[0].astype(BF16), NT)
    for part in range(1, parts):
        total += dot(sorted_[part], lags[part].astype(BF16), NT)
    out[...] = total

    share, wide = plan.share, plan.taps_lanes
    row = lax.broadcasted_iota(jnp.int32, (128, wide), 0)
    column = lax.broadcasted_iota(jnp.int32, (128, wide), 1)
    spread = (row == column // share).astype(F32).astype(BF16)
    row = lax.broadcasted_iota(jnp.int32, (channels, wide), 0)
    column = lax.broadcasted_iota(jnp.int32, (channels, wide), 1)
    same = (row % share == column % share) & (column < (steps - 1) * share)
    row = lax.broadcasted_iota(jnp.int32, (plan.area_count, channels), 0)
    column = lax.broadcasted_iota(jnp.int32, (plan.area_count, channels), 1)
    gather = (row == column // share).astype(F32).astype(BF16)
    reach[...] = jnp.zeros_like(reach)
    for pop in range(pops):
        wider = jnp.where(same, dot(sorted_[pop * kinds + 1, :, 0:128], spread), 0.0)
        packed = dot(gather, wider.astype(BF16))
        for tile in range(wide // 128):
            reach[:, tile * pops + pop, :] = packed[:, tile * 128 : tile * 128 + 128]


def known_lfp(plan, given, population, history, kernel):
    pops, kinds, trials, taps = history.shape
    channels = kernel.shape[0]
    return pl.pallas_call(
        functools.partial(known_kernel, plan),
        out_shape=(
            jax.ShapeDtypeStruct((channels, 128), F32),
            jax.ShapeDtypeStruct((plan.area_count, plan.taps, 128), F32),
        ),
        in_specs=[VMEM] * 4,
        out_specs=(VMEM, VMEM),
        scratch_shapes=[
            pltpu.VMEM((pops * kinds * trials, taps), F32),
            pltpu.VMEM((pops * kinds * trials, taps), F32),
            pltpu.VMEM((pops * kinds, 128, taps), F32),
            pltpu.VMEM((pops * kinds, channels, taps), BF16),
        ],
        compiler_params=params(16),
        name="known_lfp",
    )(given, population, history, kernel)


def pack_signal(plan, values):
    high, low = both(values)
    if not plan.compact:
        return jnp.concatenate([high, low], axis=0)
    half = plan.signal // 2
    out = high[:half]
    for index, piece in enumerate((high[half:], low[:half], low[half:]), 1):
        out = out + pltpu.roll(piece, index * plan.tile, 1)
    return out


def unpack_signal(plan, rows):
    if not plan.compact:
        half = plan.packed // 2
        return rows[:half] + rows[half:]
    lane = lax.broadcasted_iota(jnp.int32, rows.shape, 1)
    pieces = [rows] + [pltpu.roll(rows, 128 - index * plan.tile, 1) for index in (1, 2, 3)]
    value = jnp.concatenate([pieces[0] + pieces[2], pieces[1] + pieces[3]], axis=0)
    lane = lax.broadcasted_iota(jnp.int32, value.shape, 1)
    return jnp.where(lane < plan.tile, value, 0.0)


def compress_kernel(
    plan, mine, got, near, far, cycle, start, known, taps, keep, send, carried, signal, room
):
    trials, steps, delays, blocks = plan.trials, plan.steps, plan.delays, plan.blocks
    me = lax.axis_index("area")
    signal[...] = jnp.zeros_like(signal)
    room[...] = jnp.zeros_like(room)
    owner = lax.broadcasted_iota(jnp.int32, (plan.signal_lanes, 128), 0).astype(F32)

    def pair(index, _):
        source = plan.ring_place(index, me)
        sums = jnp.zeros((2 * plan.signal, plan.signal_lanes), F32)
        for bit in range(2):
            lane = 2 * index + bit
            own = (lane == 0).astype(F32)
            place = lax.bitwise_xor(plan.mask(lane), me)
            first = (lax.shift_right_logical(place, 1) * plan.pops).astype(F32)
            tops, members = [], []
            for block in range(blocks):
                arriving = mine[lane * blocks + block] + got[lane * blocks + block]
                early = arriving[0 : trials * delays] + own * cycle[block]
                arriving = jnp.concatenate([early, arriving[trials * delays :]], axis=0)
                spot = pl.multiple_of((source * blocks + block) * 8, 8)
                facts = (far if bit else near)[pl.ds(spot, 8)]
                last = facts[0:trials]
                leak = facts[trials : trials + 1]
                population = facts[trials + 1 : trials + 2]
                membrane = own * start[block]
                for step in range(steps):
                    current = arriving[step * trials : (step + 1) * trials]
                    membrane = jnp.where(last < step, leak * membrane + current, 0.0)
                spot = block * plan.each
                room[bit, spot : spot + trials] = membrane
                room[bit, spot + trials : spot + plan.each] = arriving[trials * steps :]
                tops.append(arriving[0 : plan.signal])
                members.append((owner == population + first).astype(F32).astype(BF16))
            high, low = both(jnp.concatenate(tops, axis=1))
            stacked = jnp.concatenate([high, low], axis=0).astype(BF16)
            sums += dot(stacked, jnp.concatenate(members, axis=1), NT)
            channels, reach = [], []
            for core in range(2):
                there = lax.bitwise_xor(place, core)
                rows = known[there]
                packed = rows[0:8]
                for group in range(1, plan.groups):
                    packed += pltpu.roll(rows[group * 8 : group * 8 + 8], group * plan.width, 1)
                channels.append(packed)
                reach.append(taps[there])
            reach = jnp.concatenate(reach, axis=0).astype(BF16)
            spot = pl.multiple_of(lane * 2 * plan.taps, 16)
            carried[pl.ds(spot, 2 * plan.taps)] = reach
            if bit:
                base = pl.multiple_of(index * plan.slot(0), 16)
                send[pl.ds(base, plan.main_up)] = room[bit].astype(BF16)
                spot = pl.multiple_of(base + plan.main_up, 16)
                send[pl.ds(spot, 16)] = jnp.concatenate(channels, axis=0).astype(BF16)
                spot = pl.multiple_of(base + plan.held, 16)
                send[pl.ds(spot, 2 * plan.taps)] = reach
            else:
                base = pl.multiple_of(index * plan.held, 8)
                keep[pl.ds(base, plan.main_up)] = room[bit]
                keep[pl.ds(base + plan.main_up, 8)] = channels[0]
                keep[pl.ds(base + plan.main_up + 8, 8)] = channels[1]
        signal[...] += sums[: plan.signal] + sums[plan.signal :]
        return 0

    pairs = plan.lanes // 2
    lax.fori_loop(0, pairs, pair, 0, unroll=min(pairs, 4))
    pieces = []
    for tile in range(plan.tiles):
        values = signal[:, tile * 128 : tile * 128 + plan.tile]
        if plan.tile < 128:
            blank = jnp.zeros((plan.signal, 128 - plan.tile), F32)
            values = jnp.concatenate([values, blank], axis=1)
        pieces.append(values)
    values = jnp.concatenate(pieces, axis=0) if plan.tiles > 1 else pieces[0]
    keep[pairs * plan.held :] = values
    put_signal(plan, send, pairs * plan.slot(0), values)


def put_signal(plan, out, base, values):
    rows = pack_signal(plan, values)
    if plan.packed_up > plan.packed:
        blank = jnp.zeros((plan.packed_up - plan.packed, 128), F32)
        rows = jnp.concatenate([rows, blank], axis=0)
    out[base:] = rows.astype(BF16)


def compress(plan, mine, got, near, far, cycle, start, known, taps):
    return pl.pallas_call(
        functools.partial(compress_kernel, plan),
        out_shape=(plan.keep(plan.lanes // 2), plan.send(plan.lanes // 2, 0), plan.carried()),
        in_specs=[VMEM] * 8,
        out_specs=(VMEM,) * 3,
        scratch_shapes=[
            pltpu.VMEM((plan.signal, plan.signal_lanes), F32),
            pltpu.VMEM((2, plan.main_up, 128), F32),
        ],
        compiler_params=params(32),
        name="compress",
    )(mine, got, near, far, cycle, start, known, taps)


def fold_kernel(plan, slots, stage, direct, held, got, carried, keep, *refs):
    taps = 2 * plan.taps
    if direct:
        sends, (now, room) = refs[:-2], refs[-2:]
    else:
        sends, (now,) = refs[:1], refs[1:]
    def spot_of(lane, stage):
        rest = lane & ((1 << stage) - 1)
        return (lane >> (stage + 1)) * plan.slot(stage) + plan.held + rest * taps

    for lane in range(plan.lanes):
        rows = slice(lane * taps, (lane + 1) * taps)
        if lane >> stage & 1:
            spot = spot_of(lane, stage)
            now[rows] = got[spot : spot + taps]
        else:
            now[rows] = carried[rows]
    size = plan.slot(stage)
    tail = got[slots * size : slots * size + plan.packed_up].astype(F32)[: plan.packed]
    tail = unpack_signal(plan, tail)
    tail = tail + held[slots * plan.held :]
    left = 1 if direct else slots // 2
    for slot in range(slots):
        rows = got[slot * size : slot * size + plan.held].astype(F32)
        rows = rows + held[slot * plan.held : (slot + 1) * plan.held]
        if direct and slot:
            out = sends[LATE.index(slot)]
            room[0 : plan.main] = rows[: plan.main]
            room[plan.main : plan.main + plan.packed] = pack_signal(plan, tail)
            out[0 : plan.last] = room[...].astype(BF16)
            out[plan.last : plan.last + 16] = rows[plan.main_up :].astype(BF16)
            span = plan.lanes // 4 * taps
            out[plan.last + 16 :] = now[slot * span : (slot + 1) * span]
        elif slot % 2:
            base = slot // 2 * plan.slot(stage + 1)
            sends[0][base : base + plan.held] = rows.astype(BF16)
        else:
            keep[slot // 2 * plan.held : (slot // 2 + 1) * plan.held] = rows
    keep[left * plan.held :] = tail
    if not direct:
        for lane in range(plan.lanes):
            if lane >> (stage + 1) & 1:
                spot = spot_of(lane, stage + 1)
                sends[0][spot : spot + taps] = now[lane * taps : (lane + 1) * taps]
        put_signal(plan, sends[0], left * plan.slot(stage + 1), tail)


def fold(plan, slots, stage, direct, held, got, carried):
    left = 1 if direct else slots // 2
    scratch = []
    sends = (plan.send(left, stage + 1),)
    if direct:
        sends = (plan.direct(),) * (slots - 1)
        scratch = [pltpu.VMEM((plan.last, 128), F32)]
    return pl.pallas_call(
        functools.partial(fold_kernel, plan, slots, stage, direct),
        out_shape=(plan.keep(left),) + sends + (plan.carried(),),
        in_specs=[VMEM] * 3,
        out_specs=(VMEM,) * (2 + len(sends)),
        scratch_shapes=scratch,
        compiler_params=params(32),
        name="fold",
    )(held, got, carried)


def fresh_lfp(plan, core, channels, signal, carried, gots, mixed, reach, late):
    steps, pops = plan.steps, plan.pops
    taps = 2 * plan.taps
    me = lax.shift_right_logical(lax.axis_index("area"), 1)
    span = plan.lanes // 4
    for lane in range(plan.lanes):
        far, near = divmod(lane, span)
        if far:
            spot = plan.last + 16 + near * taps
            slot = gots[LATE.index(far)][spot : spot + taps]
        else:
            slot = carried[lane * taps : (lane + 1) * taps]
        slot = slot.astype(F32)
        spot = lax.bitwise_xor(me, lane)
        for tile in range(plan.taps_lanes // 128):
            top = core * plan.taps + tile * pops
            mixed[spot, 0:pops, tile * 128 : tile * 128 + 128] = slot[top : top + pops]
    for lane in range(plan.lanes):
        reach[lane * pops : (lane + 1) * pops] = mixed[lane, 0:pops]
    products = None
    for tile in range(plan.tiles):
        right = reach[tile * 128 : tile * 128 + plan.tile].astype(BF16)
        one = dot(signal[tile][:, : plan.tile], right)
        products = one if products is None else products + one
    step_of = lax.broadcasted_iota(jnp.int32, (plan.width, 128), 0) % steps
    value = jnp.zeros((plan.width, 128), F32)
    width = products.shape[1]
    for lag in range(1, steps):
        moved = products
        if lag > 1:
            moved = pltpu.roll(products, width - (lag - 1) * plan.share, 1)
        moved = pltpu.roll(moved[:, 0:128], lag, 0)
        value = value + jnp.where(step_of >= lag, moved, 0.0)
    late[...] = jnp.zeros_like(late)
    late[0 : plan.width] = value
    fresh = jnp.transpose(late[...])
    lane = lax.broadcasted_iota(jnp.int32, (8, 128), 1)
    for group in range(plan.groups):
        piece = jnp.where(lane < plan.width, fresh[group * 8 : group * 8 + 8], 0.0)
        if group:
            piece = pltpu.roll(piece, group * plan.width, 1)
        channels = channels + piece
    return channels


def other_kernel(plan, held, carried, *refs):
    gots, (other, signal_out, mixed, reach, late) = refs[:3], refs[3:]
    trials, steps = plan.trials, plan.steps
    channels = held[plan.main_up + 8 : plan.main_up + 16]
    tail = held[plan.held :]
    for got in gots:
        channels = channels + got[plan.last : plan.last + 16].astype(F32)[8:]
        arrived = got[0 : plan.last].astype(F32)
        tail = tail + unpack_signal(plan, arrived[plan.main : plan.main + plan.packed])
    new = lax.broadcasted_iota(jnp.int32, (plan.width, plan.signal), 0)
    old = lax.broadcasted_iota(jnp.int32, (plan.width, plan.signal), 1)
    order = (old == (new % steps) * trials + new // steps).astype(F32).astype(BF16)
    signal = (tail / plan.pop_size).astype(BF16)
    signal = [
        dot(order, signal[tile * plan.signal : (tile + 1) * plan.signal]).astype(BF16)
        for tile in range(plan.tiles)
    ]
    for tile in range(plan.tiles):
        signal_out[tile * plan.width : (tile + 1) * plan.width] = signal[tile].astype(F32)
    other[...] = fresh_lfp(plan, 1, channels, signal, carried, gots, mixed, reach, late)


def own_kernel(plan, held, carried, signal_in, *refs):
    gots, (membrane, cycle, own, mixed, reach, late, parts) = refs[:3], refs[3:]
    trials, delays = plan.trials, plan.delays
    channels = held[plan.main_up : plan.main_up + 8]
    parts[0 : plan.main] = held[0 : plan.main]
    for got in gots:
        channels = channels + got[plan.last : plan.last + 16].astype(F32)[:8]
        parts[0 : plan.main] += got[0 : plan.last].astype(F32)[: plan.main]
    for block in range(plan.blocks):
        lanes = slice(block * 128, block * 128 + 128)
        base = block * plan.each
        membrane[:, lanes] = parts[base : base + trials]
        for delay in range(delays):
            spot = base + trials * (1 + delay)
            cycle[:, delay, lanes] = parts[spot : spot + trials]
    signal = [
        signal_in[tile * plan.width : (tile + 1) * plan.width].astype(BF16)
        for tile in range(plan.tiles)
    ]
    own[...] = fresh_lfp(plan, 0, channels, signal, carried, gots, mixed, reach, late)


def taps_scratch(plan):
    return [
        pltpu.VMEM((plan.lanes, 8, plan.taps_lanes), F32),
        pltpu.VMEM((plan.signal_lanes, plan.taps_lanes), F32),
        pltpu.VMEM((128, 128), F32),
    ]


def finish_other(plan, held, carried, gots):
    return pl.pallas_call(
        functools.partial(other_kernel, plan),
        out_shape=(
            jax.ShapeDtypeStruct((8, 128), F32),
            jax.ShapeDtypeStruct((plan.tiles * plan.width, 128), F32),
        ),
        in_specs=[VMEM] * (2 + len(gots)),
        out_specs=(VMEM,) * 2,
        scratch_shapes=taps_scratch(plan),
        compiler_params=params(16),
        name="finish_other",
    )(held, carried, *gots)


def finish_own(plan, neurons, held, carried, signal, gots):
    trials, delays = plan.trials, plan.delays
    return pl.pallas_call(
        functools.partial(own_kernel, plan),
        out_shape=(
            jax.ShapeDtypeStruct((trials, neurons), F32),
            jax.ShapeDtypeStruct((trials, delays, neurons), F32),
            jax.ShapeDtypeStruct((8, 128), F32),
        ),
        in_specs=[VMEM] * (3 + len(gots)),
        out_specs=(VMEM,) * 3,
        scratch_shapes=taps_scratch(plan) + [pltpu.VMEM((plan.main_up, 128), F32)],
        compiler_params=params(16),
        name="finish_own",
    )(held, carried, signal, *gots)


def swap(values, bit, area_count):
    return lax.ppermute(values, "area", [(i, i ^ bit) for i in range(area_count)])


def body(
    spikes,
    weights,
    destination,
    target_block,
    delay_slot,
    population,
    leak_rate,
    membrane_start,
    cycle_start,
    history,
    lfp_kernel,
):
    area_count = lax.axis_size("area")
    neurons = weights.shape[1]
    blocks = neurons // 128
    trials, steps = spikes.shape[:2]
    delays = cycle_start.shape[1]
    channels = lfp_kernel.shape[0]
    pops = history.shape[0]
    plan = Plan(area_count, trials, steps, delays, neurons, pops, channels)
    share = plan.share
    spikes = jnp.transpose(spikes, (1, 0, 2))
    quarter = plan.lanes // 4

    facts, given = facts_of(
        plan, spikes, leak_rate, population, destination[:, 0], target_block, delay_slot
    )
    size = facts.shape[0]
    facts = [facts] + [lax.ppermute(facts, "area", plan.ring(shift)) for shift in RING]
    mine, goes, token = payload_sums(plan, given, weights)
    got = swap(goes, 1, area_count)
    blank = jnp.zeros((max(0, PAD - 4 * size - token.shape[0]), 128), F32)
    near = jnp.concatenate(facts + [token, blank])
    count, lane = 4 * size, quarter // 2
    while True:
        more = swap(near, plan.mask(lane), area_count)
        if lane == 1:
            break
        near = jnp.stack(
            [near[:count].reshape(-1, size, 128), more[:count].reshape(-1, size, 128)], axis=1
        ).reshape(-1, 128)
        count, lane = 2 * count, lane // 2

    known, first = known_lfp(plan, given, population, history, lfp_kernel)
    known = known.reshape(area_count, share, 128)
    known = jnp.pad(known, ((0, 0), (0, plan.groups * 8 - share), (0, 0)))

    cycle = jnp.transpose(cycle_start, (1, 0, 2)).reshape(delays * trials, blocks, 128)
    cycle = jnp.transpose(cycle, (1, 0, 2))
    start = jnp.transpose(membrane_start.reshape(trials, blocks, 128), (1, 0, 2))
    keep, send, carried = compress(plan, mine, got, near, more, cycle, start, known, first)

    slots, stage = plan.lanes // 2, 0
    got = swap(send, plan.mask(1), area_count)
    while slots > 4:
        keep, send, carried = fold(plan, slots, stage, False, keep, got, carried)
        slots, stage = slots // 2, stage + 1
        got = swap(send, plan.mask(1 << stage), area_count)
    keep, *sends, carried = fold(plan, slots, stage, True, keep, got, carried)
    gots = [
        swap(send, plan.mask(index * quarter), area_count) for send, index in zip(sends, LATE)
    ]
    other, signal = finish_other(plan, keep, carried, gots)
    other = swap(other, 1, area_count)
    membrane, cycle_out, own = finish_own(plan, neurons, keep, carried, signal, gots)
    lfp = own + other
    width = plan.width
    lfp = [lfp[:, group * width : (group + 1) * width] for group in range(plan.groups)]
    lfp = jnp.concatenate(lfp, axis=0)[:share]
    return membrane, cycle_out, lfp


def solution(mesh):
    return jax.shard_map(
        body,
        mesh=mesh,
        in_specs=(
            P("runs", None, "area"),
            P("area", None, None),
            P("area", None),
            P("area"),
            P("area"),
            P("area"),
            P("area"),
            P("runs", "area"),
            P("runs", None, "area"),
            P("area", None, "runs", None),
            P(None, "area", None, None),
        ),
        out_specs=(P("runs", "area"), P("runs", None, "area"), P("area", "runs")),
        check_vma=False,
    )
```

```python
import functools

import jax
import jax.numpy as jnp
from jax import lax
from jax.experimental import pallas as pl
from jax.experimental.pallas import tpu as pltpu
from jax.sharding import PartitionSpec as P

BF16, F32 = jnp.bfloat16, jnp.float32
PAD = 112
LATE = (2, 3, 1)
RING = (1, 2, 3)
VMEM = pl.BlockSpec(memory_space=pltpu.VMEM)
HBM = pl.BlockSpec(memory_space=pltpu.HBM)
NT = (((1,), (1,)), ((), ()))


def up(value, unit):
    return -(-value // unit) * unit


def dot(left, right, dims=None):
    if dims is None:
        return jnp.dot(left, right, preferred_element_type=F32)
    return lax.dot_general(left, right, dims, preferred_element_type=F32)


def both(values):
    high = values.astype(BF16).astype(F32)
    return high, (values - high).astype(BF16).astype(F32)


def params(megabytes):
    return pltpu.CompilerParams(vmem_limit_bytes=megabytes * 2**20)


class Plan:
    def __init__(self, area_count, trials, steps, delays, neurons, pops, channels):
        self.area_count, self.trials, self.steps, self.delays = area_count, trials, steps, delays
        self.lanes = area_count // 2
        self.top = self.lanes.bit_length() - 2
        self.blocks, self.pops = neurons // 128, pops
        self.pop_size = neurons / pops
        self.arriving = trials * (steps + delays)
        self.each = trials * (1 + delays)
        self.main = self.blocks * self.each
        self.main_up = up(self.main, 16)
        self.share = channels // area_count
        self.groups = up(self.share, 8) // 8
        self.width = trials * steps
        self.taps_lanes = up((steps - 1) * self.share, 128)
        self.taps = up(self.taps_lanes // 128 * pops, 8)
        self.signal = up(trials * (steps - 1), 8)
        self.signal_lanes = pops * self.lanes
        self.tile = min(self.signal_lanes, 128)
        self.tiles = up(self.signal_lanes, 128) // 128
        self.compact = 4 * self.tile <= 128 and self.signal % 2 == 0
        self.packed = self.signal // 2 if self.compact else 2 * self.tiles * self.signal
        self.packed_up = up(self.packed, 16)
        self.held = self.main_up + 16
        self.last = up(self.main + self.packed, 16)

    def mask(self, lane):
        return (2 * lane) ^ ((lane >> self.top) ^ (lane >> (self.top - 1) & 1))

    def quarter(self, device):
        return (device >> 1) // (self.lanes // 4)

    def ring(self, shift):
        pairs = []
        for device in range(self.area_count):
            here = self.quarter(device)
            apart = here ^ (here + shift) % 4
            pairs.append((device, device ^ self.mask(apart * (self.lanes // 4))))
        return pairs

    def ring_place(self, pair, me):
        size = self.lanes // 8
        apart, rest = pair // size, pair % size
        turned = (apart % 2 == 1) & (self.quarter(me) % 2 == 0)
        shift = jnp.where(turned, 4 - apart, apart)
        place = jnp.int32(0)
        for index, value in enumerate(RING, 1):
            place = jnp.where(shift == value, index, place)
        return place * size + rest

    def keep(self, slots):
        rows = slots * self.held + self.tiles * self.signal
        return jax.ShapeDtypeStruct((rows, 128), F32)

    def slot(self, stage):
        return self.held + (2 * self.taps << stage)

    def send(self, slots, stage):
        return jax.ShapeDtypeStruct((slots * self.slot(stage) + self.packed_up, 128), BF16)

    def direct(self):
        rows = self.last + 16 + self.lanes // 4 * 2 * self.taps
        return jax.ShapeDtypeStruct((rows, 128), BF16)

    def carried(self):
        return jax.ShapeDtypeStruct((self.lanes * 2 * self.taps, 128), BF16)


def facts_kernel(plan, spikes, leak, population, destination, target_block, delay_slot, out, given):
    trials, steps = plan.trials, plan.steps
    last = jnp.full(spikes.shape[1:], -1, jnp.int32)
    for step in range(steps):
        last = jnp.where(spikes[step] > 0, step, last)
        given[step * trials : (step + 1) * trials] = spikes[step]
    high, low = both(leak[...].reshape(1, -1))
    blank = jnp.zeros((5 - trials, last.shape[1]), F32)
    rows = [last.astype(F32), high, low, population[...].astype(F32).reshape(1, -1), blank]
    rows = jnp.concatenate(rows, axis=0)
    for block in range(plan.blocks):
        out[block * 8 : block * 8 + 8] = rows[:, block * 128 : block * 128 + 128]
    given[plan.width :] = jnp.zeros((given.shape[0] - plan.width, given.shape[1]), jnp.int32)
    for row, values in enumerate((destination, target_block, delay_slot)):
        row += up(plan.width, 8)
        given[row : row + 1, 0 : values.shape[0]] = values[...].reshape(1, -1)


def facts_of(plan, spikes, leak, population, destination, target_block, delay_slot):
    rows = up(plan.width, 8) + 8
    return pl.pallas_call(
        functools.partial(facts_kernel, plan),
        out_shape=(
            pltpu.VMEM((plan.blocks * 8, 128), F32),
            pltpu.VMEM((rows, spikes.shape[2]), jnp.int32),
        ),
        in_specs=[VMEM] * 6,
        out_specs=(VMEM, VMEM),
        name="facts",
    )(spikes, leak, population, destination, target_block, delay_slot)


def payload_kernel(
    plan, given, weights, keep, send, token, codes, held, plain, lagged, total, sem, part_sems
):
    steps, trials = plan.steps, plan.trials
    unit_count = weights.shape[0]
    delays = lagged.shape[0]
    blocks = plan.blocks
    half, rows = keep.shape[:2]
    chunk = held.shape[0] // part_sems.shape[0]
    chunks = unit_count // chunk
    listed = pltpu.make_async_copy(given.at[pl.ds(up(plan.width, 8), 8)], codes, sem)
    listed.start()

    def part(index):
        where = pl.ds(index * chunk, chunk)
        return pltpu.make_async_copy(weights.at[where], held.at[where], part_sems.at[index])

    for index in range(chunks):
        part(index).start()
    total[...] = jnp.zeros_like(total)
    plain[...] = jnp.zeros_like(plain)
    lagged[...] = jnp.zeros_like(lagged)
    token[...] = jnp.zeros_like(token)
    front = trials * delays
    for step in range(steps):
        start = front + step * trials
        plain[start : start + trials, :] = given[step * trials : (step + 1) * trials].astype(F32)
    for delay in range(delays):
        start = front - trials * (delay + 1)
        lagged[delay, 0:rows, :] = plain[start : start + rows, :].astype(BF16)
    listed.wait()
    me = lax.axis_index("area")

    def some(index, _):
        part(index).wait()
        units = [index * chunk + inner for inner in range(chunk)]
        values = [
            dot(lagged[codes[2, unit]], held[unit])[0:rows].astype(BF16).astype(F32)
            for unit in units
        ]
        for unit, value in zip(units, values):
            device = lax.bitwise_xor(codes[0, unit], me)
            lane = lax.shift_right_logical(device, 1)
            bit = lax.bitwise_and(device ^ (lane >> plan.top) ^ (lane >> (plan.top - 1)), 1)
            place = bit * half + lane * blocks + codes[1, unit]
            total[place] += value
        return 0

    lax.fori_loop(0, chunks, some, 0)
    keep[...] = total[0:half]
    send[...] = total[half:]


def payload_sums(plan, given, weights):
    unit_count, neurons = weights.shape[:2]
    rows, delays = plan.arriving, plan.delays
    chunk = next(size for size in (16, 12, 8, 6, 4, 3, 2, 1) if unit_count % size == 0)
    half = jax.ShapeDtypeStruct((plan.lanes * plan.blocks, rows, 128), F32)
    return pl.pallas_call(
        functools.partial(payload_kernel, plan),
        out_shape=(half, half, jax.ShapeDtypeStruct((8, 128), F32)),
        in_specs=[VMEM, HBM],
        out_specs=(VMEM,) * 3,
        scratch_shapes=[
            pltpu.SMEM((8, neurons), jnp.int32),
            pltpu.VMEM(weights.shape, BF16),
            pltpu.VMEM((plan.trials * delays + rows, neurons), F32),
            pltpu.VMEM((delays, up(rows, 16), neurons), BF16),
            pltpu.VMEM((2 * plan.lanes * plan.blocks, rows, 128), F32),
            pltpu.SemaphoreType.DMA,
            pltpu.SemaphoreType.DMA((unit_count // chunk,)),
        ],
        compiler_params=params(24),
        name="payload",
    )(given, pltpu.with_memory_space_constraint(weights, pltpu.HBM))


def known_kernel(plan, given, population, history, kernel, out, reach, series, fresh, lags, sorted_):
    steps, trials, neurons = plan.steps, plan.trials, given.shape[1]
    pops, kinds, _, taps = history.shape
    channels, parts = kernel.shape[0], pops * kinds
    some = 256 // parts
    row = lax.broadcasted_iota(jnp.int32, (256, 256), 0)
    column = lax.broadcasted_iota(jnp.int32, (256, 256), 1)
    order = (column == row % some * parts + row // some).astype(F32).astype(BF16)
    for index in range(channels // some):
        rows = kernel[index * some : (index + 1) * some].reshape(256, taps)
        rows = dot(order, rows).astype(BF16)
        for part in range(parts):
            sorted_[part, index * some : (index + 1) * some] = rows[part * some : (part + 1) * some]
    group = kinds * trials
    lane = lax.broadcasted_iota(jnp.int32, (pops * group, taps), 1)
    for pop in range(pops):
        for kind in range(kinds):
            start = pop * group + kind * trials
            series[start : start + trials, :] = history[pop, kind]
    flip = lax.broadcasted_iota(jnp.int32, (taps, taps), 0) + lax.broadcasted_iota(
        jnp.int32, (taps, taps), 1
    )
    flip = (flip == taps - 1).astype(F32).astype(BF16)
    back = dot(series[...].astype(BF16), flip)

    which = lax.broadcasted_iota(jnp.int32, (8, neurons), 0)
    member = (which == population[...].reshape(1, -1)).astype(F32).astype(BF16)
    rows = given[0 : steps * trials].astype(F32).astype(BF16)
    rates = (dot(member, rows, NT) / (neurons / pops)).astype(BF16)
    fresh[...] = jnp.zeros_like(fresh)
    row = lax.broadcasted_iota(jnp.int32, (steps * trials, taps), 0)
    column = lax.broadcasted_iota(jnp.int32, (steps * trials, taps), 1)
    for trial in range(trials):
        place = (row == (taps - 1 - column) * trials + trial).astype(F32).astype(BF16)
        placed = dot(rates, place)
        for pop in range(pops):
            fresh[pop * group + trial : pop * group + trial + 1, :] = placed[pop : pop + 1, :]
    lags[...] = jnp.zeros_like(lags)
    recent = fresh[...]
    for step in range(steps):
        shifted = jnp.where(lane >= taps - step, recent, back)
        if step:
            shifted = pltpu.roll(shifted, step, 1)
        for part in range(pops * kinds):
            for trial in range(trials):
                row = part * trials + trial
                spot = trial * steps + step
                lags[part, spot : spot + 1, :] = shifted[row : row + 1, :]
    total = dot(sorted_[0], lags[0].astype(BF16), NT)
    for part in range(1, parts):
        total += dot(sorted_[part], lags[part].astype(BF16), NT)
    out[...] = total

    share, wide = plan.share, plan.taps_lanes
    row = lax.broadcasted_iota(jnp.int32, (128, wide), 0)
    column = lax.broadcasted_iota(jnp.int32, (128, wide), 1)
    spread = (row == column // share).astype(F32).astype(BF16)
    row = lax.broadcasted_iota(jnp.int32, (channels, wide), 0)
    column = lax.broadcasted_iota(jnp.int32, (channels, wide), 1)
    same = (row % share == column % share) & (column < (steps - 1) * share)
    row = lax.broadcasted_iota(jnp.int32, (plan.area_count, channels), 0)
    column = lax.broadcasted_iota(jnp.int32, (plan.area_count, channels), 1)
    gather = (row == column // share).astype(F32).astype(BF16)
    reach[...] = jnp.zeros_like(reach)
    for pop in range(pops):
        wider = jnp.where(same, dot(sorted_[pop * kinds + 1, :, 0:128], spread), 0.0)
        packed = dot(gather, wider.astype(BF16))
        for tile in range(wide // 128):
            reach[:, tile * pops + pop, :] = packed[:, tile * 128 : tile * 128 + 128]


def known_lfp(plan, given, population, history, kernel):
    pops, kinds, trials, taps = history.shape
    channels = kernel.shape[0]
    return pl.pallas_call(
        functools.partial(known_kernel, plan),
        out_shape=(
            jax.ShapeDtypeStruct((channels, 128), F32),
            jax.ShapeDtypeStruct((plan.area_count, plan.taps, 128), F32),
        ),
        in_specs=[VMEM] * 4,
        out_specs=(VMEM, VMEM),
        scratch_shapes=[
            pltpu.VMEM((pops * kinds * trials, taps), F32),
            pltpu.VMEM((pops * kinds * trials, taps), F32),
            pltpu.VMEM((pops * kinds, 128, taps), F32),
            pltpu.VMEM((pops * kinds, channels, taps), BF16),
        ],
        compiler_params=params(16),
        name="known_lfp",
    )(given, population, history, kernel)


def pack_signal(plan, values):
    high, low = both(values)
    if not plan.compact:
        return jnp.concatenate([high, low], axis=0)
    half = plan.signal // 2
    out = high[:half]
    for index, piece in enumerate((high[half:], low[:half], low[half:]), 1):
        out = out + pltpu.roll(piece, index * plan.tile, 1)
    return out


def unpack_signal(plan, rows):
    if not plan.compact:
        half = plan.packed // 2
        return rows[:half] + rows[half:]
    lane = lax.broadcasted_iota(jnp.int32, rows.shape, 1)
    pieces = [rows] + [pltpu.roll(rows, 128 - index * plan.tile, 1) for index in (1, 2, 3)]
    value = jnp.concatenate([pieces[0] + pieces[2], pieces[1] + pieces[3]], axis=0)
    lane = lax.broadcasted_iota(jnp.int32, value.shape, 1)
    return jnp.where(lane < plan.tile, value, 0.0)


def compress_kernel(
    plan, mine, got, near, far, cycle, start, known, taps, keep, send, carried, signal, room
):
    trials, steps, delays, blocks = plan.trials, plan.steps, plan.delays, plan.blocks
    me = lax.axis_index("area")
    signal[...] = jnp.zeros_like(signal)
    room[...] = jnp.zeros_like(room)
    owner = lax.broadcasted_iota(jnp.int32, (plan.signal_lanes, 128), 0).astype(F32)

    def pair(index, _):
        source = plan.ring_place(index, me)
        sums = jnp.zeros((2 * plan.signal, plan.signal_lanes), F32)
        for bit in range(2):
            lane = 2 * index + bit
            own = (lane == 0).astype(F32)
            place = lax.bitwise_xor(plan.mask(lane), me)
            first = (lax.shift_right_logical(place, 1) * plan.pops).astype(F32)
            tops, members = [], []
            for block in range(blocks):
                arriving = mine[lane * blocks + block] + got[lane * blocks + block]
                early = arriving[0 : trials * delays] + own * cycle[block]
                arriving = jnp.concatenate([early, arriving[trials * delays :]], axis=0)
                spot = pl.multiple_of((source * blocks + block) * 8, 8)
                facts = (far if bit else near)[pl.ds(spot, 8)]
                last = facts[0:trials]
                leak = facts[trials : trials + 1] + facts[trials + 1 : trials + 2]
                population = facts[trials + 2 : trials + 3]
                membrane = own * start[block]
                for step in range(steps):
                    current = arriving[step * trials : (step + 1) * trials]
                    membrane = jnp.where(last < step, leak * membrane + current, 0.0)
                spot = block * plan.each
                room[bit, spot : spot + trials] = membrane
                room[bit, spot + trials : spot + plan.each] = arriving[trials * steps :]
                tops.append(arriving[0 : plan.signal])
                members.append((owner == population + first).astype(F32).astype(BF16))
            high, low = both(jnp.concatenate(tops, axis=1))
            stacked = jnp.concatenate([high, low], axis=0).astype(BF16)
            sums += dot(stacked, jnp.concatenate(members, axis=1), NT)
            channels, reach = [], []
            for core in range(2):
                there = lax.bitwise_xor(place, core)
                rows = known[there]
                packed = rows[0:8]
                for group in range(1, plan.groups):
                    packed += pltpu.roll(rows[group * 8 : group * 8 + 8], group * plan.width, 1)
                channels.append(packed)
                reach.append(taps[there])
            reach = jnp.concatenate(reach, axis=0).astype(BF16)
            spot = pl.multiple_of(lane * 2 * plan.taps, 16)
            carried[pl.ds(spot, 2 * plan.taps)] = reach
            if bit:
                base = pl.multiple_of(index * plan.slot(0), 16)
                send[pl.ds(base, plan.main_up)] = room[bit].astype(BF16)
                spot = pl.multiple_of(base + plan.main_up, 16)
                send[pl.ds(spot, 16)] = jnp.concatenate(channels, axis=0).astype(BF16)
                spot = pl.multiple_of(base + plan.held, 16)
                send[pl.ds(spot, 2 * plan.taps)] = reach
            else:
                base = pl.multiple_of(index * plan.held, 8)
                keep[pl.ds(base, plan.main_up)] = room[bit]
                keep[pl.ds(base + plan.main_up, 8)] = channels[0]
                keep[pl.ds(base + plan.main_up + 8, 8)] = channels[1]
        signal[...] += sums[: plan.signal] + sums[plan.signal :]
        return 0

    pairs = plan.lanes // 2
    lax.fori_loop(0, pairs, pair, 0, unroll=min(pairs, 4))
    pieces = []
    for tile in range(plan.tiles):
        values = signal[:, tile * 128 : tile * 128 + plan.tile]
        if plan.tile < 128:
            blank = jnp.zeros((plan.signal, 128 - plan.tile), F32)
            values = jnp.concatenate([values, blank], axis=1)
        pieces.append(values)
    values = jnp.concatenate(pieces, axis=0) if plan.tiles > 1 else pieces[0]
    keep[pairs * plan.held :] = values
    put_signal(plan, send, pairs * plan.slot(0), values)


def put_signal(plan, out, base, values):
    rows = pack_signal(plan, values)
    if plan.packed_up > plan.packed:
        blank = jnp.zeros((plan.packed_up - plan.packed, 128), F32)
        rows = jnp.concatenate([rows, blank], axis=0)
    out[base:] = rows.astype(BF16)


def compress(plan, mine, got, near, far, cycle, start, known, taps):
    return pl.pallas_call(
        functools.partial(compress_kernel, plan),
        out_shape=(plan.keep(plan.lanes // 2), plan.send(plan.lanes // 2, 0), plan.carried()),
        in_specs=[VMEM] * 8,
        out_specs=(VMEM,) * 3,
        scratch_shapes=[
            pltpu.VMEM((plan.signal, plan.signal_lanes), F32),
            pltpu.VMEM((2, plan.main_up, 128), F32),
        ],
        compiler_params=params(32),
        name="compress",
    )(mine, got, near, far, cycle, start, known, taps)


def fold_kernel(plan, slots, stage, direct, held, got, carried, keep, *refs):
    taps = 2 * plan.taps
    if direct:
        sends, (now, room) = refs[:-2], refs[-2:]
    else:
        sends, (now,) = refs[:1], refs[1:]
    def spot_of(lane, stage):
        rest = lane & ((1 << stage) - 1)
        return (lane >> (stage + 1)) * plan.slot(stage) + plan.held + rest * taps

    for lane in range(plan.lanes):
        rows = slice(lane * taps, (lane + 1) * taps)
        if lane >> stage & 1:
            spot = spot_of(lane, stage)
            now[rows] = got[spot : spot + taps]
        else:
            now[rows] = carried[rows]
    size = plan.slot(stage)
    tail = got[slots * size : slots * size + plan.packed_up].astype(F32)[: plan.packed]
    tail = unpack_signal(plan, tail)
    tail = tail + held[slots * plan.held :]
    left = 1 if direct else slots // 2
    for slot in range(slots):
        rows = got[slot * size : slot * size + plan.held].astype(F32)
        rows = rows + held[slot * plan.held : (slot + 1) * plan.held]
        if direct and slot:
            out = sends[LATE.index(slot)]
            room[0 : plan.main] = rows[: plan.main]
            room[plan.main : plan.main + plan.packed] = pack_signal(plan, tail)
            out[0 : plan.last] = room[...].astype(BF16)
            out[plan.last : plan.last + 16] = rows[plan.main_up :].astype(BF16)
            span = plan.lanes // 4 * taps
            out[plan.last + 16 :] = now[slot * span : (slot + 1) * span]
        elif slot % 2:
            base = slot // 2 * plan.slot(stage + 1)
            sends[0][base : base + plan.held] = rows.astype(BF16)
        else:
            keep[slot // 2 * plan.held : (slot // 2 + 1) * plan.held] = rows
    keep[left * plan.held :] = tail
    if not direct:
        for lane in range(plan.lanes):
            if lane >> (stage + 1) & 1:
                spot = spot_of(lane, stage + 1)
                sends[0][spot : spot + taps] = now[lane * taps : (lane + 1) * taps]
        put_signal(plan, sends[0], left * plan.slot(stage + 1), tail)


def fold(plan, slots, stage, direct, held, got, carried):
    left = 1 if direct else slots // 2
    scratch = []
    sends = (plan.send(left, stage + 1),)
    if direct:
        sends = (plan.direct(),) * (slots - 1)
        scratch = [pltpu.VMEM((plan.last, 128), F32)]
    return pl.pallas_call(
        functools.partial(fold_kernel, plan, slots, stage, direct),
        out_shape=(plan.keep(left),) + sends + (plan.carried(),),
        in_specs=[VMEM] * 3,
        out_specs=(VMEM,) * (2 + len(sends)),
        scratch_shapes=scratch,
        compiler_params=params(32),
        name="fold",
    )(held, got, carried)


def fresh_lfp(plan, core, channels, signal, carried, gots, mixed, reach, late):
    steps, pops = plan.steps, plan.pops
    taps = 2 * plan.taps
    me = lax.shift_right_logical(lax.axis_index("area"), 1)
    span = plan.lanes // 4
    for lane in range(plan.lanes):
        far, near = divmod(lane, span)
        if far:
            spot = plan.last + 16 + near * taps
            slot = gots[LATE.index(far)][spot : spot + taps]
        else:
            slot = carried[lane * taps : (lane + 1) * taps]
        slot = slot.astype(F32)
        spot = lax.bitwise_xor(me, lane)
        for tile in range(plan.taps_lanes // 128):
            top = core * plan.taps + tile * pops
            mixed[spot, 0:pops, tile * 128 : tile * 128 + 128] = slot[top : top + pops]
    for lane in range(plan.lanes):
        reach[lane * pops : (lane + 1) * pops] = mixed[lane, 0:pops]
    products = None
    for tile in range(plan.tiles):
        right = reach[tile * 128 : tile * 128 + plan.tile].astype(BF16)
        one = dot(signal[tile][:, : plan.tile], right)
        products = one if products is None else products + one
    step_of = lax.broadcasted_iota(jnp.int32, (plan.width, 128), 0) % steps
    value = jnp.zeros((plan.width, 128), F32)
    width = products.shape[1]
    for lag in range(1, steps):
        moved = products
        if lag > 1:
            moved = pltpu.roll(products, width - (lag - 1) * plan.share, 1)
        moved = pltpu.roll(moved[:, 0:128], lag, 0)
        value = value + jnp.where(step_of >= lag, moved, 0.0)
    late[...] = jnp.zeros_like(late)
    late[0 : plan.width] = value
    fresh = jnp.transpose(late[...])
    lane = lax.broadcasted_iota(jnp.int32, (8, 128), 1)
    for group in range(plan.groups):
        piece = jnp.where(lane < plan.width, fresh[group * 8 : group * 8 + 8], 0.0)
        if group:
            piece = pltpu.roll(piece, group * plan.width, 1)
        channels = channels + piece
    return channels


def other_kernel(plan, held, carried, *refs):
    gots, (other, signal_out, mixed, reach, late) = refs[:3], refs[3:]
    trials, steps = plan.trials, plan.steps
    channels = held[plan.main_up + 8 : plan.main_up + 16]
    tail = held[plan.held :]
    for got in gots:
        channels = channels + got[plan.last : plan.last + 16].astype(F32)[8:]
        arrived = got[0 : plan.last].astype(F32)
        tail = tail + unpack_signal(plan, arrived[plan.main : plan.main + plan.packed])
    new = lax.broadcasted_iota(jnp.int32, (plan.width, plan.signal), 0)
    old = lax.broadcasted_iota(jnp.int32, (plan.width, plan.signal), 1)
    order = (old == (new % steps) * trials + new // steps).astype(F32).astype(BF16)
    signal = (tail / plan.pop_size).astype(BF16)
    signal = [
        dot(order, signal[tile * plan.signal : (tile + 1) * plan.signal]).astype(BF16)
        for tile in range(plan.tiles)
    ]
    for tile in range(plan.tiles):
        signal_out[tile * plan.width : (tile + 1) * plan.width] = signal[tile].astype(F32)
    other[...] = fresh_lfp(plan, 1, channels, signal, carried, gots, mixed, reach, late)


def own_kernel(plan, held, carried, signal_in, *refs):
    gots, (membrane, cycle, own, mixed, reach, late, parts) = refs[:3], refs[3:]
    trials, delays = plan.trials, plan.delays
    channels = held[plan.main_up : plan.main_up + 8]
    parts[0 : plan.main] = held[0 : plan.main]
    for got in gots:
        channels = channels + got[plan.last : plan.last + 16].astype(F32)[:8]
        parts[0 : plan.main] += got[0 : plan.last].astype(F32)[: plan.main]
    for block in range(plan.blocks):
        lanes = slice(block * 128, block * 128 + 128)
        base = block * plan.each
        membrane[:, lanes] = parts[base : base + trials]
        for delay in range(delays):
            spot = base + trials * (1 + delay)
            cycle[:, delay, lanes] = parts[spot : spot + trials]
    signal = [
        signal_in[tile * plan.width : (tile + 1) * plan.width].astype(BF16)
        for tile in range(plan.tiles)
    ]
    own[...] = fresh_lfp(plan, 0, channels, signal, carried, gots, mixed, reach, late)


def taps_scratch(plan):
    return [
        pltpu.VMEM((plan.lanes, 8, plan.taps_lanes), F32),
        pltpu.VMEM((plan.signal_lanes, plan.taps_lanes), F32),
        pltpu.VMEM((128, 128), F32),
    ]


def finish_other(plan, held, carried, gots):
    return pl.pallas_call(
        functools.partial(other_kernel, plan),
        out_shape=(
            jax.ShapeDtypeStruct((8, 128), F32),
            jax.ShapeDtypeStruct((plan.tiles * plan.width, 128), F32),
        ),
        in_specs=[VMEM] * (2 + len(gots)),
        out_specs=(VMEM,) * 2,
        scratch_shapes=taps_scratch(plan),
        compiler_params=params(16),
        name="finish_other",
    )(held, carried, *gots)


def finish_own(plan, neurons, held, carried, signal, gots):
    trials, delays = plan.trials, plan.delays
    return pl.pallas_call(
        functools.partial(own_kernel, plan),
        out_shape=(
            jax.ShapeDtypeStruct((trials, neurons), F32),
            jax.ShapeDtypeStruct((trials, delays, neurons), F32),
            jax.ShapeDtypeStruct((8, 128), F32),
        ),
        in_specs=[VMEM] * (3 + len(gots)),
        out_specs=(VMEM,) * 3,
        scratch_shapes=taps_scratch(plan) + [pltpu.VMEM((plan.main_up, 128), F32)],
        compiler_params=params(16),
        name="finish_own",
    )(held, carried, signal, *gots)


def swap(values, bit, area_count):
    return lax.ppermute(values, "area", [(i, i ^ bit) for i in range(area_count)])


def body(
    spikes,
    weights,
    destination,
    target_block,
    delay_slot,
    population,
    leak_rate,
    membrane_start,
    cycle_start,
    history,
    lfp_kernel,
):
    area_count = lax.axis_size("area")
    neurons = weights.shape[1]
    blocks = neurons // 128
    trials, steps = spikes.shape[:2]
    delays = cycle_start.shape[1]
    channels = lfp_kernel.shape[0]
    pops = history.shape[0]
    plan = Plan(area_count, trials, steps, delays, neurons, pops, channels)
    share = plan.share
    spikes = jnp.transpose(spikes, (1, 0, 2))
    quarter = plan.lanes // 4

    facts, given = facts_of(
        plan, spikes, leak_rate, population, destination[:, 0], target_block, delay_slot
    )
    size = facts.shape[0]
    facts = [facts] + [lax.ppermute(facts, "area", plan.ring(shift)) for shift in RING]
    mine, goes, token = payload_sums(plan, given, weights)
    blank = jnp.zeros((max(0, PAD - 4 * size - token.shape[0]), 128), F32)
    near = jnp.concatenate(facts + [token, blank])
    near, goes = lax.optimization_barrier((near, goes))
    count, lane = 4 * size, quarter // 2
    while True:
        more = swap(near.astype(BF16), plan.mask(lane), area_count).astype(F32)
        if lane == 1:
            break
        near = jnp.stack(
            [near[:count].reshape(-1, size, 128), more[:count].reshape(-1, size, 128)], axis=1
        ).reshape(-1, 128)
        count, lane = 2 * count, lane // 2

    got = swap(goes, 1, area_count)
    known, first = known_lfp(plan, given, population, history, lfp_kernel)
    known = known.reshape(area_count, share, 128)
    known = jnp.pad(known, ((0, 0), (0, plan.groups * 8 - share), (0, 0)))

    cycle = jnp.transpose(cycle_start, (1, 0, 2)).reshape(delays * trials, blocks, 128)
    cycle = jnp.transpose(cycle, (1, 0, 2))
    start = jnp.transpose(membrane_start.reshape(trials, blocks, 128), (1, 0, 2))
    keep, send, carried = compress(plan, mine, got, near, more, cycle, start, known, first)

    slots, stage = plan.lanes // 2, 0
    got = swap(send, plan.mask(1), area_count)
    while slots > 4:
        keep, send, carried = fold(plan, slots, stage, False, keep, got, carried)
        slots, stage = slots // 2, stage + 1
        got = swap(send, plan.mask(1 << stage), area_count)
    keep, *sends, carried = fold(plan, slots, stage, True, keep, got, carried)
    gots = [
        swap(send, plan.mask(index * quarter), area_count) for send, index in zip(sends, LATE)
    ]
    other, signal = finish_other(plan, keep, carried, gots)
    other = swap(other, 1, area_count)
    membrane, cycle_out, own = finish_own(plan, neurons, keep, carried, signal, gots)
    width = plan.width
    lanes = [slice(group * width, (group + 1) * width) for group in range(plan.groups)]
    lfp = jnp.concatenate([own[:, part] + other[:, part] for part in lanes])[:share]
    return membrane, cycle_out, lfp


def solution(mesh):
    return jax.shard_map(
        body,
        mesh=mesh,
        in_specs=(
            P("runs", None, "area"),
            P("area", None, None),
            P("area", None),
            P("area"),
            P("area"),
            P("area"),
            P("area"),
            P("runs", "area"),
            P("runs", None, "area"),
            P("area", None, "runs", None),
            P(None, "area", None, None),
        ),
        out_specs=(P("runs", "area"), P("runs", None, "area"), P("area", "runs")),
        check_vma=False,
    )
```
